32 devices in a mesh: pipe: 2 (over core), dp: 16 (over z, y, x).
Axes of the slice: x: 2, y: 2, z: 4, core: 2. Of those that a mesh axis runs over, the one named last changes fastest.
Arguments:
- x_global: bfloat16 [32, 197, 768], P('dp'), may hold values from -6 to 6
- x_local: bfloat16 [32, 37, 768], P('dp'), may hold values from -6 to 6
- cot_global: bfloat16 [32, 197, 768], P('dp'), may hold values from -6 to 6
- cot_local: bfloat16 [32, 37, 768], P('dp'), may hold values from -6 to 6
- global_count: int32 [16], P('dp'), may hold values from 1 to 2, as said below
- local_count: int32 [16], P('dp'), may hold values from 1 to 2, as said below
- w_qkv: bfloat16 [2, 768, 2304], P('pipe'), may hold values from -0.21875 to 0.21875
- w_proj: bfloat16 [2, 768, 768], P('pipe'), may hold values from -0.75 to 0.75
- w_fc1: bfloat16 [2, 768, 3072], P('pipe'), may hold values from -0.21875 to 0.21875
- w_fc2: bfloat16 [2, 3072, 768], P('pipe'), may hold values from -0.109375 to 0.109375
- norm1_gain: bfloat16 [2, 768], P('pipe'), may hold values from 0.5 to 1.5
- norm1_shift: bfloat16 [2, 768], P('pipe'), may hold values from -1.75 to 1.75
- q_bias: bfloat16 [2, 768], P('pipe'), may hold values from -1.75 to 1.75
- v_bias: bfloat16 [2, 768], P('pipe'), may hold values from -1.75 to 1.75
- proj_bias: bfloat16 [2, 768], P('pipe'), may hold values from -1.75 to 1.75
- scale_attn: bfloat16 [2, 768], P('pipe'), may hold values from 0.5 to 1.5
- norm2_gain: bfloat16 [2, 768], P('pipe'), may hold values from 0.5 to 1.5
- norm2_shift: bfloat16 [2, 768], P('pipe'), may hold values from -1.75 to 1.75
- fc1_bias: bfloat16 [2, 3072], P('pipe'), may hold values from -1.75 to 1.75
- fc2_bias: bfloat16 [2, 768], P('pipe'), may hold values from -1.75 to 1.75
- scale_mlp: bfloat16 [2, 768], P('pipe'), may hold values from 0.5 to 1.5
- table_global: bfloat16 [2, 732, 12], P('pipe'), may hold values from -6 to 6
- table_local: bfloat16 [2, 124, 12], P('pipe'), may hold values from -6 to 6
Outputs:
- out_global: bfloat16 [2, 32, 197, 768], P('pipe', 'dp')
- out_local: bfloat16 [2, 32, 37, 768], P('pipe', 'dp')
- grad_global_in: bfloat16 [2, 32, 197, 768], P('pipe', 'dp')
- grad_local_in: bfloat16 [2, 32, 37, 768], P('pipe', 'dp')
- grad_w_qkv: float32 [2, 768, 2304], P('pipe', 'dp')
- grad_w_proj: float32 [2, 768, 768], P('pipe', 'dp')
- grad_w_fc1: float32 [2, 768, 3072], P('pipe', 'dp')
- grad_w_fc2: float32 [2, 3072, 768], P('pipe', 'dp')
- grad_norm1_gain: float32 [2, 768], P('pipe')
- grad_norm1_shift: float32 [2, 768], P('pipe')
- grad_q_bias: float32 [2, 768], P('pipe')
- grad_v_bias: float32 [2, 768], P('pipe')
- grad_proj_bias: float32 [2, 768], P('pipe')
- grad_scale_attn: float32 [2, 768], P('pipe')
- grad_norm2_gain: float32 [2, 768], P('pipe')
- grad_norm2_shift: float32 [2, 768], P('pipe')
- grad_fc1_bias: float32 [2, 3072], P('pipe')
- grad_fc2_bias: float32 [2, 768], P('pipe')
- grad_scale_mlp: float32 [2, 768], P('pipe')
- grad_table_global: float32 [2, 732, 12], P('pipe')
- grad_table_local: float32 [2, 124, 12], P('pipe')
The draws below stay inside these ranges and needn't reach their ends.
Inputs may be any that keep to these rules, and one draw needn't show every extreme that they name: `global_count`: live global crops of each data device: its crops at or after this count are masked; some device has 2 and some has 1. `local_count`: live local crops of each data device: its crops at or after this count are masked; some device has 2 and some has 1.
All inputs are finite; a program needn't handle non-finite values.
Results may differ from the reference program's by a relative error of at most 0.02.
Values may be sent and summed in bfloat16 or wider, within the bound.
A program may use at most 256 MiB of HBM per device.

```python
import math
import jax
import jax.numpy as jnp
import numpy as np
from jax import lax

D = 768
HEADS = 12
HEAD_DIM = 64
FF = 3072
GRID_G = 14
GRID_L = 6
TG = 197
TL = 37
NUM_G = 732
NUM_L = 124
G_DEV = 2
L_DEV = 2
DATA_SHARDS = 16
GLOBAL_CROPS = 32
LOCAL_CROPS = 32


def count_draw(key, slots):
    first_key, second_key = jax.random.split(key)
    counts = jax.random.randint(first_key, (DATA_SHARDS,), 1, slots + 1)
    shuffled = jax.random.permutation(second_key, DATA_SHARDS)
    counts = counts.at[shuffled[0]].set(slots)
    counts = counts.at[shuffled[1]].set(1)
    return counts.astype(jnp.int32)


def draw_global_count(key, part):
    return count_draw(jax.random.fold_in(key, 11), G_DEV)


def draw_local_count(key, part):
    return count_draw(jax.random.fold_in(key, 23), L_DEV)


def steps_of(stream_key, shape, cuts, least, top_value):
    def one(position, blocks):
        draws = jax.random.uniform(jax.random.fold_in(jax.random.fold_in(stream_key, 6), position), (blocks,), jnp.float32, least / len(cuts), top_value / len(cuts))
        return jnp.repeat(jnp.exp(draws), shape[position] // blocks).reshape((-1,) + (1,) * (len(shape) - position - 1))

    level = one(*cuts[0])
    for cut in cuts[1:]:
        level = level * one(*cut)
    return level


def noise(stream_key, shape, spread, bound, shards=(), kind=jnp.bfloat16):
    level = steps_of(stream_key, shape, shards, -0.22, 0.18) if shards else 1.0
    drawn = jax.random.normal(stream_key, shape, jnp.float32) * spread * level
    return jnp.minimum(jnp.maximum(drawn, -bound), bound).astype(kind)


def setup_inputs(seed: int = 0) -> dict:
    streams_of = jax.random.split(jax.random.key(seed), 24)
    x_global = noise(streams_of[0], (GLOBAL_CROPS, TG, D), 1.0, 6.0, ((0, 16),))
    x_local = noise(streams_of[1], (LOCAL_CROPS, TL, D), 1.0, 6.0, ((0, 16),))
    cot_global = noise(streams_of[2], (GLOBAL_CROPS, TG, D), 1.0, 6.0, ((0, 16),))
    cot_local = noise(streams_of[3], (LOCAL_CROPS, TL, D), 1.0, 6.0, ((0, 16),))
    global_count = draw_global_count(jax.random.fold_in(streams_of[23], 71), 0)
    local_count = draw_local_count(jax.random.fold_in(streams_of[23], 71), 0)
    w_qkv = noise(streams_of[6], (2, D, 3 * D), D ** -0.5, 0.21875, ((0, 2),))
    w_proj = noise(streams_of[7], (2, D, D), HEAD_DIM ** -0.5, 0.75, ((0, 2),))
    w_fc1 = noise(streams_of[8], (2, D, FF), D ** -0.5, 0.21875, ((0, 2),))
    w_fc2 = noise(streams_of[9], (2, FF, D), FF ** -0.5, 0.109375, ((0, 2),))
    norm1_gain = jnp.clip(1.0 + 0.1 * jax.random.normal(streams_of[10], (2, D), jnp.float32), 0.5, 1.5).astype(jnp.bfloat16)
    norm1_shift = noise(streams_of[11], (2, D), 0.3, 1.75, ((0, 2),))
    q_bias = noise(streams_of[12], (2, D), 0.3, 1.75, ((0, 2),))
    v_bias = noise(streams_of[13], (2, D), 0.3, 1.75, ((0, 2),))
    proj_bias = noise(streams_of[14], (2, D), 0.3, 1.75, ((0, 2),))
    scale_attn = jnp.clip(jnp.exp(math.log(1.5) - 1.0986123 * jax.random.uniform(streams_of[15], (2, D), jnp.float32) ** steps_of(streams_of[15], (2, D), ((0, 2),), -0.2, 0.2)), 0.5, 1.5).astype(jnp.bfloat16)
    norm2_gain = jnp.clip(1.0 + 0.1 * jax.random.normal(streams_of[16], (2, D), jnp.float32), 0.5, 1.5).astype(jnp.bfloat16)
    norm2_shift = noise(streams_of[17], (2, D), 0.3, 1.75, ((0, 2),))
    fc1_bias = noise(streams_of[18], (2, FF), 0.3, 1.75, ((0, 2),))
    fc2_bias = noise(streams_of[19], (2, D), 0.3, 1.75, ((0, 2),))
    scale_mlp = jnp.clip(jnp.exp(math.log(1.5) - 1.0986123 * jax.random.uniform(streams_of[20], (2, D), jnp.float32) ** steps_of(streams_of[20], (2, D), ((0, 2),), -0.2, 0.2)), 0.5, 1.5).astype(jnp.bfloat16)
    table_global = noise(streams_of[21], (2, NUM_G, HEADS), 1.0, 6.0, ((0, 2),))
    table_local = noise(streams_of[22], (2, NUM_L, HEADS), 1.0, 6.0, ((0, 2),))
    return dict(x_global=x_global, x_local=x_local, cot_global=cot_global, cot_local=cot_local, global_count=global_count, local_count=local_count, w_qkv=w_qkv, w_proj=w_proj, w_fc1=w_fc1, w_fc2=w_fc2, norm1_gain=norm1_gain, norm1_shift=norm1_shift, q_bias=q_bias, v_bias=v_bias, proj_bias=proj_bias, scale_attn=scale_attn, norm2_gain=norm2_gain, norm2_shift=norm2_shift, fc1_bias=fc1_bias, fc2_bias=fc2_bias, scale_mlp=scale_mlp, table_global=table_global, table_local=table_local)


@jax.custom_vjp
def low(v):
    return lax.optimization_barrier(v.astype(jnp.bfloat16)).astype(jnp.float32)

@jax.custom_vjp
def low_back(v):
    return v

def low_keep(v):
    return (low(v), None)

def low_pass(kept, grad):
    return (grad,)

def back_keep(v):
    return (v, None)

def back_low(kept, grad):
    return (low(grad),)
low.defvjp(low_keep, low_pass)
low_back.defvjp(back_keep, back_low)
HIGHEST_PRECISION = lax.Precision.HIGHEST
eps = 1e-06

def position_table(grid_side):
    coordinates = np.stack(np.meshgrid(np.arange(grid_side), np.arange(grid_side), indexing='ij')).reshape(2, -1)
    relative = coordinates[:, :, None] - coordinates[:, None, :] + grid_side - 1
    entries = (2 * grid_side - 1) ** 2
    lookup = np.zeros((grid_side * grid_side + 1, grid_side * grid_side + 1), np.int32)
    lookup[1:, 1:] = relative[0] * (2 * grid_side - 1) + relative[1]
    lookup[0, 1:] = entries
    lookup[1:, 0] = entries + 1
    lookup[0, 0] = entries + 2
    return lookup

def layer_norm(values, gain, shift):
    centered = values - lax.optimization_barrier(jnp.mean(values, axis=-1, keepdims=True))
    variance = lax.optimization_barrier(jnp.mean(centered * centered, axis=-1, keepdims=True))
    return centered * lax.rsqrt(variance + eps) * gain + shift

def rounded(v):
    return low(low_back(v))

def attend(queries, key_rows, value_rows, bias):
    scores = jnp.einsum('cqhe,ckhe->chqk', queries, key_rows, precision=HIGHEST_PRECISION) + bias[None]
    scores = low_back(scores)
    weights = low(jax.nn.softmax(scores, axis=-1))
    return jnp.einsum('chqk,ckhe->cqhe', weights, value_rows, precision=HIGHEST_PRECISION)

def block(crops_g, crops_l, params, lookups):
    w_qkv, w_proj, w_fc1, w_fc2, norm1_gain, norm1_shift, q_bias, v_bias, proj_bias, scale_attn, norm2_gain, norm2_shift, fc1_bias, fc2_bias, scale_mlp, table_global, table_local = params
    split = crops_g.shape[0] * TG
    stacked = jnp.concatenate([crops_g.reshape(-1, D), crops_l.reshape(-1, D)], 0)
    normed = low(layer_norm(stacked, norm1_gain, norm1_shift))
    mixed = jnp.dot(normed, w_qkv, precision=HIGHEST_PRECISION) + jnp.concatenate([q_bias, jnp.zeros_like(q_bias), v_bias])
    queries = rounded(mixed[:, :D] * HEAD_DIM ** (-0.5))
    key_rows = rounded(mixed[:, D:2 * D])
    value_rows = rounded(mixed[:, 2 * D:])
    parts = []
    for start_row, end_row, tokens, table, lookup in ((0, split, TG, table_global, lookups[0]), (split, stacked.shape[0], TL, table_local, lookups[1])):
        bias = jnp.transpose(table[lookup], (2, 0, 1))
        shaped = [m[start_row:end_row].reshape(-1, tokens, HEADS, HEAD_DIM) for m in (queries, key_rows, value_rows)]
        parts.append(attend(shaped[0], shaped[1], shaped[2], bias).reshape(-1, D))
    merged = rounded(jnp.concatenate(parts, 0))
    branch = low_back(jnp.dot(merged, w_proj, precision=HIGHEST_PRECISION) + proj_bias)
    middle = stacked + scale_attn * branch
    normed2 = low(layer_norm(middle, norm2_gain, norm2_shift))
    hidden = low_back(jnp.dot(normed2, w_fc1, precision=HIGHEST_PRECISION) + fc1_bias)
    active = low(jax.nn.gelu(hidden, approximate=False))
    branch2 = low_back(jnp.dot(active, w_fc2, precision=HIGHEST_PRECISION) + fc2_bias)
    result = middle + scale_mlp * branch2
    return (result[:split].reshape(crops_g.shape), result[split:].reshape(crops_l.shape))

def reference(x_global, x_local, cot_global, cot_local, global_count, local_count, w_qkv, w_proj, w_fc1, w_fc2, norm1_gain, norm1_shift, q_bias, v_bias, proj_bias, scale_attn, norm2_gain, norm2_shift, fc1_bias, fc2_bias, scale_mlp, table_global, table_local):
    stacked = tuple((p.astype(jnp.float32) for p in (w_qkv, w_proj, w_fc1, w_fc2, norm1_gain, norm1_shift, q_bias, v_bias, proj_bias, scale_attn, norm2_gain, norm2_shift, fc1_bias, fc2_bias, scale_mlp, table_global, table_local)))
    lookups = (jnp.asarray(position_table(GRID_G)), jnp.asarray(position_table(GRID_L)))
    crops_g = x_global.astype(jnp.float32).reshape(DATA_SHARDS, G_DEV, TG, D)
    crops_l = x_local.astype(jnp.float32).reshape(DATA_SHARDS, L_DEV, TL, D)

    def forward(params, inputs_g, inputs_l, added_g, added_l):
        first_layer = tuple((p[0] for p in params))
        second_layer = tuple((p[1] for p in params))

        def step(items):
            part_g, part_l, extra_g, extra_l = items
            mid_g, mid_l = block(part_g, part_l, first_layer, lookups)
            mid_g = rounded(mid_g + extra_g)
            mid_l = rounded(mid_l + extra_l)
            end_g, end_l = block(mid_g, mid_l, second_layer, lookups)
            return (mid_g, mid_l, end_g, end_l)
        return lax.map(jax.checkpoint(step), (inputs_g, inputs_l, added_g, added_l))
    results, pull = jax.vjp(forward, stacked, crops_g, crops_l, jnp.zeros_like(crops_g), jnp.zeros_like(crops_l))
    mid_g, mid_l, end_g, end_l = results
    live_g = (jnp.arange(G_DEV, dtype=jnp.int32)[None, :] < global_count[:, None]).astype(jnp.float32)[:, :, None, None]
    live_l = (jnp.arange(L_DEV, dtype=jnp.int32)[None, :] < local_count[:, None]).astype(jnp.float32)[:, :, None, None]
    cotangents = (jnp.zeros_like(mid_g), jnp.zeros_like(mid_l), cot_global.astype(jnp.float32).reshape(crops_g.shape) * live_g, cot_local.astype(jnp.float32).reshape(crops_l.shape) * live_l)
    grad_params, grad_g, grad_l, grad_mid_g, grad_mid_l = pull(cotangents)
    out_global = (jnp.stack([mid_g, end_g]) * live_g[None]).reshape(2, GLOBAL_CROPS, TG, D).astype(jnp.bfloat16)
    out_local = (jnp.stack([mid_l, end_l]) * live_l[None]).reshape(2, LOCAL_CROPS, TL, D).astype(jnp.bfloat16)
    grad_global_in = jnp.stack([grad_g, grad_mid_g]).reshape(2, GLOBAL_CROPS, TG, D).astype(jnp.bfloat16)
    grad_local_in = jnp.stack([grad_l, grad_mid_l]).reshape(2, LOCAL_CROPS, TL, D).astype(jnp.bfloat16)
    grad_qkv, grad_proj, grad_fc1, grad_fc2, grad_n1g, grad_n1s, grad_qb, grad_vb, grad_pb, grad_sa, grad_n2g, grad_n2s, grad_f1b, grad_f2b, grad_sm, grad_tg, grad_tl = grad_params
    return (out_global, out_local, grad_global_in, grad_local_in, grad_qkv, grad_proj, grad_fc1, grad_fc2, grad_n1g, grad_n1s, grad_qb, grad_vb, grad_pb, grad_sa, grad_n2g, grad_n2s, grad_f1b, grad_f2b, grad_sm, grad_tg, grad_tl)
```

```python
import functools
import jax
import jax.numpy as jnp
import numpy as np
from jax import lax
from jax.experimental import pallas as pl
from jax.experimental.pallas import tpu as pltpu
from jax.sharding import PartitionSpec as P

GRID_G = 14
GRID_L = 6
ROWS = 256
LOCAL_ROW = 208
LANES_G = 512
LANES_L = 128
FRONT_L = 51
BLOCK = 256
NEG = -1e30
eps = 1e-06
F32 = jnp.float32
BF16 = jnp.bfloat16
INV_SQRT2 = 0.7071067811865476
INV_SQRT_2PI = 0.3989422804014327
N1G, N1S, QB, VB, PB, SA, N2G, N2S, F2B, SM, F1B = range(11)


def spread_index(grid, rows, lanes, front, cls_lane):
    side = 2 * grid - 1
    entries = side * side
    index = np.full((rows, lanes), -1, np.int32)
    for q in range(grid):
        for a in range(side):
            for k in range(grid):
                index[q, front + a * grid + k] = (side - 1 - a) * side + (q - k + grid - 1)
    index[rows - 2, :] = entries
    index[rows - 2, cls_lane] = entries + 2
    index[rows - 1, :] = entries + 1
    return index


INDEX_G = spread_index(GRID_G, 16, LANES_G, 1, 0)
INDEX_L = spread_index(GRID_L, 8, LANES_L, FRONT_L, LOCAL_ROW - 128)


def one_hot(index, count):
    flat = jnp.asarray(index.reshape(1, -1))
    return (lax.broadcasted_iota(jnp.int32, (count, flat.shape[1]), 0) == flat).astype(BF16)


def spread(table, index):
    heads = table.shape[1]
    flat = lax.dot_general(
        table, one_hot(index, table.shape[0]), (((0,), (0,)), ((), ())), preferred_element_type=F32
    )
    return flat.astype(BF16).reshape(heads, *index.shape)


def gather_back(values, index, count):
    heads = values.shape[0]
    flat = values.reshape(heads, -1)
    high = flat.astype(BF16)
    low = (flat - high.astype(F32)).astype(BF16)
    both = jnp.concatenate([high, low], 0)
    sums = lax.dot_general(
        one_hot(index, count), both, (((1,), (1,)), ((), ())), preferred_element_type=F32
    )
    return sums[:, :heads] + sums[:, heads:]


def dot(a, b):
    return lax.dot_general(a, b, (((1,), (0,)), ((), ())), preferred_element_type=F32)


def dot_cols(a, b):
    return lax.dot_general(a, b, (((1,), (1,)), ((), ())), preferred_element_type=F32)


def dot_rows(a, b):
    return lax.dot_general(a, b, (((0,), (0,)), ((), ())), preferred_element_type=F32)


def fetch(layer, pairs, sems):
    section = lax.axis_index("pipe")
    for number, (own, other, held) in enumerate(pairs):

        @pl.when(section == layer)
        def _():
            pltpu.make_async_copy(own, held, sems.at[number]).start()

        @pl.when(section != layer)
        def _():
            pltpu.make_async_copy(other, held, sems.at[number]).start()


def arrive(pairs, sems, number):
    own, other, held = pairs[number]
    pltpu.make_async_copy(own, held, sems.at[number]).wait()


def normalised(x):
    centered = x - jnp.mean(x, axis=-1, keepdims=True)
    rstd = lax.rsqrt(jnp.mean(centered * centered, axis=-1, keepdims=True) + eps)
    return centered * rstd, rstd


def row_steps(step, body):
    def one(i, carry):
        body(pl.ds(pl.multiple_of(i * step, step), step))
        return carry

    lax.fori_loop(0, ROWS // step, one, 0)


def build_bias(spread_g, spread_l, bias):
    for r in range(GRID_G):
        shifted = pltpu.roll(spread_g, (LANES_G - (GRID_G - 1 - r) * GRID_G) % LANES_G, 1)
        bias[pl.ds(1 + GRID_G * r, GRID_G), :] = shifted[:GRID_G, :ROWS]
    for r in range(GRID_L):
        shifted = pltpu.roll(spread_l, GRID_L * r, 1)
        bias[pl.ds(LOCAL_ROW + 1 + GRID_L * r, GRID_L), pl.ds(128, 128)] = shifted[:GRID_L, :]
    tokens_g = GRID_G * GRID_G + 1
    tokens_l = GRID_L * GRID_L + 1
    top = bias[:LOCAL_ROW, :]
    row = lax.broadcasted_iota(jnp.int32, top.shape, 0)
    col = lax.broadcasted_iota(jnp.int32, top.shape, 1)
    top = jnp.where(col == 0, spread_g[15:16, :ROWS], top)
    top = jnp.where(row == 0, spread_g[14:15, :ROWS], top)
    top = jnp.where(row >= tokens_g, 0.0, top)
    top = jnp.where(col >= tokens_g, NEG, top)
    low = bias[LOCAL_ROW:, 128:]
    row = lax.broadcasted_iota(jnp.int32, low.shape, 0)
    col = lax.broadcasted_iota(jnp.int32, low.shape, 1) - (LOCAL_ROW - 128)
    low = jnp.where(col == 0, spread_l[7:8], low)
    low = jnp.where(row == 0, spread_l[6:7], low)
    low = jnp.where(row >= tokens_l, 0.0, low)
    low = jnp.where((col >= 0) & (col < tokens_l), low, NEG)
    bottom = jnp.concatenate([jnp.full((ROWS - LOCAL_ROW, 128), NEG, F32), low], 1)
    return jnp.concatenate([top, bottom], 0)


def forward_kernel(
    layer, scale,
    x_ref, vec_ref, sg_ref, sl_ref,
    own_qkv, own_proj, own_fc1, own_fc2, oth_qkv, oth_proj, oth_fc1, oth_fc2,
    out_ref, n1_ref, q_ref, k_ref, v_ref, p_ref, merged_ref, branch_ref, middle_ref,
    n2_ref, act_ref, dact_ref, branch2_ref,
    w_qkv, w_proj, w_fc1, w_fc2, bias, sems,
):
    pairs = (
        (own_qkv, oth_qkv, w_qkv), (own_proj, oth_proj, w_proj),
        (own_fc1, oth_fc1, w_fc1), (own_fc2, oth_fc2, w_fc2),
    )
    fetch(layer, pairs, sems)
    width = x_ref.shape[1]
    heads = p_ref.shape[0]

    def vec(row):
        return vec_ref[row:row + 1, :]

    def norm1(rows):
        xhat, _ = normalised(x_ref[rows, :].astype(F32))
        n1_ref[rows, :] = (xhat * vec(N1G) + vec(N1S)).astype(BF16)

    row_steps(32, norm1)
    arrive(pairs, sems, 0)
    n1 = n1_ref[...]
    for b in range(0, width, BLOCK):
        cols = slice(b, b + BLOCK)
        mixed = dot(n1, w_qkv[:, b:b + BLOCK]) + vec_ref[QB:QB + 1, cols]
        q_ref[:, cols] = (mixed * scale).astype(BF16)
        k_ref[:, cols] = dot(n1, w_qkv[:, width + b:width + b + BLOCK]).astype(BF16)
        mixed = dot(n1, w_qkv[:, 2 * width + b:2 * width + b + BLOCK]) + vec_ref[VB:VB + 1, cols]
        v_ref[:, cols] = mixed.astype(BF16)
    lane = lax.broadcasted_iota(jnp.int32, (1, 128), 1)
    for pair in range(heads // 2):
        cols = slice(pair * 128, pair * 128 + 128)
        q, k, v = q_ref[:, cols], k_ref[:, cols], v_ref[:, cols]
        result = None
        for half in range(2):
            head = 2 * pair + half
            mine = (lane < 64) if half == 0 else (lane >= 64)
            scores = dot_cols(q, jnp.where(mine, k, jnp.zeros_like(k))) + build_bias(
                sg_ref[head].astype(F32), sl_ref[head].astype(F32), bias.at[head % 2]
            )
            expo = jnp.exp(scores - jnp.max(scores, axis=-1, keepdims=True))
            probs = expo * (1.0 / jnp.sum(expo, axis=-1, keepdims=True))
            p_ref[head] = probs
            part = dot(probs.astype(BF16), jnp.where(mine, v, jnp.zeros_like(v)))
            result = part if result is None else result + part
        merged_ref[:, cols] = result.astype(BF16)
    arrive(pairs, sems, 1)
    merged = merged_ref[...]
    for b in range(0, width, BLOCK):
        cols = slice(b, b + BLOCK)
        branch = dot(merged, w_proj[:, cols]) + vec_ref[PB:PB + 1, cols]
        branch_ref[:, cols] = branch
        middle_ref[:, cols] = x_ref[:, cols].astype(F32) + vec_ref[SA:SA + 1, cols] * branch

    def norm2(rows):
        xhat, _ = normalised(middle_ref[rows, :])
        n2_ref[rows, :] = (xhat * vec(N2G) + vec(N2S)).astype(BF16)

    row_steps(32, norm2)
    arrive(pairs, sems, 2)
    n2 = n2_ref[...]
    for b in range(0, w_fc1.shape[1], BLOCK):
        cols = slice(b, b + BLOCK)
        part = b // width
        hidden = dot(n2, w_fc1[:, cols]) + vec_ref[
            F1B + part:F1B + part + 1, b - part * width:b - part * width + BLOCK
        ]
        cdf = 0.5 + 0.5 * lax.erf(hidden * INV_SQRT2)
        act_ref[:, cols] = (hidden * cdf).astype(BF16)
        dact_ref[:, cols] = cdf + hidden * (INV_SQRT_2PI * jnp.exp(-0.5 * hidden * hidden))
    arrive(pairs, sems, 3)
    for b in range(0, width, BLOCK):
        cols = slice(b, b + BLOCK)
        branch2 = dot(act_ref[...], w_fc2[:, cols]) + vec_ref[F2B:F2B + 1, cols]
        branch2_ref[:, cols] = branch2
        out_ref[:, cols] = (middle_ref[:, cols] + vec_ref[SM:SM + 1, cols] * branch2).astype(BF16)


def backward_kernel(
    layer, scale,
    x_ref, g_ref, vec_ref, q_ref, k_ref, v_ref, p_ref, branch_ref, middle_ref, dact_ref, branch2_ref,
    own_qkv, own_proj, own_fc1, own_fc2, oth_qkv, oth_proj, oth_fc1, oth_fc2,
    gx_ref, gmixed_ref, gbranch_ref, ghidden_ref, gb2_ref, small_ref, tg_ref, tl_ref,
    w_qkv, w_proj, w_fc1, w_fc2, gmid, gnorm, gmerged, gs_ref, sems,
):
    pairs = (
        (own_fc2, oth_fc2, w_fc2), (own_fc1, oth_fc1, w_fc1),
        (own_proj, oth_proj, w_proj), (own_qkv, oth_qkv, w_qkv),
    )
    fetch(layer, pairs, sems)
    width = x_ref.shape[1]
    heads = p_ref.shape[0]
    small_ref[...] = jnp.zeros_like(small_ref)

    def vec(row):
        return vec_ref[row:row + 1, :]

    def add_small(row, values):
        small_ref[row:row + 1, :] += jnp.sum(values, axis=0, keepdims=True)

    def scaled(rows):
        grad = g_ref[rows, :].astype(F32)
        low = (vec(SM) * grad).astype(BF16)
        gb2_ref[rows, :] = low
        add_small(SM, grad * branch2_ref[rows, :])
        add_small(F2B, low.astype(F32))

    row_steps(32, scaled)
    arrive(pairs, sems, 0)
    gb2 = gb2_ref[...]
    for b in range(0, w_fc1.shape[1], BLOCK):
        cols = slice(b, b + BLOCK)
        part = b // width
        ghidden = (dot_cols(gb2, w_fc2[cols, :]) * dact_ref[:, cols]).astype(BF16)
        ghidden_ref[:, cols] = ghidden
        small_ref[F1B + part:F1B + part + 1, b - part * width:b - part * width + BLOCK] = jnp.sum(
            ghidden.astype(F32), axis=0, keepdims=True
        )
    arrive(pairs, sems, 1)
    for b in range(0, width, BLOCK):
        gnorm[:, b:b + BLOCK] = dot_cols(ghidden_ref[...], w_fc1[b:b + BLOCK, :])

    def norm_back(values, grad, gain):
        xhat, rstd = normalised(values)
        scaled_grad = grad * gain
        mean1 = jnp.mean(scaled_grad, axis=-1, keepdims=True)
        mean2 = jnp.mean(scaled_grad * xhat, axis=-1, keepdims=True)
        return xhat, rstd * (scaled_grad - mean1 - xhat * mean2)

    def norm2(rows):
        grad = gnorm[rows, :]
        xhat, through = norm_back(middle_ref[rows, :], grad, vec(N2G))
        grad_middle = g_ref[rows, :].astype(F32) + through
        gmid[rows, :] = grad_middle
        add_small(N2G, grad * xhat)
        add_small(N2S, grad)
        add_small(SA, grad_middle * branch_ref[rows, :])
        low = (vec(SA) * grad_middle).astype(BF16)
        gbranch_ref[rows, :] = low
        add_small(PB, low.astype(F32))

    row_steps(32, norm2)
    arrive(pairs, sems, 2)
    for b in range(0, width, BLOCK):
        gmerged[:, b:b + BLOCK] = dot_cols(gbranch_ref[...], w_proj[b:b + BLOCK, :]).astype(BF16)
    lane = lax.broadcasted_iota(jnp.int32, (1, 128), 1)
    lane_all = lax.broadcasted_iota(jnp.int32, (1, ROWS), 1)
    for pair in range(heads // 2):
        cols = slice(pair * 128, pair * 128 + 128)
        q, k, v, gm = q_ref[:, cols], k_ref[:, cols], v_ref[:, cols], gmerged[:, cols]
        gq = gk = gv = 0.0
        for half in range(2):
            head = 2 * pair + half
            mine = (lane < 64) if half == 0 else (lane >= 64)

            def only(values):
                return jnp.where(mine, values, jnp.zeros_like(values))

            probs = p_ref[head]
            grad_probs = dot_cols(gm, only(v))
            total = jnp.sum(probs * grad_probs, axis=-1, keepdims=True)
            gscores = (probs * (grad_probs - total)).astype(BF16)
            gv += dot_rows(probs.astype(BF16), only(gm))
            gq += dot(gscores, only(k))
            gk += dot_rows(gscores, only(q))
            wide = gscores.astype(F32)
            gs = gs_ref.at[head % 2]
            gs[...] = jnp.where((lane_all == 0) | (lane_all == LOCAL_ROW), 0.0, wide)
            acc = jnp.zeros((GRID_G, LANES_G), F32)
            for r in range(GRID_G):
                block = gs[pl.ds(1 + GRID_G * r, GRID_G), :]
                block = jnp.concatenate([block, jnp.zeros_like(block)], 1)
                acc += pltpu.roll(block, (GRID_G - 1 - r) * GRID_G, 1)
            first_row = wide[0:1, :]
            to_class = jnp.sum(wide[:LOCAL_ROW, :], axis=0, keepdims=True) - first_row
            to_class = jnp.where(lane_all == 0, to_class, 0.0)
            blank = jnp.zeros((1, LANES_G - ROWS), F32)
            tg_ref[head, 0:GRID_G, :] = acc
            tg_ref[head, 14:15, :] = jnp.concatenate([first_row, blank], 1)
            tg_ref[head, 15:16, :] = jnp.concatenate([to_class, blank], 1)
            acc = jnp.zeros((GRID_L, LANES_L), F32)
            for r in range(GRID_L):
                block = gs[pl.ds(LOCAL_ROW + 1 + GRID_L * r, GRID_L), pl.ds(128, 128)]
                acc += pltpu.roll(block, (LANES_L - GRID_L * r) % LANES_L, 1)
            first_row = wide[LOCAL_ROW:LOCAL_ROW + 1, 128:]
            to_class = jnp.sum(wide[LOCAL_ROW:, 128:], axis=0, keepdims=True) - first_row
            to_class = jnp.where(lane == LOCAL_ROW - 128, to_class, 0.0)
            tl_ref[head, 0:GRID_L, :] = acc
            tl_ref[head, 6:7, :] = first_row
            tl_ref[head, 7:8, :] = to_class
        gmixed_ref[:, cols] = gq.astype(BF16) * jnp.asarray(scale, BF16)
        gmixed_ref[:, slice(width + cols.start, width + cols.stop)] = gk.astype(BF16)
        gmixed_ref[:, slice(2 * width + cols.start, 2 * width + cols.stop)] = gv.astype(BF16)

    def biases(rows):
        add_small(QB, gmixed_ref[rows, :width].astype(F32))
        add_small(VB, gmixed_ref[rows, 2 * width:].astype(F32))

    row_steps(32, biases)
    arrive(pairs, sems, 3)
    for b in range(0, width, BLOCK):
        gnorm[:, b:b + BLOCK] = dot_cols(gmixed_ref[...], w_qkv[b:b + BLOCK, :])

    def norm1(rows):
        grad = gnorm[rows, :]
        xhat, through = norm_back(x_ref[rows, :].astype(F32), grad, vec(N1G))
        add_small(N1G, grad * xhat)
        add_small(N1S, grad)
        gx_ref[rows, :] = (gmid[rows, :] + through).astype(BF16)

    row_steps(32, norm1)


def shape(*dims, dtype=BF16):
    return jax.ShapeDtypeStruct(dims, dtype)


def forward(layer, x, vec, sg, sl, own, other):
    width = x.shape[1]
    hidden = own[2].shape[1]
    heads = sg.shape[0]
    scale = (width // heads) ** (-0.5)
    inside = pl.BlockSpec(memory_space=pltpu.VMEM)
    outside = pl.BlockSpec(memory_space=pl.ANY)
    return pl.pallas_call(
        functools.partial(forward_kernel, layer, scale),
        out_shape=(
            shape(ROWS, width), shape(ROWS, width), shape(ROWS, width), shape(ROWS, width),
            shape(ROWS, width), shape(heads, ROWS, ROWS, dtype=F32), shape(ROWS, width),
            shape(ROWS, width, dtype=F32), shape(ROWS, width, dtype=F32), shape(ROWS, width),
            shape(ROWS, hidden), shape(ROWS, hidden, dtype=F32), shape(ROWS, width, dtype=F32),
        ),
        in_specs=[inside] * 4 + [outside] * 8,
        out_specs=(inside,) * 13,
        scratch_shapes=[pltpu.VMEM(w.shape, BF16) for w in own]
        + [pltpu.VMEM((2, ROWS, ROWS), F32), pltpu.SemaphoreType.DMA((4,))],
        compiler_params=pltpu.CompilerParams(vmem_limit_bytes=60 * 2**20),
        name="layer_forward",
    )(x, vec, sg, sl, *own, *other)


def backward(layer, x, grad, vec, kept, heads, own, other):
    width = x.shape[1]
    hidden = own[2].shape[1]
    scale = (width // heads) ** (-0.5)
    inside = pl.BlockSpec(memory_space=pltpu.VMEM)
    outside = pl.BlockSpec(memory_space=pl.ANY)
    _, n1, q, k, v, probs, merged, branch, middle, n2, act, dact, branch2 = kept
    return pl.pallas_call(
        functools.partial(backward_kernel, layer, scale),
        out_shape=(
            shape(ROWS, width), shape(ROWS, 3 * width), shape(ROWS, width), shape(ROWS, hidden),
            shape(ROWS, width), shape(16, width, dtype=F32),
            shape(heads, 16, LANES_G, dtype=F32), shape(heads, 8, LANES_L, dtype=F32),
        ),
        in_specs=[inside] * 11 + [outside] * 8,
        out_specs=(inside,) * 8,
        scratch_shapes=[pltpu.VMEM(w.shape, BF16) for w in own]
        + [
            pltpu.VMEM((ROWS, width), F32), pltpu.VMEM((ROWS, width), F32),
            pltpu.VMEM((ROWS, width), BF16), pltpu.VMEM((2, ROWS, ROWS), F32),
            pltpu.SemaphoreType.DMA((4,)),
        ],
        compiler_params=pltpu.CompilerParams(vmem_limit_bytes=60 * 2**20),
        name="layer_backward",
    )(x, grad, vec, q, k, v, probs, branch, middle, dact, branch2, *own, *other)


def swapped(value):
    return lax.ppermute(value, "pipe", [(0, 1), (1, 0)])


def body(
    x_global, x_local, cot_global, cot_local, global_count, local_count,
    w_qkv, w_proj, w_fc1, w_fc2,
    norm1_gain, norm1_shift, q_bias, v_bias, proj_bias, scale_attn,
    norm2_gain, norm2_shift, fc1_bias, fc2_bias, scale_mlp,
    table_global, table_local,
):
    section = lax.axis_index("pipe")
    width = x_global.shape[2]
    heads = table_global.shape[2]
    tokens_g, tokens_l = x_global.shape[1], x_local.shape[1]
    own = (w_qkv[0], w_proj[0], w_fc1[0], w_fc2[0])
    other = tuple(swapped(w) for w in own)
    vec = jnp.concatenate(
        [norm1_gain, norm1_shift, q_bias, v_bias, proj_bias, scale_attn, norm2_gain, norm2_shift,
         fc2_bias, scale_mlp, fc1_bias.reshape(-1, width)], 0)
    sg = spread(table_global[0], INDEX_G)
    sl = spread(table_local[0], INDEX_L)
    smalls_own = (vec, sg, sl)
    smalls_other = tuple(swapped(s) for s in smalls_own)

    def by_layer(mine, theirs):
        first = jnp.where(section == 0, mine, theirs)
        second = jnp.where(section == 0, theirs, mine)
        return first, second

    (vec0, vec1), (sg0, sg1), (sl0, sl1) = (by_layer(a, b) for a, b in zip(smalls_own, smalls_other))
    vec0, vec1 = vec0.astype(F32), vec1.astype(F32)

    def packed(array_g, array_l):
        crop_g = lax.dynamic_index_in_dim(array_g, section, 0, keepdims=False)
        crop_l = lax.dynamic_index_in_dim(array_l, section, 0, keepdims=False)
        crop_g = jnp.pad(crop_g, ((0, LOCAL_ROW - tokens_g), (0, 0)))
        crop_l = jnp.pad(crop_l, ((0, ROWS - LOCAL_ROW - tokens_l), (0, 0)))
        return jnp.concatenate([crop_g, crop_l], 0)

    x = packed(x_global, x_local)
    live_g = (global_count[0] > section).astype(BF16)
    live_l = (local_count[0] > section).astype(BF16)
    cot = packed(cot_global * live_g, cot_local * live_l)

    kept0 = forward(0, x, vec0, sg0, sl0, own, other)
    first = kept0[0]
    kept1 = forward(1, first, vec1, sg1, sl1, own, other)
    second = kept1[0]
    back1 = backward(1, first, cot, vec1, kept1, heads, own, other)
    grad_first = back1[0]
    back0 = backward(0, x, grad_first, vec0, kept0, heads, own, other)
    grad_x = back0[0]

    def exchange(layer0, layer1):
        keep = jnp.where(section == 0, layer0, layer1)
        send = jnp.where(section == 0, layer1, layer0)
        return keep, swapped(send)

    def both_crops(keep, came):
        low = jnp.where(section == 0, keep, came)
        high = jnp.where(section == 0, came, keep)
        return (
            jnp.stack([low[:tokens_g], high[:tokens_g]]),
            jnp.stack([low[LOCAL_ROW:LOCAL_ROW + tokens_l], high[LOCAL_ROW:LOCAL_ROW + tokens_l]]),
        )

    out_g, out_l = both_crops(*exchange(first, second))
    crop = jnp.arange(2, dtype=jnp.int32)[:, None, None]
    out_g = jnp.where(crop < global_count[0], out_g, jnp.zeros_like(out_g))
    out_l = jnp.where(crop < local_count[0], out_l, jnp.zeros_like(out_l))
    gin_g, gin_l = both_crops(*exchange(grad_x, grad_first))

    def operand(layer0, layer1):
        return jnp.concatenate(exchange(layer0, layer1), 0)

    lefts = [operand(kept0[i], kept1[i]) for i in (1, 6, 9, 10)]
    rights = [operand(back0[i], back1[i]) for i in (1, 2, 3, 4)]
    shares = [
        lax.psum_scatter(dot_rows(a, b).astype(BF16), "dp", scatter_dimension=0, tiled=True).astype(F32)
        for a, b in zip(lefts, rights)
    ]
    keep, came = [], []
    for i in (5, 6, 7):
        a, b = exchange(back0[i], back1[i])
        keep.append(a)
        came.append(b)
    small, tg, tl = (a + b for a, b in zip(keep, came))
    tg = gather_back(tg, INDEX_G, table_global.shape[1])
    tl = gather_back(tl, INDEX_L, table_local.shape[1])
    small, tg, tl = lax.psum((small, tg, tl), "dp")
    hidden = fc1_bias.shape[1]
    return (
        out_g[None], out_l[None], gin_g[None], gin_l[None],
        *(s[None] for s in shares),
        small[N1G:N1G + 1], small[N1S:N1S + 1], small[QB:QB + 1], small[VB:VB + 1],
        small[PB:PB + 1], small[SA:SA + 1], small[N2G:N2G + 1], small[N2S:N2S + 1],
        small[F1B:F1B + hidden // width].reshape(1, hidden),
        small[F2B:F2B + 1], small[SM:SM + 1],
        tg[None], tl[None],
    )


def solution(mesh):
    three, two = P("pipe", None, None), P("pipe", None)
    rows = P("dp", None, None)
    in_specs = (rows,) * 4 + (P("dp"),) * 2 + (three,) * 4 + (two,) * 11 + (three,) * 2
    crops = P("pipe", "dp", None, None)
    out_specs = (crops,) * 4 + (P("pipe", "dp", None),) * 4 + (two,) * 11 + (three,) * 2
    return jax.shard_map(body, mesh=mesh, in_specs=in_specs, out_specs=out_specs, check_vma=False)
```

```python
import functools
import jax
import jax.numpy as jnp
import numpy as np
from jax import lax
from jax.experimental import pallas as pl
from jax.experimental.pallas import tpu as pltpu
from jax.sharding import PartitionSpec as P

GRID_G = 14
GRID_L = 6
ROWS = 256
LOCAL_ROW = 208
LANES_G = 512
LANES_L = 128
FRONT_L = 51
BLOCK = 256
NEG = -1e30
eps = 1e-06
F32 = jnp.float32
BF16 = jnp.bfloat16
INV_SQRT2 = 0.7071067811865476
INV_SQRT_2PI = 0.3989422804014327
N1G, N1S, QB, VB, PB, SA, N2G, N2S, F2B, SM, F1B = range(11)


def spread_index(grid, rows, lanes, front, cls_lane):
    side = 2 * grid - 1
    entries = side * side
    index = np.full((rows, lanes), -1, np.int32)
    for q in range(grid):
        for a in range(side):
            for k in range(grid):
                index[q, front + a * grid + k] = (side - 1 - a) * side + (q - k + grid - 1)
    index[rows - 2, :] = entries
    index[rows - 2, cls_lane] = entries + 2
    index[rows - 1, :] = entries + 1
    return index


INDEX_G = spread_index(GRID_G, 16, LANES_G, 1, 0)
INDEX_L = spread_index(GRID_L, 8, LANES_L, FRONT_L, LOCAL_ROW - 128)


def one_hot(index, count):
    flat = jnp.asarray(index.reshape(1, -1))
    return (lax.broadcasted_iota(jnp.int32, (count, flat.shape[1]), 0) == flat).astype(BF16)


def spread(table, index):
    heads = table.shape[1]
    flat = lax.dot_general(
        table, one_hot(index, table.shape[0]), (((0,), (0,)), ((), ())), preferred_element_type=F32
    )
    return flat.astype(BF16).reshape(heads, *index.shape)


def gather_back(values, index, count):
    heads = values.shape[0]
    flat = values.reshape(heads, -1)
    high = flat.astype(BF16)
    low = (flat - high.astype(F32)).astype(BF16)
    both = jnp.concatenate([high, low], 0)
    sums = lax.dot_general(
        one_hot(index, count), both, (((1,), (1,)), ((), ())), preferred_element_type=F32
    )
    return sums[:, :heads] + sums[:, heads:]


def dot(a, b):
    return lax.dot_general(a, b, (((1,), (0,)), ((), ())), preferred_element_type=F32)


def dot_cols(a, b):
    return lax.dot_general(a, b, (((1,), (1,)), ((), ())), preferred_element_type=F32)


def dot_rows(a, b):
    return lax.dot_general(a, b, (((0,), (0,)), ((), ())), preferred_element_type=F32)


def fetch(layer, pairs, sems):
    section = lax.axis_index("pipe")
    for number, (own, other, held) in enumerate(pairs):

        @pl.when(section == layer)
        def _():
            pltpu.make_async_copy(own, held, sems.at[number]).start()

        @pl.when(section != layer)
        def _():
            pltpu.make_async_copy(other, held, sems.at[number]).start()


def arrive(pairs, sems, number):
    own, other, held = pairs[number]
    pltpu.make_async_copy(own, held, sems.at[number]).wait()


def normalised(x):
    centered = x - jnp.mean(x, axis=-1, keepdims=True)
    rstd = lax.rsqrt(jnp.mean(centered * centered, axis=-1, keepdims=True) + eps)
    return centered * rstd, rstd


def row_steps(step, body):
    def one(i, carry):
        body(pl.ds(pl.multiple_of(i * step, step), step))
        return carry

    lax.fori_loop(0, ROWS // step, one, 0)


def build_bias(spread_g, spread_l, bias):
    for r in range(GRID_G):
        shifted = pltpu.roll(spread_g, (LANES_G - (GRID_G - 1 - r) * GRID_G) % LANES_G, 1)
        bias[pl.ds(1 + GRID_G * r, GRID_G), :] = shifted[:GRID_G, :ROWS]
    for r in range(GRID_L):
        shifted = pltpu.roll(spread_l, GRID_L * r, 1)
        bias[pl.ds(LOCAL_ROW + 1 + GRID_L * r, GRID_L), pl.ds(128, 128)] = shifted[:GRID_L, :]
    tokens_g = GRID_G * GRID_G + 1
    tokens_l = GRID_L * GRID_L + 1
    top = bias[:LOCAL_ROW, :]
    row = lax.broadcasted_iota(jnp.int32, top.shape, 0)
    col = lax.broadcasted_iota(jnp.int32, top.shape, 1)
    top = jnp.where(col == 0, spread_g[15:16, :ROWS], top)
    top = jnp.where(row == 0, spread_g[14:15, :ROWS], top)
    top = jnp.where(row >= tokens_g, 0.0, top)
    top = jnp.where(col >= tokens_g, NEG, top)
    low = bias[LOCAL_ROW:, 128:]
    row = lax.broadcasted_iota(jnp.int32, low.shape, 0)
    col = lax.broadcasted_iota(jnp.int32, low.shape, 1) - (LOCAL_ROW - 128)
    low = jnp.where(col == 0, spread_l[7:8], low)
    low = jnp.where(row == 0, spread_l[6:7], low)
    low = jnp.where(row >= tokens_l, 0.0, low)
    low = jnp.where((col >= 0) & (col < tokens_l), low, NEG)
    bottom = jnp.concatenate([jnp.full((ROWS - LOCAL_ROW, 128), NEG, F32), low], 1)
    return jnp.concatenate([top, bottom], 0)


def forward_kernel(
    layer, scale,
    x_ref, vec_ref, sg_ref, sl_ref,
    own_qkv, own_proj, own_fc1, own_fc2, oth_qkv, oth_proj, oth_fc1, oth_fc2,
    out_ref, n1_ref, q_ref, k_ref, v_ref, p_ref, merged_ref, branch_ref, middle_ref,
    n2_ref, act_ref, dact_ref, branch2_ref,
    w_qkv, w_proj, w_fc1, w_fc2, bias, sems,
):
    pairs = (
        (own_qkv, oth_qkv, w_qkv), (own_proj, oth_proj, w_proj),
        (own_fc1, oth_fc1, w_fc1), (own_fc2, oth_fc2, w_fc2),
    )
    fetch(layer, pairs, sems)
    width = x_ref.shape[1]
    heads = p_ref.shape[0]

    def vec(row):
        return vec_ref[row:row + 1, :]

    def norm1(rows):
        xhat, _ = normalised(x_ref[rows, :].astype(F32))
        n1_ref[rows, :] = (xhat * vec(N1G) + vec(N1S)).astype(BF16)

    row_steps(32, norm1)
    arrive(pairs, sems, 0)
    n1 = n1_ref[...]
    for b in range(0, width, BLOCK):
        cols = slice(b, b + BLOCK)
        mixed = dot(n1, w_qkv[:, b:b + BLOCK]) + vec_ref[QB:QB + 1, cols]
        q_ref[:, cols] = (mixed * scale).astype(BF16)
        k_ref[:, cols] = dot(n1, w_qkv[:, width + b:width + b + BLOCK]).astype(BF16)
        mixed = dot(n1, w_qkv[:, 2 * width + b:2 * width + b + BLOCK]) + vec_ref[VB:VB + 1, cols]
        v_ref[:, cols] = mixed.astype(BF16)
    lane = lax.broadcasted_iota(jnp.int32, (1, 128), 1)
    for pair in range(heads // 2):
        cols = slice(pair * 128, pair * 128 + 128)
        q, k, v = q_ref[:, cols], k_ref[:, cols], v_ref[:, cols]
        result = None
        for half in range(2):
            head = 2 * pair + half
            mine = (lane < 64) if half == 0 else (lane >= 64)
            scores = dot_cols(q, jnp.where(mine, k, jnp.zeros_like(k))) + build_bias(
                sg_ref[head].astype(F32), sl_ref[head].astype(F32), bias.at[head % 2]
            )
            expo = jnp.exp(scores - jnp.max(scores, axis=-1, keepdims=True))
            probs = expo * (1.0 / jnp.sum(expo, axis=-1, keepdims=True))
            p_ref[head] = probs
            part = dot(probs.astype(BF16), jnp.where(mine, v, jnp.zeros_like(v)))
            result = part if result is None else result + part
        merged_ref[:, cols] = result.astype(BF16)
    arrive(pairs, sems, 1)
    merged = merged_ref[...]
    for b in range(0, width, BLOCK):
        cols = slice(b, b + BLOCK)
        branch = dot(merged, w_proj[:, cols]) + vec_ref[PB:PB + 1, cols]
        branch_ref[:, cols] = branch
        middle_ref[:, cols] = x_ref[:, cols].astype(F32) + vec_ref[SA:SA + 1, cols] * branch

    def norm2(rows):
        xhat, _ = normalised(middle_ref[rows, :])
        n2_ref[rows, :] = (xhat * vec(N2G) + vec(N2S)).astype(BF16)

    row_steps(32, norm2)
    arrive(pairs, sems, 2)
    n2 = n2_ref[...]
    for b in range(0, w_fc1.shape[1], BLOCK):
        cols = slice(b, b + BLOCK)
        part = b // width
        hidden = dot(n2, w_fc1[:, cols]) + vec_ref[
            F1B + part:F1B + part + 1, b - part * width:b - part * width + BLOCK
        ]
        cdf = 0.5 + 0.5 * lax.erf(hidden * INV_SQRT2)
        act_ref[:, cols] = (hidden * cdf).astype(BF16)
        dact_ref[:, cols] = cdf + hidden * (INV_SQRT_2PI * jnp.exp(-0.5 * hidden * hidden))
    arrive(pairs, sems, 3)
    for b in range(0, width, BLOCK):
        cols = slice(b, b + BLOCK)
        branch2 = dot(act_ref[...], w_fc2[:, cols]) + vec_ref[F2B:F2B + 1, cols]
        branch2_ref[:, cols] = branch2
        out_ref[:, cols] = (middle_ref[:, cols] + vec_ref[SM:SM + 1, cols] * branch2).astype(BF16)


def backward_kernel(
    layer, scale,
    x_ref, g_ref, vec_ref, q_ref, k_ref, v_ref, p_ref, branch_ref, middle_ref, dact_ref, branch2_ref,
    own_qkv, own_proj, own_fc1, own_fc2, oth_qkv, oth_proj, oth_fc1, oth_fc2,
    gx_ref, gmixed_ref, gbranch_ref, ghidden_ref, gb2_ref, small_ref, tg_ref, tl_ref,
    w_qkv, w_proj, w_fc1, w_fc2, gmid, gnorm, gmerged, gs_ref, sems,
):
    pairs = (
        (own_fc2, oth_fc2, w_fc2), (own_fc1, oth_fc1, w_fc1),
        (own_proj, oth_proj, w_proj), (own_qkv, oth_qkv, w_qkv),
    )
    fetch(layer, pairs, sems)
    width = x_ref.shape[1]
    heads = p_ref.shape[0]
    small_ref[...] = jnp.zeros_like(small_ref)

    def vec(row):
        return vec_ref[row:row + 1, :]

    def add_small(row, values):
        small_ref[row:row + 1, :] += jnp.sum(values, axis=0, keepdims=True)

    def scaled(rows):
        grad = g_ref[rows, :].astype(F32)
        low = (vec(SM) * grad).astype(BF16)
        gb2_ref[rows, :] = low
        add_small(SM, grad * branch2_ref[rows, :])
        add_small(F2B, low.astype(F32))

    row_steps(32, scaled)
    arrive(pairs, sems, 0)
    gb2 = gb2_ref[...]
    for b in range(0, w_fc1.shape[1], BLOCK):
        cols = slice(b, b + BLOCK)
        part = b // width
        ghidden = (dot_cols(gb2, w_fc2[cols, :]) * dact_ref[:, cols]).astype(BF16)
        ghidden_ref[:, cols] = ghidden
        small_ref[F1B + part:F1B + part + 1, b - part * width:b - part * width + BLOCK] = jnp.sum(
            ghidden.astype(F32), axis=0, keepdims=True
        )
    arrive(pairs, sems, 1)
    for b in range(0, width, BLOCK):
        gnorm[:, b:b + BLOCK] = dot_cols(ghidden_ref[...], w_fc1[b:b + BLOCK, :])

    def norm_back(values, grad, gain):
        xhat, rstd = normalised(values)
        scaled_grad = grad * gain
        mean1 = jnp.mean(scaled_grad, axis=-1, keepdims=True)
        mean2 = jnp.mean(scaled_grad * xhat, axis=-1, keepdims=True)
        return xhat, rstd * (scaled_grad - mean1 - xhat * mean2)

    def norm2(rows):
        grad = gnorm[rows, :]
        xhat, through = norm_back(middle_ref[rows, :], grad, vec(N2G))
        grad_middle = g_ref[rows, :].astype(F32) + through
        gmid[rows, :] = grad_middle
        add_small(N2G, grad * xhat)
        add_small(N2S, grad)
        add_small(SA, grad_middle * branch_ref[rows, :])
        low = (vec(SA) * grad_middle).astype(BF16)
        gbranch_ref[rows, :] = low
        add_small(PB, low.astype(F32))

    row_steps(32, norm2)
    arrive(pairs, sems, 2)
    for b in range(0, width, BLOCK):
        gmerged[:, b:b + BLOCK] = dot_cols(gbranch_ref[...], w_proj[b:b + BLOCK, :]).astype(BF16)
    lane = lax.broadcasted_iota(jnp.int32, (1, 128), 1)
    lane_all = lax.broadcasted_iota(jnp.int32, (1, ROWS), 1)
    for pair in range(heads // 2):
        cols = slice(pair * 128, pair * 128 + 128)
        q, k, v, gm = q_ref[:, cols], k_ref[:, cols], v_ref[:, cols], gmerged[:, cols]
        gq = gk = gv = 0.0
        for half in range(2):
            head = 2 * pair + half
            mine = (lane < 64) if half == 0 else (lane >= 64)

            def only(values):
                return jnp.where(mine, values, jnp.zeros_like(values))

            probs = p_ref[head]
            grad_probs = dot_cols(gm, only(v))
            total = jnp.sum(probs * grad_probs, axis=-1, keepdims=True)
            gscores = (probs * (grad_probs - total)).astype(BF16)
            gv += dot_rows(probs.astype(BF16), only(gm))
            gq += dot(gscores, only(k))
            gk += dot_rows(gscores, only(q))
            wide = gscores.astype(F32)
            gs = gs_ref.at[head % 2]
            gs[...] = jnp.where((lane_all == 0) | (lane_all == LOCAL_ROW), 0.0, wide)
            acc = jnp.zeros((GRID_G, LANES_G), F32)
            for r in range(GRID_G):
                block = gs[pl.ds(1 + GRID_G * r, GRID_G), :]
                block = jnp.concatenate([block, jnp.zeros_like(block)], 1)
                acc += pltpu.roll(block, (GRID_G - 1 - r) * GRID_G, 1)
            first_row = wide[0:1, :]
            to_class = jnp.sum(wide[:LOCAL_ROW, :], axis=0, keepdims=True) - first_row
            to_class = jnp.where(lane_all == 0, to_class, 0.0)
            blank = jnp.zeros((1, LANES_G - ROWS), F32)
            tg_ref[head, 0:GRID_G, :] = acc
            tg_ref[head, 14:15, :] = jnp.concatenate([first_row, blank], 1)
            tg_ref[head, 15:16, :] = jnp.concatenate([to_class, blank], 1)
            acc = jnp.zeros((GRID_L, LANES_L), F32)
            for r in range(GRID_L):
                block = gs[pl.ds(LOCAL_ROW + 1 + GRID_L * r, GRID_L), pl.ds(128, 128)]
                acc += pltpu.roll(block, (LANES_L - GRID_L * r) % LANES_L, 1)
            first_row = wide[LOCAL_ROW:LOCAL_ROW + 1, 128:]
            to_class = jnp.sum(wide[LOCAL_ROW:, 128:], axis=0, keepdims=True) - first_row
            to_class = jnp.where(lane == LOCAL_ROW - 128, to_class, 0.0)
            tl_ref[head, 0:GRID_L, :] = acc
            tl_ref[head, 6:7, :] = first_row
            tl_ref[head, 7:8, :] = to_class
        gmixed_ref[:, cols] = gq.astype(BF16) * jnp.asarray(scale, BF16)
        gmixed_ref[:, slice(width + cols.start, width + cols.stop)] = gk.astype(BF16)
        gmixed_ref[:, slice(2 * width + cols.start, 2 * width + cols.stop)] = gv.astype(BF16)

    def biases(rows):
        add_small(QB, gmixed_ref[rows, :width].astype(F32))
        add_small(VB, gmixed_ref[rows, 2 * width:].astype(F32))

    row_steps(32, biases)
    arrive(pairs, sems, 3)
    for b in range(0, width, BLOCK):
        gnorm[:, b:b + BLOCK] = dot_cols(gmixed_ref[...], w_qkv[b:b + BLOCK, :])

    def norm1(rows):
        grad = gnorm[rows, :]
        xhat, through = norm_back(x_ref[rows, :].astype(F32), grad, vec(N1G))
        add_small(N1G, grad * xhat)
        add_small(N1S, grad)
        gx_ref[rows, :] = (gmid[rows, :] + through).astype(BF16)

    row_steps(32, norm1)


def shape(*dims, dtype=BF16):
    return jax.ShapeDtypeStruct(dims, dtype)


def forward(layer, x, vec, sg, sl, own, other):
    width = x.shape[1]
    hidden = own[2].shape[1]
    heads = sg.shape[0]
    scale = (width // heads) ** (-0.5)
    inside = pl.BlockSpec(memory_space=pltpu.VMEM)
    outside = pl.BlockSpec(memory_space=pl.ANY)
    return pl.pallas_call(
        functools.partial(forward_kernel, layer, scale),
        out_shape=(
            shape(ROWS, width), shape(ROWS, width), shape(ROWS, width), shape(ROWS, width),
            shape(ROWS, width), shape(heads, ROWS, ROWS, dtype=F32), shape(ROWS, width),
            shape(ROWS, width, dtype=F32), shape(ROWS, width, dtype=F32), shape(ROWS, width),
            shape(ROWS, hidden), shape(ROWS, hidden, dtype=F32), shape(ROWS, width, dtype=F32),
        ),
        in_specs=[inside] * 4 + [outside] * 8,
        out_specs=(inside,) * 13,
        scratch_shapes=[pltpu.VMEM(w.shape, BF16) for w in own]
        + [pltpu.VMEM((2, ROWS, ROWS), F32), pltpu.SemaphoreType.DMA((4,))],
        compiler_params=pltpu.CompilerParams(vmem_limit_bytes=60 * 2**20),
        name="layer_forward",
    )(x, vec, sg, sl, *own, *other)


def backward(layer, x, grad, vec, kept, heads, own, other):
    width = x.shape[1]
    hidden = own[2].shape[1]
    scale = (width // heads) ** (-0.5)
    inside = pl.BlockSpec(memory_space=pltpu.VMEM)
    outside = pl.BlockSpec(memory_space=pl.ANY)
    _, n1, q, k, v, probs, merged, branch, middle, n2, act, dact, branch2 = kept
    return pl.pallas_call(
        functools.partial(backward_kernel, layer, scale),
        out_shape=(
            shape(ROWS, width), shape(ROWS, 3 * width), shape(ROWS, width), shape(ROWS, hidden),
            shape(ROWS, width), shape(16, width, dtype=F32),
            shape(heads, 16, LANES_G, dtype=F32), shape(heads, 8, LANES_L, dtype=F32),
        ),
        in_specs=[inside] * 11 + [outside] * 8,
        out_specs=(inside,) * 8,
        scratch_shapes=[pltpu.VMEM(w.shape, BF16) for w in own]
        + [
            pltpu.VMEM((ROWS, width), F32), pltpu.VMEM((ROWS, width), F32),
            pltpu.VMEM((ROWS, width), BF16), pltpu.VMEM((2, ROWS, ROWS), F32),
            pltpu.SemaphoreType.DMA((4,)),
        ],
        compiler_params=pltpu.CompilerParams(vmem_limit_bytes=60 * 2**20),
        name="layer_backward",
    )(x, grad, vec, q, k, v, probs, branch, middle, dact, branch2, *own, *other)


MESH = pl.DeviceIdType.MESH
SIDE = 2


def remote(source, target, sent, came, **device):
    return pltpu.make_async_remote_copy(
        src_ref=source, dst_ref=target, send_sem=sent, recv_sem=came,
        device_id=device, device_id_type=MESH,
    )


def add_rows(total, start, extra, count):
    def one(i, carry):
        rows = pl.ds(pl.multiple_of(start + i * 16, 16), 16)
        here = pl.ds(pl.multiple_of(i * 16, 16), 16)
        total[rows, :] = (total[rows, :].astype(F32) + extra[here, :].astype(F32)).astype(BF16)
        return carry

    lax.fori_loop(0, count // 16, one, 0)


def scatter_kernel(count, *refs):
    first, second = refs[:8], refs[8:16]
    out_qkv, out_proj, out_fc1, out_fc2 = refs[16:20]
    held = refs[20:28]
    sum_a, sum_b, sum_c = refs[28:31]
    in_a1, in_a2, in_a3, in_b1, in_b2, in_b3, in_c1, in_c2, in_c3 = refs[31:40]
    local_sem, swap_sent, swap_came = refs[40:43]
    sent, came = refs[43:52], refs[52:61]
    depth = count // (SIDE * SIDE)
    width = held[0].shape[1]
    section = lax.axis_index("pipe")
    place = lax.axis_index("dp")
    x = place % SIDE
    y = (place // SIDE) % SIDE
    z = place // (SIDE * SIDE)

    def index(zz, yy, xx):
        return (zz * SIDE + yy) * SIDE + xx

    across_x, across_y = index(z, y, 1 - x), index(z, 1 - y, x)

    barrier = pltpu.get_barrier_semaphore()
    pl.semaphore_signal(barrier, inc=1, device_id={"pipe": 1 - section}, device_id_type=MESH)
    for peer in (across_x, across_y):
        pl.semaphore_signal(barrier, inc=1, device_id={"dp": peer}, device_id_type=MESH)
    for step in range(1, depth):
        peer = index((z + step) % depth, y, x)
        pl.semaphore_signal(barrier, inc=1, device_id={"dp": peer}, device_id_type=MESH)
    pl.semaphore_wait(barrier, 3 + depth - 1)

    order = (0, 4, 2, 6, 1, 5, 3, 7)
    for i in order:
        mine = held[i].at[pl.ds(0, ROWS), :]
        theirs = held[i].at[pl.ds(ROWS, ROWS), :]

        @pl.when(section == 0)
        def _():
            remote(second[i], theirs, swap_sent.at[i], swap_came.at[i], pipe=1 - section).start()
            pltpu.make_async_copy(first[i], mine, local_sem.at[i]).start()

        @pl.when(section != 0)
        def _():
            remote(first[i], theirs, swap_sent.at[i], swap_came.at[i], pipe=1 - section).start()
            pltpu.make_async_copy(second[i], mine, local_sem.at[i]).start()

    def operands(*numbers):
        for i in numbers:
            mine = held[i].at[pl.ds(0, ROWS), :]
            theirs = held[i].at[pl.ds(ROWS, ROWS), :]
            pltpu.make_async_copy(first[i], mine, local_sem.at[i]).wait()
            remote(first[i], theirs, swap_sent.at[i], swap_came.at[i], pipe=1 - section).wait_recv()

    def product(left, right, total, offset):
        def one(i, carry):
            start = pl.multiple_of(i * BLOCK, BLOCK)
            rows = left[:, pl.ds(start, BLOCK)]
            for b in range(0, right.shape[1], width):
                part = dot_rows(rows, right[:, b:b + width])
                total[pl.ds(start, BLOCK), offset + b:offset + b + width] = part.astype(BF16)
            return carry

        lax.fori_loop(0, left.shape[1] // BLOCK, one, 0)

    def target(k):
        low = jnp.where(k < depth - 1 - z, depth - 1 - k, k - (depth - 1 - z))
        high = jnp.where(k < z, k, depth - 1 - (k - z))
        return jnp.where(z < depth // 2, low, high)

    targets = [target(k) for k in range(depth)]
    ups = [jnp.where(targets[k] > z, 1, 0) for k in range(depth - 1)]
    starts_line = (z == 0) | (z == depth - 1)

    def chunk(total, zz, yy, xx):
        rows = total.shape[0] // count
        return pl.ds(pl.multiple_of(index(zz, yy, xx) * rows, rows), rows)

    def accumulate(total, zz, yy, xx, extra):
        rows = total.shape[0] // count
        add_rows(total, pl.multiple_of(index(zz, yy, xx) * rows, rows), extra, rows)

    def line_copy(total, slots, group, k, c, yy, xx, width_of):
        up = ups[k]
        slot = (targets[k] + up) * width_of + c
        number = k * width_of + c
        source = total.at[chunk(total, targets[k], yy, xx), :]
        peer = index(z + 2 * up - 1, y, x)
        return slot, remote(
            source, slots.at[slot], sent[group].at[number], came[group].at[slot], dp=peer
        )

    def line_receive(total, slots, group, k, slot, yy, xx):
        here = slots.at[slot]
        peer = index(z + 1 - 2 * ups[k], y, x)
        remote(here, here, sent[group].at[0], came[group].at[slot], dp=peer).wait_recv()
        accumulate(total, targets[k], yy, xx, here)

    c_parts = ((1 - y, 1 - x), (y, 1 - x), (1 - y, x), (y, x))
    operands(0, 4)
    product(held[0], held[4], sum_c, 0)

    @pl.when(starts_line)
    def _():
        for k in range(depth - 1):
            for c, (yy, xx) in enumerate(c_parts):
                line_copy(sum_c, in_c1, 6, k, c, yy, xx, 4)[1].start()

    def line_c(k, c):
        yy, xx = c_parts[c]

        @pl.when(jnp.logical_not(starts_line))
        def _():
            slot, copy = line_copy(sum_c, in_c1, 6, k, c, yy, xx, 4)
            line_receive(sum_c, in_c1, 6, k, slot, yy, xx)
            copy.start()

    def first_copy(which, i):
        yy_other = i < depth
        zz = targets[i % depth]
        if which == 0:
            where = (zz, 1 - y if yy_other else y, 1 - x)
            total, slots, peer = sum_a, in_a1, across_x
        else:
            where = (zz, 1 - y, 1 - x if yy_other else x)
            total, slots, peer = sum_b, in_b1, across_y
        source = total.at[chunk(total, *where), :]
        group = 0 if which == 0 else 3
        return remote(source, slots.at[i], sent[group].at[i], came[group].at[i], dp=peer)

    def second_copy(which, i):
        where = (targets[i], 1 - y, x) if which == 0 else (targets[i], y, 1 - x)
        total, slots, peer = (sum_a, in_a2, across_y) if which == 0 else (sum_b, in_b2, across_x)
        group = 1 if which == 0 else 4
        source = total.at[chunk(total, *where), :]
        return remote(source, slots.at[i], sent[group].at[i], came[group].at[i], dp=peer)

    def first_receive(which, i):
        first_copy(which, i).wait_recv()
        zz = targets[i % depth]
        if which == 0:
            where = (zz, 1 - y if i < depth else y, x)
            accumulate(sum_a, *where, in_a1.at[i])
        else:
            where = (zz, y, 1 - x if i < depth else x)
            accumulate(sum_b, *where, in_b1.at[i])
        if i < depth:
            second_copy(which, i).start()

    def line(which, k):
        total, came_in, slots = (sum_a, in_a2, in_a3) if which == 0 else (sum_b, in_b2, in_b3)
        group = 2 if which == 0 else 5
        second_copy(which, k).wait_recv()
        accumulate(total, targets[k], y, x, came_in.at[k])
        if k < depth - 1:
            slot, copy = line_copy(total, slots, group, k, 0, y, x, 1)

            @pl.when(jnp.logical_not(starts_line))
            def _():
                line_receive(total, slots, group, k, slot, y, x)

            copy.start()

    def line_end(total, slots, group, slot_below, slot_above, add):
        @pl.when(z > 0)
        def _():
            here = slots.at[slot_below]
            peer = index(z - 1, y, x)
            remote(here, here, sent[group].at[0], came[group].at[slot_below], dp=peer).wait_recv()
            add(here)

        @pl.when(z < depth - 1)
        def _():
            here = slots.at[slot_above]
            peer = index(z + 1, y, x)
            remote(here, here, sent[group].at[0], came[group].at[slot_above], dp=peer).wait_recv()
            add(here)

    def finish(which):
        total, slots, group = (sum_a, in_a3, 2) if which == 0 else (sum_b, in_b3, 5)
        own = chunk(total, z, y, x)
        if which == 0:
            hidden = out_fc1.shape[1]
            out_fc1[...] = total[own, :hidden].astype(F32)
            out_proj[...] = total[own, hidden:].astype(F32)

            def add(here):
                out_fc1[...] += here[:, :hidden].astype(F32)
                out_proj[...] += here[:, hidden:].astype(F32)
        else:
            out_fc2[...] = total[own, :].astype(F32)

            def add(here):
                out_fc2[...] += here[...].astype(F32)

        line_end(total, slots, group, z + 1, z, add)

    operands(2, 6, 1, 5)
    product(held[2], held[6], sum_a, 0)
    product(held[1], held[5], sum_a, held[6].shape[1])
    for i in range(2 * depth):
        first_copy(0, i).start()
    operands(3, 7)
    product(held[3], held[7], sum_b, 0)
    for i in range(2 * depth):
        first_copy(1, i).start()

    for i in range(depth):
        first_receive(1, i)
        first_receive(0, i)
        if i < 4:
            line_c(0, i)
    for c in range(depth, 4):
        line_c(0, c)
    for i in range(depth):
        first_receive(1, depth + i)
        first_receive(0, depth + i)
        if i < 4 and depth > 2:
            line_c(1, i)
    for k in range(2, depth - 1):
        for c in range(4):
            line_c(k, c)

    def end_c(c):
        yy, xx = c_parts[c]
        line_end(
            sum_c, in_c1, 6, (z + 1) * 4 + c, z * 4 + c,
            lambda here: accumulate(sum_c, z, yy, xx, here),
        )

    def copy_c2(c):
        yy, xx = c_parts[c]
        source = sum_c.at[chunk(sum_c, z, yy, xx), :]
        return remote(source, in_c2.at[c], sent[7].at[c], came[7].at[c], dp=across_x)

    def copy_c3():
        source = sum_c.at[chunk(sum_c, z, 1 - y, x), :]
        return remote(source, in_c3, sent[8].at[0], came[8].at[0], dp=across_y)

    line(1, 0)
    line(0, 0)
    for c in range(2):
        end_c(c)
        copy_c2(c).start()
    end_c(2)
    end_c(3)
    for k in range(1, depth - 1):
        line(1, k)
        line(0, k)
        if k == 1:
            copy_c2(0).wait_recv()
            accumulate(sum_c, z, 1 - y, x, in_c2.at[0])
            copy_c3().start()
            copy_c2(1).wait_recv()
            accumulate(sum_c, z, y, x, in_c2.at[1])
    line(1, depth - 1)
    line(0, depth - 1)
    copy_c3().wait_recv()
    out_qkv[...] = sum_c[chunk(sum_c, z, y, x), :].astype(F32) + in_c3[...].astype(F32)
    finish(1)
    finish(0)

    for i in order:
        theirs = held[i].at[pl.ds(ROWS, ROWS), :]
        remote(first[i], theirs, swap_sent.at[i], swap_came.at[i], pipe=1 - section).wait_send()
    for which in range(2):
        for i in range(2 * depth):
            first_copy(which, i).wait_send()
        for i in range(depth):
            second_copy(which, i).wait_send()
        for k in range(depth - 1):
            total, slots = (sum_a, in_a3) if which == 0 else (sum_b, in_b3)
            line_copy(total, slots, 2 if which == 0 else 5, k, 0, y, x, 1)[1].wait_send()
    for k in range(depth - 1):
        for c, (yy, xx) in enumerate(c_parts):
            line_copy(sum_c, in_c1, 6, k, c, yy, xx, 4)[1].wait_send()
    copy_c2(0).wait_send()
    copy_c2(1).wait_send()
    copy_c3().wait_send()


def scattered(count, first, second):
    widths = [a.shape[1] for a in first]
    n1, merged, n2, act, gmixed, gbranch, ghidden, gb2 = widths
    depth = count // (SIDE * SIDE)
    inside = pl.BlockSpec(memory_space=pltpu.VMEM)
    outside = pl.BlockSpec(memory_space=pl.ANY)
    rows, rows_b = n1 // count, act // count
    cols_a = ghidden + gbranch
    dma = pltpu.SemaphoreType.DMA
    copies = (2 * depth, depth, depth - 1, 2 * depth, depth, depth - 1, 4 * (depth - 1), 2, 1)
    arrivals = (2 * depth, depth, depth + 1, 2 * depth, depth, depth + 1, 4 * (depth + 1), 2, 1)
    return pl.pallas_call(
        functools.partial(scatter_kernel, count),
        out_shape=(
            shape(rows, gmixed, dtype=F32), shape(rows, gbranch, dtype=F32),
            shape(rows, ghidden, dtype=F32), shape(rows_b, gb2, dtype=F32),
        ),
        in_specs=[outside] * 16,
        out_specs=(inside,) * 4,
        scratch_shapes=[pltpu.VMEM((2 * ROWS, w), BF16) for w in widths]
        + [pltpu.VMEM((n1, cols_a), BF16), pltpu.VMEM((act, gb2), BF16), pltpu.VMEM((n1, gmixed), BF16)]
        + [pltpu.VMEM((slots, rows, cols_a), BF16) for slots in (2 * depth, depth, depth + 1)]
        + [pltpu.VMEM((slots, rows_b, gb2), BF16) for slots in (2 * depth, depth, depth + 1)]
        + [pltpu.VMEM((4 * (depth + 1), rows, gmixed), BF16), pltpu.VMEM((2, rows, gmixed), BF16),
           pltpu.VMEM((rows, gmixed), BF16)]
        + [dma((8,)), dma((8,)), dma((8,))]
        + [dma((c,)) for c in copies] + [dma((a,)) for a in arrivals],
        compiler_params=pltpu.CompilerParams(
            vmem_limit_bytes=60 * 2**20, collective_id=1, has_side_effects=True
        ),
        name="gradient_scatter",
    )(*first, *second)


def swapped(value):
    return lax.ppermute(value, "pipe", [(0, 1), (1, 0)])


def body(
    x_global, x_local, cot_global, cot_local, global_count, local_count,
    w_qkv, w_proj, w_fc1, w_fc2,
    norm1_gain, norm1_shift, q_bias, v_bias, proj_bias, scale_attn,
    norm2_gain, norm2_shift, fc1_bias, fc2_bias, scale_mlp,
    table_global, table_local,
):
    section = lax.axis_index("pipe")
    width = x_global.shape[2]
    heads = table_global.shape[2]
    tokens_g, tokens_l = x_global.shape[1], x_local.shape[1]
    own = (w_qkv[0], w_proj[0], w_fc1[0], w_fc2[0])
    other = tuple(swapped(w) for w in own)
    vec = jnp.concatenate(
        [norm1_gain, norm1_shift, q_bias, v_bias, proj_bias, scale_attn, norm2_gain, norm2_shift,
         fc2_bias, scale_mlp, fc1_bias.reshape(-1, width)], 0)
    sg = spread(table_global[0], INDEX_G)
    sl = spread(table_local[0], INDEX_L)
    smalls_own = (vec, sg, sl)
    smalls_other = tuple(swapped(s) for s in smalls_own)

    def by_layer(mine, theirs):
        first = jnp.where(section == 0, mine, theirs)
        second = jnp.where(section == 0, theirs, mine)
        return first, second

    (vec0, vec1), (sg0, sg1), (sl0, sl1) = (by_layer(a, b) for a, b in zip(smalls_own, smalls_other))
    vec0, vec1 = vec0.astype(F32), vec1.astype(F32)

    def packed(array_g, array_l):
        crop_g = lax.dynamic_index_in_dim(array_g, section, 0, keepdims=False)
        crop_l = lax.dynamic_index_in_dim(array_l, section, 0, keepdims=False)
        crop_g = jnp.pad(crop_g, ((0, LOCAL_ROW - tokens_g), (0, 0)))
        crop_l = jnp.pad(crop_l, ((0, ROWS - LOCAL_ROW - tokens_l), (0, 0)))
        return jnp.concatenate([crop_g, crop_l], 0)

    x = packed(x_global, x_local)
    live_g = (global_count[0] > section).astype(BF16)
    live_l = (local_count[0] > section).astype(BF16)
    cot = packed(cot_global * live_g, cot_local * live_l)

    kept0 = forward(0, x, vec0, sg0, sl0, own, other)
    first = kept0[0]
    kept1 = forward(1, first, vec1, sg1, sl1, own, other)
    second = kept1[0]
    back1 = backward(1, first, cot, vec1, kept1, heads, own, other)
    grad_first = back1[0]
    back0 = backward(0, x, grad_first, vec0, kept0, heads, own, other)
    grad_x = back0[0]

    def exchange(layer0, layer1):
        keep = jnp.where(section == 0, layer0, layer1)
        send = jnp.where(section == 0, layer1, layer0)
        return keep, swapped(send)

    def both_crops(keep, came):
        low = jnp.where(section == 0, keep, came)
        high = jnp.where(section == 0, came, keep)
        return (
            jnp.stack([low[:tokens_g], high[:tokens_g]]),
            jnp.stack([low[LOCAL_ROW:LOCAL_ROW + tokens_l], high[LOCAL_ROW:LOCAL_ROW + tokens_l]]),
        )

    out_g, out_l = both_crops(*exchange(first, second))
    crop = jnp.arange(2, dtype=jnp.int32)[:, None, None]
    out_g = jnp.where(crop < global_count[0], out_g, jnp.zeros_like(out_g))
    out_l = jnp.where(crop < local_count[0], out_l, jnp.zeros_like(out_l))
    gin_g, gin_l = both_crops(*exchange(grad_x, grad_first))

    count = lax.axis_size("dp")
    first_operands = [kept0[i] for i in (1, 6, 9, 10)] + [back0[i] for i in (1, 2, 3, 4)]
    second_operands = [kept1[i] for i in (1, 6, 9, 10)] + [back1[i] for i in (1, 2, 3, 4)]
    if count % (2 * SIDE * SIDE) == 0 and width % (16 * count) == 0:
        shares = scattered(count, first_operands, second_operands)
    else:
        whole = [jnp.concatenate(exchange(a, b), 0) for a, b in zip(first_operands, second_operands)]
        shares = [
            lax.psum_scatter(
                dot_rows(a, b).astype(BF16), "dp", scatter_dimension=0, tiled=True
            ).astype(F32)
            for a, b in zip(whole[:4], whole[4:])
        ]
    keep, came = [], []
    for i in (5, 6, 7):
        a, b = exchange(back0[i], back1[i])
        keep.append(a)
        came.append(b)
    small, tg, tl = (a + b for a, b in zip(keep, came))
    tg = gather_back(tg, INDEX_G, table_global.shape[1])
    tl = gather_back(tl, INDEX_L, table_local.shape[1])
    small, tg, tl = lax.psum((small, tg, tl), "dp")
    hidden = fc1_bias.shape[1]
    return (
        out_g[None], out_l[None], gin_g[None], gin_l[None],
        *(s[None] for s in shares),
        small[N1G:N1G + 1], small[N1S:N1S + 1], small[QB:QB + 1], small[VB:VB + 1],
        small[PB:PB + 1], small[SA:SA + 1], small[N2G:N2G + 1], small[N2S:N2S + 1],
        small[F1B:F1B + hidden // width].reshape(1, hidden),
        small[F2B:F2B + 1], small[SM:SM + 1],
        tg[None], tl[None],
    )


def solution(mesh):
    three, two = P("pipe", None, None), P("pipe", None)
    rows = P("dp", None, None)
    in_specs = (rows,) * 4 + (P("dp"),) * 2 + (three,) * 4 + (two,) * 11 + (three,) * 2
    crops = P("pipe", "dp", None, None)
    out_specs = (crops,) * 4 + (P("pipe", "dp", None),) * 4 + (two,) * 11 + (three,) * 2
    return jax.shard_map(body, mesh=mesh, in_specs=in_specs, out_specs=out_specs, check_vma=False)
```

```python
import functools
import jax
import jax.numpy as jnp
import numpy as np
from jax import lax
from jax.experimental import pallas as pl
from jax.experimental.pallas import tpu as pltpu
from jax.sharding import PartitionSpec as P

GRID_G = 14
GRID_L = 6
ROWS = 256
LOCAL_ROW = 208
LANES_G = 512
LANES_L = 128
FRONT_L = 51
BLOCK = 256
NEG = -1e30
eps = 1e-06
F32 = jnp.float32
BF16 = jnp.bfloat16
INV_SQRT2 = 0.7071067811865476
INV_SQRT_2PI = 0.3989422804014327
N1G, N1S, QB, VB, PB, SA, N2G, N2S, F2B, SM, F1B = range(11)


def spread_index(grid, rows, lanes, front, cls_lane):
    side = 2 * grid - 1
    entries = side * side
    index = np.full((rows, lanes), -1, np.int32)
    for q in range(grid):
        for a in range(side):
            for k in range(grid):
                index[q, front + a * grid + k] = (side - 1 - a) * side + (q - k + grid - 1)
    index[rows - 2, :] = entries
    index[rows - 2, cls_lane] = entries + 2
    index[rows - 1, :] = entries + 1
    return index


INDEX_G = spread_index(GRID_G, 16, LANES_G, 1, 0)
INDEX_L = spread_index(GRID_L, 8, LANES_L, FRONT_L, LOCAL_ROW - 128)


def dot(a, b):
    return lax.dot_general(a, b, (((1,), (0,)), ((), ())), preferred_element_type=F32)


def dot_cols(a, b):
    return lax.dot_general(a, b, (((1,), (1,)), ((), ())), preferred_element_type=F32)


def dot_rows(a, b):
    return lax.dot_general(a, b, (((0,), (0,)), ((), ())), preferred_element_type=F32)


def normalised(x):
    centered = x - jnp.mean(x, axis=-1, keepdims=True)
    rstd = lax.rsqrt(jnp.mean(centered * centered, axis=-1, keepdims=True) + eps)
    return centered * rstd, rstd


def row_steps(step, body):
    def one(i, carry):
        body(pl.ds(pl.multiple_of(i * step, step), step))
        return carry

    lax.fori_loop(0, ROWS // step, one, 0)


def build_bias(spread_g, spread_l, bias):
    for r in range(GRID_G):
        shifted = pltpu.roll(spread_g, (LANES_G - (GRID_G - 1 - r) * GRID_G) % LANES_G, 1)
        bias[pl.ds(1 + GRID_G * r, GRID_G), :] = shifted[:GRID_G, :ROWS]
    for r in range(GRID_L):
        shifted = pltpu.roll(spread_l, GRID_L * r, 1)
        bias[pl.ds(LOCAL_ROW + 1 + GRID_L * r, GRID_L), pl.ds(128, 128)] = shifted[:GRID_L, :]
    tokens_g = GRID_G * GRID_G + 1
    tokens_l = GRID_L * GRID_L + 1
    top = bias[:LOCAL_ROW, :]
    row = lax.broadcasted_iota(jnp.int32, top.shape, 0)
    col = lax.broadcasted_iota(jnp.int32, top.shape, 1)
    top = jnp.where(col == 0, spread_g[15:16, :ROWS], top)
    top = jnp.where(row == 0, spread_g[14:15, :ROWS], top)
    top = jnp.where(row >= tokens_g, 0.0, top)
    top = jnp.where(col >= tokens_g, NEG, top)
    low = bias[LOCAL_ROW:, 128:]
    row = lax.broadcasted_iota(jnp.int32, low.shape, 0)
    col = lax.broadcasted_iota(jnp.int32, low.shape, 1) - (LOCAL_ROW - 128)
    low = jnp.where(col == 0, spread_l[7:8], low)
    low = jnp.where(row == 0, spread_l[6:7], low)
    low = jnp.where(row >= tokens_l, 0.0, low)
    low = jnp.where((col >= 0) & (col < tokens_l), low, NEG)
    bottom = jnp.concatenate([jnp.full((ROWS - LOCAL_ROW, 128), NEG, F32), low], 1)
    return jnp.concatenate([top, bottom], 0)


MESH = pl.DeviceIdType.MESH
SIDE = 2
TABLE_ROW, TABLE_ROW_L, SMALL_ROWS = 16, 32, 48


def remote(source, target, sent, came, **device):
    return pltpu.make_async_remote_copy(
        src_ref=source, dst_ref=target, send_sem=sent, recv_sem=came,
        device_id=device, device_id_type=MESH,
    )


def hot(index_row, count):
    number = lax.broadcasted_iota(jnp.int32, (count, index_row.shape[1]), 0)
    return jnp.where(number == index_row, 1.0, 0.0).astype(BF16)


def place_crops(target, global_ref, local_ref, section, live_g=None, live_l=None):
    target[...] = jnp.zeros_like(target)
    for ref, start, live in ((global_ref, 0, live_g), (local_ref, LOCAL_ROW, live_l)):
        rows = jnp.where(section == 0, ref[:, 0, :].astype(F32), ref[:, 1, :].astype(F32))
        if live is not None:
            rows = rows * live
        target[start:start + ref.shape[0], :] = rows.astype(BF16)


def forward_kernel(
    scale,
    xg_ref, xl_ref, vec_refs, tg_ref, tl_ref, index_g, index_l, own_qkv, own_proj, own_fc1, own_fc2,
    oth_qkv, oth_proj, oth_fc1, oth_fc2,
    out_all, n1_all, q_all, k_all, v_all, p_all, merged_all, branch_all, middle_all,
    n2_all, act_all, dact_all, branch2_all, small_out,
    w_qkv, w_proj, w_fc1, w_fc2, small_in, small, vec_all, x_in, out_ref, n1_ref, q_ref, k_ref, v_ref, p_ref,
    merged_ref, branch_ref, middle_ref, n2_ref, act_ref, dact_ref, branch2_ref,
    spread_g, spread_l, bias, own_sem, sent, came, keep_sem, store_sem, small_sem,
):
    section = lax.axis_index("pipe")
    partner = 1 - section
    own = (own_qkv, own_proj, own_fc1, own_fc2)
    oth = (oth_qkv, oth_proj, oth_fc1, oth_fc2)
    held = (w_qkv, w_proj, w_fc1, w_fc2)
    width = x_in.shape[1]
    heads = p_ref.shape[0]
    half = SMALL_ROWS

    barrier = pltpu.get_barrier_semaphore()
    pl.semaphore_signal(barrier, inc=1, device_id={"pipe": partner}, device_id_type=MESH)
    for i in range(4):
        pltpu.make_async_copy(own[i], held[i].at[section], own_sem.at[i]).start()
    small_rows = small.at[pl.ds(pl.multiple_of(section * half, half), half), :]
    small_in[...] = jnp.zeros_like(small_in)
    row = 0
    for ref in vec_refs:
        for b in range(0, ref.shape[1], width):
            small_in[row:row + 1, :] = ref[:, b:b + width].astype(F32)
            row += 1
    small_in[TABLE_ROW:TABLE_ROW + heads, 0:tg_ref.shape[1]] = tg_ref[...].astype(F32)
    small_in[TABLE_ROW_L:TABLE_ROW_L + heads, 0:tl_ref.shape[1]] = tl_ref[...].astype(F32)
    pl.semaphore_wait(barrier, 1)
    small_copy = remote(small_in, small_rows, small_sem.at[0], small_sem.at[1], pipe=partner)
    small_copy.start()

    def weight_copy(i):
        return remote(own[i], held[i].at[section], sent.at[i], came.at[i], pipe=partner)

    for i in range(4):
        weight_copy(i).start()
    small_rows[...] = small_in[...]
    place_crops(x_in, xg_ref, xl_ref, section)
    small_copy.wait_recv()
    vec_all[...] = small[...]
    small_out[...] = vec_all[...]
    tables_g = jnp.concatenate(
        [small[TABLE_ROW:TABLE_ROW + 16, :], small[half + TABLE_ROW:half + TABLE_ROW + 16, :]], 0
    ).astype(BF16)
    tables_l = jnp.concatenate(
        [small[TABLE_ROW_L:TABLE_ROW_L + 16, :128], small[half + TABLE_ROW_L:half + TABLE_ROW_L + 16, :128]], 0
    ).astype(BF16)
    for r in range(16):
        found = dot(tables_g, hot(index_g[r:r + 1, :], width))
        spread_g[0, :, r, :] = found[:16]
        spread_g[1, :, r, :] = found[16:]
    for r in range(8):
        found = dot(tables_l, hot(index_l[r:r + 1, :], 128))
        spread_l[0, :, r, :] = found[:16]
        spread_l[1, :, r, :] = found[16:]

    stores = (
        (out_ref, out_all), (n1_ref, n1_all), (q_ref, q_all), (k_ref, k_all), (v_ref, v_all),
        (p_ref, p_all), (merged_ref, merged_all), (branch_ref, branch_all), (middle_ref, middle_all),
        (n2_ref, n2_all), (act_ref, act_all), (dact_ref, dact_all), (branch2_ref, branch2_all),
    )
    OUT, N1, Q, K, V, PR, ME, BR, MI, N2, AC, DA, B2 = range(13)

    def store_copy(number, layer):
        source, target = stores[number]
        if number == OUT:
            source = source.at[layer]
        return pltpu.make_async_copy(source, target.at[layer], store_sem.at[number])

    def store(layer, *numbers):
        for number in numbers:
            store_copy(number, layer).start()

    def stored(layer, *numbers):
        for number in numbers:
            store_copy(number, layer).wait()

    def weight(i, layer):
        @pl.when(section == layer)
        def _():
            pltpu.make_async_copy(own[i], held[i].at[section], own_sem.at[i]).wait()

        @pl.when(section != layer)
        def _():
            here = held[i].at[partner]
            remote(here, here, sent.at[i], came.at[i], pipe=partner).wait_recv()
            pltpu.make_async_copy(here, oth[i], keep_sem.at[i]).start()

    lane = lax.broadcasted_iota(jnp.int32, (1, 128), 1)
    for layer in range(2):
        entering = x_in if layer == 0 else out_ref.at[0]
        base = layer * half

        def vec(row):
            return vec_all[base + row:base + row + 1, :]

        def norm1(rows):
            xhat, _ = normalised(entering[rows, :].astype(F32))
            n1_ref[rows, :] = (xhat * vec(N1G) + vec(N1S)).astype(BF16)

        row_steps(32, norm1)
        store(layer, N1)
        weight(0, layer)
        n1 = n1_ref[...]
        for b in range(0, width, BLOCK):
            cols = slice(b, b + BLOCK)
            mixed = dot(n1, w_qkv[layer, :, b:b + BLOCK]) + vec(QB)[:, cols]
            q_ref[:, cols] = (mixed * scale).astype(BF16)
            k_ref[:, cols] = dot(n1, w_qkv[layer, :, width + b:width + b + BLOCK]).astype(BF16)
            mixed = dot(n1, w_qkv[layer, :, 2 * width + b:2 * width + b + BLOCK]) + vec(VB)[:, cols]
            v_ref[:, cols] = mixed.astype(BF16)
        store(layer, Q, K, V)
        for pair in range(heads // 2):
            cols = slice(pair * 128, pair * 128 + 128)
            q, k, v = q_ref[:, cols], k_ref[:, cols], v_ref[:, cols]
            result = None
            for part in range(2):
                head = 2 * pair + part
                mine = (lane < 64) if part == 0 else (lane >= 64)
                scores = dot_cols(q, jnp.where(mine, k, jnp.zeros_like(k))) + build_bias(
                    spread_g[layer, head], spread_l[layer, head], bias.at[head % 2]
                )
                expo = jnp.exp(scores - jnp.max(scores, axis=-1, keepdims=True))
                probs = expo * (1.0 / jnp.sum(expo, axis=-1, keepdims=True))
                p_ref[head] = probs
                piece = dot(probs.astype(BF16), jnp.where(mine, v, jnp.zeros_like(v)))
                result = piece if result is None else result + piece
            merged_ref[:, cols] = result.astype(BF16)
        store(layer, PR, ME)
        weight(1, layer)
        merged = merged_ref[...]
        for b in range(0, width, BLOCK):
            cols = slice(b, b + BLOCK)
            branch = dot(merged, w_proj[layer, :, cols]) + vec(PB)[:, cols]
            branch_ref[:, cols] = branch
            middle_ref[:, cols] = entering[:, cols].astype(F32) + vec(SA)[:, cols] * branch
        store(layer, BR, MI)

        def norm2(rows):
            xhat, _ = normalised(middle_ref[rows, :])
            n2_ref[rows, :] = (xhat * vec(N2G) + vec(N2S)).astype(BF16)

        row_steps(32, norm2)
        store(layer, N2)
        weight(2, layer)
        if layer == 1:
            stored(0, AC, DA, B2)
        n2 = n2_ref[...]
        for b in range(0, w_fc1.shape[2], BLOCK):
            cols = slice(b, b + BLOCK)
            part = b // width
            hidden = dot(n2, w_fc1[layer, :, cols]) + vec(F1B + part)[:, b - part * width:b - part * width + BLOCK]
            cdf = 0.5 + 0.5 * lax.erf(hidden * INV_SQRT2)
            act_ref[:, cols] = (hidden * cdf).astype(BF16)
            dact_ref[:, cols] = cdf + hidden * (INV_SQRT_2PI * jnp.exp(-0.5 * hidden * hidden))
        store(layer, AC, DA)
        weight(3, layer)
        for b in range(0, width, BLOCK):
            cols = slice(b, b + BLOCK)
            branch2 = dot(act_ref[...], w_fc2[layer, :, cols]) + vec(F2B)[:, cols]
            branch2_ref[:, cols] = branch2
            out_ref[layer, :, cols] = (middle_ref[:, cols] + vec(SM)[:, cols] * branch2).astype(BF16)
        store(layer, B2, OUT)
        if layer == 0:
            stored(0, N1, Q, K, V, PR, ME, BR, MI, N2, OUT)
    stored(1, *range(13))
    for i in range(4):
        weight_copy(i).wait_send()
        pltpu.make_async_copy(held[i].at[partner], oth[i], keep_sem.at[i]).wait()
    small_copy.wait_send()


def backward_kernel(
    layer, scale, *refs,
):
    if layer == 1:
        cg_ref, cl_ref, gcount, lcount = refs[:4]
        refs = refs[4:]
    else:
        gin_ref, refs = refs[0], refs[1:]
    vec_all, x_all, q_all, k_all, v_all, p_all, branch_all, middle_all, dact_all, branch2_all = refs[:10]
    own, oth = refs[10:14], refs[14:18]
    gx_ref, gmixed_out, gbranch_out, ghidden_out, gb2_out, small_ref, tg_ref, tl_ref = refs[18:26]
    (
        g_ref, x_ref, q_ref, k_ref, v_ref, p_ref, branch_ref, middle_ref, dact_ref, branch2_ref,
        w_qkv, w_proj, w_fc1, w_fc2, gmixed_ref, gbranch_ref, ghidden_ref, gb2_ref,
        gmid, gnorm, gmerged, gs_ref, load_sem, weight_sem, store_sem,
    ) = refs[26:]
    section = lax.axis_index("pipe")
    held = (w_qkv, w_proj, w_fc1, w_fc2)
    loads = (
        (x_all, x_ref), (q_all, q_ref), (k_all, k_ref), (v_all, v_ref), (p_all, p_ref),
        (branch_all, branch_ref), (middle_all, middle_ref), (dact_all, dact_ref), (branch2_all, branch2_ref),
    )
    X, Q, K, V, PR, BR, MI, DA, B2 = range(9)

    def load_copy(number):
        source, target = loads[number]
        if layer == 1 or number != X:
            source = source.at[0 if number == X else layer]
        return pltpu.make_async_copy(source, target, load_sem.at[number])

    def load_weight(i):
        @pl.when(section == layer)
        def _():
            pltpu.make_async_copy(own[i], held[i], weight_sem.at[i]).start()

        @pl.when(section != layer)
        def _():
            pltpu.make_async_copy(oth[i], held[i], weight_sem.at[i]).start()

    def weight(i):
        pltpu.make_async_copy(own[i], held[i], weight_sem.at[i]).wait()

    def loaded(*numbers):
        for number in numbers:
            load_copy(number).wait()

    load_copy(B2).start()
    load_weight(3)
    load_copy(DA).start()
    load_weight(2)
    for number in (MI, BR):
        load_copy(number).start()
    load_weight(1)
    for number in (V, PR, K, Q):
        load_copy(number).start()
    load_weight(0)
    if layer == 1:
        load_copy(X).start()

    width = g_ref.shape[1]
    heads = p_ref.shape[0]
    small_ref[...] = jnp.zeros_like(small_ref)

    def vec(row):
        return vec_all[layer * SMALL_ROWS + row:layer * SMALL_ROWS + row + 1, :]

    def add_small(row, values):
        small_ref[row:row + 1, :] += jnp.sum(values, axis=0, keepdims=True)

    if layer == 1:
        live_g = jnp.where(gcount[0] > section, 1.0, 0.0)
        live_l = jnp.where(lcount[0] > section, 1.0, 0.0)
        place_crops(g_ref, cg_ref, cl_ref, section, live_g, live_l)
    else:
        g_ref = gin_ref
        place_crops(x_ref, *x_all, section)

    stores = (
        (gmixed_ref, gmixed_out), (gbranch_ref, gbranch_out), (ghidden_ref, ghidden_out), (gb2_ref, gb2_out),
    )

    def store_copy(number):
        return pltpu.make_async_copy(*stores[number], store_sem.at[number])

    loaded(B2)

    def scaled(rows):
        grad = g_ref[rows, :].astype(F32)
        low = (vec(SM) * grad).astype(BF16)
        gb2_ref[rows, :] = low
        add_small(SM, grad * branch2_ref[rows, :])
        add_small(F2B, low.astype(F32))

    row_steps(32, scaled)
    store_copy(3).start()
    weight(3)
    loaded(DA)
    gb2 = gb2_ref[...]
    for b in range(0, w_fc1.shape[1], BLOCK):
        cols = slice(b, b + BLOCK)
        part = b // width
        ghidden = (dot_cols(gb2, w_fc2[cols, :]) * dact_ref[:, cols]).astype(BF16)
        ghidden_ref[:, cols] = ghidden
        small_ref[F1B + part:F1B + part + 1, b - part * width:b - part * width + BLOCK] = jnp.sum(
            ghidden.astype(F32), axis=0, keepdims=True
        )
    store_copy(2).start()
    weight(2)
    for b in range(0, width, BLOCK):
        gnorm[:, b:b + BLOCK] = dot_cols(ghidden_ref[...], w_fc1[b:b + BLOCK, :])

    def norm_back(values, grad, gain):
        xhat, rstd = normalised(values)
        scaled_grad = grad * gain
        mean1 = jnp.mean(scaled_grad, axis=-1, keepdims=True)
        mean2 = jnp.mean(scaled_grad * xhat, axis=-1, keepdims=True)
        return xhat, rstd * (scaled_grad - mean1 - xhat * mean2)

    loaded(MI, BR)

    def norm2(rows):
        grad = gnorm[rows, :]
        xhat, through = norm_back(middle_ref[rows, :], grad, vec(N2G))
        grad_middle = g_ref[rows, :].astype(F32) + through
        gmid[rows, :] = grad_middle
        add_small(N2G, grad * xhat)
        add_small(N2S, grad)
        add_small(SA, grad_middle * branch_ref[rows, :])
        low = (vec(SA) * grad_middle).astype(BF16)
        gbranch_ref[rows, :] = low
        add_small(PB, low.astype(F32))

    row_steps(32, norm2)
    store_copy(1).start()
    weight(1)
    for b in range(0, width, BLOCK):
        gmerged[:, b:b + BLOCK] = dot_cols(gbranch_ref[...], w_proj[b:b + BLOCK, :]).astype(BF16)
    lane = lax.broadcasted_iota(jnp.int32, (1, 128), 1)
    loaded(V, PR, K, Q)
    lane_all = lax.broadcasted_iota(jnp.int32, (1, ROWS), 1)
    for pair in range(heads // 2):
        cols = slice(pair * 128, pair * 128 + 128)
        q, k, v, gm = q_ref[:, cols], k_ref[:, cols], v_ref[:, cols], gmerged[:, cols]
        gq = gk = gv = 0.0
        for half in range(2):
            head = 2 * pair + half
            mine = (lane < 64) if half == 0 else (lane >= 64)

            def only(values):
                return jnp.where(mine, values, jnp.zeros_like(values))

            probs = p_ref[head]
            grad_probs = dot_cols(gm, only(v))
            total = jnp.sum(probs * grad_probs, axis=-1, keepdims=True)
            gscores = (probs * (grad_probs - total)).astype(BF16)
            gv += dot_rows(probs.astype(BF16), only(gm))
            gq += dot(gscores, only(k))
            gk += dot_rows(gscores, only(q))
            wide = gscores.astype(F32)
            gs = gs_ref.at[head % 2]
            gs[...] = jnp.where((lane_all == 0) | (lane_all == LOCAL_ROW), 0.0, wide)
            acc = jnp.zeros((GRID_G, LANES_G), F32)
            for r in range(GRID_G):
                block = gs[pl.ds(1 + GRID_G * r, GRID_G), :]
                block = jnp.concatenate([block, jnp.zeros_like(block)], 1)
                acc += pltpu.roll(block, (GRID_G - 1 - r) * GRID_G, 1)
            first_row = wide[0:1, :]
            to_class = jnp.sum(wide[:LOCAL_ROW, :], axis=0, keepdims=True) - first_row
            to_class = jnp.where(lane_all == 0, to_class, 0.0)
            blank = jnp.zeros((1, LANES_G - ROWS), F32)
            tg_ref[0:GRID_G, head, :] = acc
            tg_ref[14, head:head + 1, :] = jnp.concatenate([first_row, blank], 1)
            tg_ref[15, head:head + 1, :] = jnp.concatenate([to_class, blank], 1)
            acc = jnp.zeros((GRID_L, LANES_L), F32)
            for r in range(GRID_L):
                block = gs[pl.ds(LOCAL_ROW + 1 + GRID_L * r, GRID_L), pl.ds(128, 128)]
                acc += pltpu.roll(block, (LANES_L - GRID_L * r) % LANES_L, 1)
            first_row = wide[LOCAL_ROW:LOCAL_ROW + 1, 128:]
            to_class = jnp.sum(wide[LOCAL_ROW:, 128:], axis=0, keepdims=True) - first_row
            to_class = jnp.where(lane == LOCAL_ROW - 128, to_class, 0.0)
            tl_ref[0:GRID_L, head, :] = acc
            tl_ref[6, head:head + 1, :] = first_row
            tl_ref[7, head:head + 1, :] = to_class
        gmixed_ref[:, cols] = gq.astype(BF16) * jnp.asarray(scale, BF16)
        gmixed_ref[:, slice(width + cols.start, width + cols.stop)] = gk.astype(BF16)
        gmixed_ref[:, slice(2 * width + cols.start, 2 * width + cols.stop)] = gv.astype(BF16)

    def biases(rows):
        add_small(QB, gmixed_ref[rows, :width].astype(F32))
        add_small(VB, gmixed_ref[rows, 2 * width:].astype(F32))

    store_copy(0).start()
    row_steps(32, biases)
    weight(0)
    if layer == 1:
        loaded(X)
    for b in range(0, width, BLOCK):
        gnorm[:, b:b + BLOCK] = dot_cols(gmixed_ref[...], w_qkv[b:b + BLOCK, :])

    def norm1(rows):
        grad = gnorm[rows, :]
        xhat, through = norm_back(x_ref[rows, :].astype(F32), grad, vec(N1G))
        add_small(N1G, grad * xhat)
        add_small(N1S, grad)
        gx_ref[rows, :] = (gmid[rows, :] + through).astype(BF16)

    row_steps(32, norm1)
    for number in range(4):
        store_copy(number).wait()


def shape(*dims, dtype=BF16):
    return jax.ShapeDtypeStruct(dims, dtype)


INSIDE = pl.BlockSpec(memory_space=pltpu.VMEM)
OUTSIDE = pl.BlockSpec(memory_space=pl.ANY)
SCALARS = pl.BlockSpec(memory_space=pltpu.SMEM)
DMA = pltpu.SemaphoreType.DMA


def forward(x_global, x_local, vec, tables, own):
    width = x_global.shape[2]
    heads = tables[0].shape[0]
    hidden = own[2].shape[1]
    scale = (width // heads) ** (-0.5)
    kept = (
        ((ROWS, width), BF16), ((ROWS, width), BF16), ((ROWS, width), BF16), ((ROWS, width), BF16),
        ((ROWS, width), BF16), ((heads, ROWS, ROWS), F32), ((ROWS, width), BF16),
        ((ROWS, width), F32), ((ROWS, width), F32), ((ROWS, width), BF16),
        ((ROWS, hidden), BF16), ((ROWS, hidden), F32), ((ROWS, width), F32),
    )
    scratch = [pltpu.VMEM((2, *w.shape), BF16) for w in own]
    scratch += [pltpu.VMEM((SMALL_ROWS, width), F32)] + [pltpu.VMEM((2 * SMALL_ROWS, width), F32)] * 2
    scratch += [pltpu.VMEM((ROWS, width), BF16), pltpu.VMEM((2, ROWS, width), BF16)]
    scratch += [pltpu.VMEM(dims, kind) for dims, kind in kept[1:]]
    scratch += [
        pltpu.VMEM((2, 16, 16, LANES_G), F32), pltpu.VMEM((2, 16, 8, LANES_L), F32),
        pltpu.VMEM((2, ROWS, ROWS), F32),
        DMA((4,)), DMA((4,)), DMA((4,)), DMA((4,)), DMA((13,)), DMA((2,)),
    ]

    def kernel(xg, xl, *refs):
        count = len(vec)
        forward_kernel(scale, xg, xl, refs[:count], *refs[count:])

    return pl.pallas_call(
        kernel,
        out_shape=tuple(shape(*w.shape) for w in own)
        + tuple(shape(2, *dims, dtype=kind) for dims, kind in kept)
        + (shape(2 * SMALL_ROWS, width, dtype=F32),),
        in_specs=[INSIDE] * (6 + len(vec)) + [OUTSIDE] * 4,
        out_specs=(OUTSIDE,) * 17 + (INSIDE,),
        scratch_shapes=scratch,
        compiler_params=pltpu.CompilerParams(
            vmem_limit_bytes=60 * 2**20, collective_id=2, has_side_effects=True
        ),
        name="forward_layers",
    )(x_global, x_local, *vec, *tables, jnp.asarray(INDEX_G), jnp.asarray(INDEX_L), *own)


def backward(layer, grads, entering, vec, kept, heads, own, other):
    width = vec.shape[1]
    hidden = own[2].shape[1]
    scale = (width // heads) ** (-0.5)
    _, n1, q, k, v, probs, merged, branch, middle, n2, act, dact, branch2 = kept
    if layer == 1:
        inputs = (*grads, vec, entering, q, k, v, probs, branch, middle, dact, branch2, *own, *other)
        specs = [INSIDE] * 2 + [SCALARS] * 2 + [INSIDE] + [OUTSIDE] * 17
        kernel = functools.partial(backward_kernel, 1, scale)
    else:
        inputs = (grads, vec, *entering, q, k, v, probs, branch, middle, dact, branch2, *own, *other)
        specs = [INSIDE] * 4 + [OUTSIDE] * 16

        def kernel(gin, vec_all, xg, xl, *refs):
            backward_kernel(0, scale, gin, vec_all, (xg, xl), *refs)

    return pl.pallas_call(
        kernel,
        out_shape=(
            shape(ROWS, width), shape(ROWS, 3 * width), shape(ROWS, width), shape(ROWS, hidden),
            shape(ROWS, width), shape(16, width, dtype=F32),
            shape(16, heads, LANES_G, dtype=F32), shape(8, heads, LANES_L, dtype=F32),
        ),
        in_specs=specs,
        out_specs=(INSIDE,) + (OUTSIDE,) * 4 + (INSIDE,) * 3,
        scratch_shapes=[pltpu.VMEM((ROWS, width), BF16) for _ in range(5)]
        + [pltpu.VMEM((heads, ROWS, ROWS), F32), pltpu.VMEM((ROWS, width), F32),
           pltpu.VMEM((ROWS, width), F32), pltpu.VMEM((ROWS, hidden), F32), pltpu.VMEM((ROWS, width), F32)]
        + [pltpu.VMEM(w.shape, BF16) for w in own]
        + [pltpu.VMEM((ROWS, c), BF16) for c in (3 * width, width, hidden, width)]
        + [
            pltpu.VMEM((ROWS, width), F32), pltpu.VMEM((ROWS, width), F32),
            pltpu.VMEM((ROWS, width), BF16), pltpu.VMEM((2, ROWS, ROWS), F32),
            DMA((9,)), DMA((4,)), DMA((4,)),
        ],
        compiler_params=pltpu.CompilerParams(vmem_limit_bytes=60 * 2**20),
        name="layer_backward",
    )(*inputs)


def add_rows(total, start, extra, count):
    def one(i, carry):
        rows = pl.ds(pl.multiple_of(start + i * 16, 16), 16)
        here = pl.ds(pl.multiple_of(i * 16, 16), 16)
        total[rows, :] = (total[rows, :].astype(F32) + extra[here, :].astype(F32)).astype(BF16)
        return carry

    lax.fori_loop(0, count // 16, one, 0)


def scatter_kernel(count, *refs):
    kept, back0, back1 = refs[:4], refs[4:8], refs[8:12]
    small0, tg0, tl0, small1, tg1, tl1, index_g, index_l = refs[12:20]
    outs_all, gx0, gx1, gcount, lcount = refs[20:25]
    refs = refs[25:]
    out_qkv, out_proj, out_fc1, out_fc2, out_g, out_l, gin_g, gin_l = refs[:8]
    out_small, out_tg, out_tl = refs[8:19], *refs[19:21]
    refs = refs[21:]
    held = refs[:8]
    sum_a, sum_b, sum_c = refs[8:11]
    in_a1, in_a2, in_a3, in_b1, in_b2, in_b3, in_c1, in_c2, in_c3 = refs[11:20]
    local_sem, swap_sent, swap_came = refs[20:23]
    sent, came = refs[23:32], refs[32:41]
    pair_small, pair_tg, pair_tl, pair_out, pair_gx, sums, slots_z, extra_sent, extra_came = refs[41:]
    first = tuple(r.at[0] for r in kept) + tuple(back0)
    second = tuple(r.at[1] for r in kept) + tuple(back1)
    depth = count // (SIDE * SIDE)
    width = held[0].shape[1]
    section = lax.axis_index("pipe")
    place = lax.axis_index("dp")
    x = place % SIDE
    y = (place // SIDE) % SIDE
    z = place // (SIDE * SIDE)

    def index(zz, yy, xx):
        return (zz * SIDE + yy) * SIDE + xx

    across_x, across_y = index(z, y, 1 - x), index(z, 1 - y, x)

    barrier = pltpu.get_barrier_semaphore()
    pl.semaphore_signal(barrier, inc=1, device_id={"pipe": 1 - section}, device_id_type=MESH)
    for peer in (across_x, across_y):
        pl.semaphore_signal(barrier, inc=1, device_id={"dp": peer}, device_id_type=MESH)
    for step in range(1, depth):
        peer = index((z + step) % depth, y, x)
        pl.semaphore_signal(barrier, inc=1, device_id={"dp": peer}, device_id_type=MESH)
    pl.semaphore_wait(barrier, 3 + depth - 1)

    extras = (
        (small0, small1, pair_small), (tg0, tg1, pair_tg), (tl0, tl1, pair_tl),
        (outs_all.at[0], outs_all.at[1], pair_out), (gx0, gx1, pair_gx),
    )

    def extra_copy(i, layer):
        return remote(
            extras[i][layer], extras[i][2], extra_sent.at[i], extra_came.at[i], pipe=1 - section
        )

    @pl.when(section == 0)
    def _():
        for i in range(3):
            extra_copy(i, 1).start()

    @pl.when(section != 0)
    def _():
        for i in range(3):
            extra_copy(i, 0).start()

    order = (0, 4, 2, 6, 1, 5, 3, 7)
    for i in order:
        mine = held[i].at[pl.ds(0, ROWS), :]
        theirs = held[i].at[pl.ds(ROWS, ROWS), :]

        @pl.when(section == 0)
        def _():
            remote(second[i], theirs, swap_sent.at[i], swap_came.at[i], pipe=1 - section).start()
            pltpu.make_async_copy(first[i], mine, local_sem.at[i]).start()

        @pl.when(section != 0)
        def _():
            remote(first[i], theirs, swap_sent.at[i], swap_came.at[i], pipe=1 - section).start()
            pltpu.make_async_copy(second[i], mine, local_sem.at[i]).start()

    @pl.when(section == 0)
    def _():
        for i in range(3, 5):
            extra_copy(i, 1).start()

    @pl.when(section != 0)
    def _():
        for i in range(3, 5):
            extra_copy(i, 0).start()

    def swapped_outputs():
        extra_copy(3, 0).wait_recv()
        extra_copy(4, 0).wait_recv()

        def live(count_ref, crop):
            return jnp.where(count_ref[0] > crop, 1.0, 0.0)

        def place(crop, values, grads):
            for out, gin, start, count_ref in ((out_g, gin_g, 0, gcount), (out_l, gin_l, LOCAL_ROW, lcount)):
                rows = slice(start, start + out.shape[0])
                out[:, crop, :] = (values[rows].astype(F32) * live(count_ref, crop)).astype(BF16)
                gin[:, crop, :] = grads[rows]

        @pl.when(section == 0)
        def _():
            place(0, outs_all[0], gx0[...])
            place(1, pair_out[...], pair_gx[...])

        @pl.when(section != 0)
        def _():
            place(0, pair_out[...], pair_gx[...])
            place(1, outs_all[1], gx1[...])

    def fold_back(mine, pair, index_ref, entries):
        heads = pair.shape[1]

        def one(r, result):
            total = jnp.where(section == 0, mine[0][r], mine[1][r]) + pair[r]
            high = total.astype(BF16)
            low = (total - high.astype(F32)).astype(BF16)
            spot = hot(index_ref[pl.ds(r, 1), :], entries)
            return result + dot_cols(high, spot) + dot_cols(low, spot)

        return lax.fori_loop(0, index_ref.shape[0], one, jnp.zeros((heads, entries), F32))

    def small_start():
        for i in range(3):
            extra_copy(i, 0).wait_recv()
        sums[0] = jnp.zeros((SMALL_ROWS, width), F32)
        sums[0, 0:16, :] = jnp.where(section == 0, small0[...], small1[...]) + pair_small[...]
        heads = pair_tg.shape[1]
        sums[0, TABLE_ROW:TABLE_ROW + heads, :] = fold_back((tg0, tg1), pair_tg, index_g, width)
        sums[0, TABLE_ROW_L:TABLE_ROW_L + heads, 0:128] = fold_back((tl0, tl1), pair_tl, index_l, 128)
        small_x().start()

    def small_x():
        return remote(sums.at[0], sums.at[3], extra_sent.at[5], extra_came.at[5], dp=across_x)

    def small_y():
        return remote(sums.at[1], sums.at[4], extra_sent.at[6], extra_came.at[6], dp=across_y)

    def small_z(step):
        peer = index((z + step) % depth, y, x)
        return remote(
            sums.at[2], slots_z.at[z], extra_sent.at[6 + step], extra_came.at[6 + step], dp=peer
        )

    def small_second():
        small_x().wait_recv()
        sums[1] = sums[0] + sums[3]
        small_y().start()

    def small_third():
        small_y().wait_recv()
        sums[2] = sums[1] + sums[4]
        for step in range(1, depth):
            small_z(step).start()
        slots_z[z] = sums[2]

    def small_end():
        for step in range(1, depth):
            here = slots_z.at[(z + depth - step) % depth]
            peer = index((z + step) % depth, y, x)
            remote(here, here, extra_sent.at[6 + step], extra_came.at[6 + step], dp=peer).wait_recv()
        total = slots_z[0]
        for zz in range(1, depth):
            total = total + slots_z[zz]
        row = 0
        for ref in out_small:
            for b in range(0, ref.shape[1], width):
                ref[:, b:b + width] = total[row:row + 1]
                row += 1
        for ref, start in ((out_tg, TABLE_ROW), (out_tl, TABLE_ROW_L)):
            ref[:, 0, :] = total[start:start + ref.shape[0], 0:ref.shape[2]]

    def operands(*numbers):
        for i in numbers:
            mine = held[i].at[pl.ds(0, ROWS), :]
            theirs = held[i].at[pl.ds(ROWS, ROWS), :]
            pltpu.make_async_copy(first[i], mine, local_sem.at[i]).wait()
            remote(first[i], theirs, swap_sent.at[i], swap_came.at[i], pipe=1 - section).wait_recv()

    def product(left, right, total, offset):
        def one(i, carry):
            start = pl.multiple_of(i * BLOCK, BLOCK)
            rows = left[:, pl.ds(start, BLOCK)]
            for b in range(0, right.shape[1], width):
                part = dot_rows(rows, right[:, b:b + width])
                total[pl.ds(start, BLOCK), offset + b:offset + b + width] = part.astype(BF16)
            return carry

        lax.fori_loop(0, left.shape[1] // BLOCK, one, 0)

    def target(k):
        low = jnp.where(k < depth - 1 - z, depth - 1 - k, k - (depth - 1 - z))
        high = jnp.where(k < z, k, depth - 1 - (k - z))
        return jnp.where(z < depth // 2, low, high)

    targets = [target(k) for k in range(depth)]
    ups = [jnp.where(targets[k] > z, 1, 0) for k in range(depth - 1)]
    starts_line = (z == 0) | (z == depth - 1)

    def chunk(total, zz, yy, xx):
        rows = total.shape[0] // count
        return pl.ds(pl.multiple_of(index(zz, yy, xx) * rows, rows), rows)

    def accumulate(total, zz, yy, xx, extra):
        rows = total.shape[0] // count
        add_rows(total, pl.multiple_of(index(zz, yy, xx) * rows, rows), extra, rows)

    def line_copy(total, slots, group, k, c, yy, xx, width_of):
        up = ups[k]
        slot = (targets[k] + up) * width_of + c
        number = k * width_of + c
        source = total.at[chunk(total, targets[k], yy, xx), :]
        peer = index(z + 2 * up - 1, y, x)
        return slot, remote(
            source, slots.at[slot], sent[group].at[number], came[group].at[slot], dp=peer
        )

    def line_receive(total, slots, group, k, slot, yy, xx):
        here = slots.at[slot]
        peer = index(z + 1 - 2 * ups[k], y, x)
        remote(here, here, sent[group].at[0], came[group].at[slot], dp=peer).wait_recv()
        accumulate(total, targets[k], yy, xx, here)

    c_parts = ((1 - y, 1 - x), (y, 1 - x), (1 - y, x), (y, x))
    small_start()
    operands(0, 4)
    product(held[0], held[4], sum_c, 0)
    small_second()

    @pl.when(starts_line)
    def _():
        for k in range(depth - 1):
            for c, (yy, xx) in enumerate(c_parts):
                line_copy(sum_c, in_c1, 6, k, c, yy, xx, 4)[1].start()

    def line_c(k, c):
        yy, xx = c_parts[c]

        @pl.when(jnp.logical_not(starts_line))
        def _():
            slot, copy = line_copy(sum_c, in_c1, 6, k, c, yy, xx, 4)
            line_receive(sum_c, in_c1, 6, k, slot, yy, xx)
            copy.start()

    def first_copy(which, i):
        yy_other = i < depth
        zz = targets[i % depth]
        if which == 0:
            where = (zz, 1 - y if yy_other else y, 1 - x)
            total, slots, peer = sum_a, in_a1, across_x
        else:
            where = (zz, 1 - y, 1 - x if yy_other else x)
            total, slots, peer = sum_b, in_b1, across_y
        source = total.at[chunk(total, *where), :]
        group = 0 if which == 0 else 3
        return remote(source, slots.at[i], sent[group].at[i], came[group].at[i], dp=peer)

    def second_copy(which, i):
        where = (targets[i], 1 - y, x) if which == 0 else (targets[i], y, 1 - x)
        total, slots, peer = (sum_a, in_a2, across_y) if which == 0 else (sum_b, in_b2, across_x)
        group = 1 if which == 0 else 4
        source = total.at[chunk(total, *where), :]
        return remote(source, slots.at[i], sent[group].at[i], came[group].at[i], dp=peer)

    def first_receive(which, i):
        first_copy(which, i).wait_recv()
        zz = targets[i % depth]
        if which == 0:
            where = (zz, 1 - y if i < depth else y, x)
            accumulate(sum_a, *where, in_a1.at[i])
        else:
            where = (zz, y, 1 - x if i < depth else x)
            accumulate(sum_b, *where, in_b1.at[i])
        if i < depth:
            second_copy(which, i).start()

    def line(which, k):
        total, came_in, slots = (sum_a, in_a2, in_a3) if which == 0 else (sum_b, in_b2, in_b3)
        group = 2 if which == 0 else 5
        second_copy(which, k).wait_recv()
        accumulate(total, targets[k], y, x, came_in.at[k])
        if k < depth - 1:
            slot, copy = line_copy(total, slots, group, k, 0, y, x, 1)

            @pl.when(jnp.logical_not(starts_line))
            def _():
                line_receive(total, slots, group, k, slot, y, x)

            copy.start()

    def line_end(total, slots, group, slot_below, slot_above, add):
        @pl.when(z > 0)
        def _():
            here = slots.at[slot_below]
            peer = index(z - 1, y, x)
            remote(here, here, sent[group].at[0], came[group].at[slot_below], dp=peer).wait_recv()
            add(here)

        @pl.when(z < depth - 1)
        def _():
            here = slots.at[slot_above]
            peer = index(z + 1, y, x)
            remote(here, here, sent[group].at[0], came[group].at[slot_above], dp=peer).wait_recv()
            add(here)

    def finish(which):
        total, slots, group = (sum_a, in_a3, 2) if which == 0 else (sum_b, in_b3, 5)
        own = chunk(total, z, y, x)
        if which == 0:
            hidden = out_fc1.shape[1]
            out_fc1[...] = total[own, :hidden].astype(F32)
            out_proj[...] = total[own, hidden:].astype(F32)

            def add(here):
                out_fc1[...] += here[:, :hidden].astype(F32)
                out_proj[...] += here[:, hidden:].astype(F32)
        else:
            out_fc2[...] = total[own, :].astype(F32)

            def add(here):
                out_fc2[...] += here[...].astype(F32)

        line_end(total, slots, group, z + 1, z, add)

    operands(2, 6, 1, 5)
    product(held[2], held[6], sum_a, 0)
    product(held[1], held[5], sum_a, held[6].shape[1])
    small_third()
    for i in range(2 * depth):
        first_copy(0, i).start()
    operands(3, 7)
    product(held[3], held[7], sum_b, 0)
    for i in range(2 * depth):
        first_copy(1, i).start()

    swapped_outputs()
    for i in range(depth):
        first_receive(1, i)
        first_receive(0, i)
        if i < 4:
            line_c(0, i)
    for c in range(depth, 4):
        line_c(0, c)
    for i in range(depth):
        first_receive(1, depth + i)
        first_receive(0, depth + i)
        if i < 4 and depth > 2:
            line_c(1, i)
    for k in range(2, depth - 1):
        for c in range(4):
            line_c(k, c)

    def end_c(c):
        yy, xx = c_parts[c]
        line_end(
            sum_c, in_c1, 6, (z + 1) * 4 + c, z * 4 + c,
            lambda here: accumulate(sum_c, z, yy, xx, here),
        )

    def copy_c2(c):
        yy, xx = c_parts[c]
        source = sum_c.at[chunk(sum_c, z, yy, xx), :]
        return remote(source, in_c2.at[c], sent[7].at[c], came[7].at[c], dp=across_x)

    def copy_c3():
        source = sum_c.at[chunk(sum_c, z, 1 - y, x), :]
        return remote(source, in_c3, sent[8].at[0], came[8].at[0], dp=across_y)

    line(1, 0)
    line(0, 0)
    for c in range(2):
        end_c(c)
        copy_c2(c).start()
    end_c(2)
    end_c(3)
    for k in range(1, depth - 1):
        line(1, k)
        line(0, k)
        if k == 1:
            copy_c2(0).wait_recv()
            accumulate(sum_c, z, 1 - y, x, in_c2.at[0])
            copy_c3().start()
            copy_c2(1).wait_recv()
            accumulate(sum_c, z, y, x, in_c2.at[1])
    line(1, depth - 1)
    line(0, depth - 1)
    copy_c3().wait_recv()
    out_qkv[...] = sum_c[chunk(sum_c, z, y, x), :].astype(F32) + in_c3[...].astype(F32)
    small_end()
    finish(1)
    finish(0)

    for i in range(5):
        extra_copy(i, 0).wait_send()
    small_x().wait_send()
    small_y().wait_send()
    for step in range(1, depth):
        small_z(step).wait_send()
    for i in order:
        theirs = held[i].at[pl.ds(ROWS, ROWS), :]
        remote(first[i], theirs, swap_sent.at[i], swap_came.at[i], pipe=1 - section).wait_send()
    for which in range(2):
        for i in range(2 * depth):
            first_copy(which, i).wait_send()
        for i in range(depth):
            second_copy(which, i).wait_send()
        for k in range(depth - 1):
            total, slots = (sum_a, in_a3) if which == 0 else (sum_b, in_b3)
            line_copy(total, slots, 2 if which == 0 else 5, k, 0, y, x, 1)[1].wait_send()
    for k in range(depth - 1):
        for c, (yy, xx) in enumerate(c_parts):
            line_copy(sum_c, in_c1, 6, k, c, yy, xx, 4)[1].wait_send()
    copy_c2(0).wait_send()
    copy_c2(1).wait_send()
    copy_c3().wait_send()


def scattered(count, kept, back0, back1, counts, tokens, entries):
    lefts = [kept[i] for i in (1, 6, 9, 10)]
    widths = [a.shape[2] for a in lefts] + [back0[i].shape[1] for i in (1, 2, 3, 4)]
    n1, merged, n2, act, gmixed, gbranch, ghidden, gb2 = widths
    heads = back0[6].shape[1]
    depth = count // (SIDE * SIDE)
    rows, rows_b = n1 // count, act // count
    cols_a = ghidden + gbranch
    copies = (2 * depth, depth, depth - 1, 2 * depth, depth, depth - 1, 4 * (depth - 1), 2, 1)
    arrivals = (2 * depth, depth, depth + 1, 2 * depth, depth, depth + 1, 4 * (depth + 1), 2, 1)
    tokens_g, tokens_l = tokens
    return pl.pallas_call(
        functools.partial(scatter_kernel, count),
        out_shape=(
            shape(rows, gmixed, dtype=F32), shape(rows, gbranch, dtype=F32),
            shape(rows, ghidden, dtype=F32), shape(rows_b, gb2, dtype=F32),
            shape(tokens_g, 2, n1), shape(tokens_l, 2, n1), shape(tokens_g, 2, n1), shape(tokens_l, 2, n1),
            *(shape(1, n1, dtype=F32) for _ in range(10)), shape(1, act, dtype=F32),
            shape(heads, 1, entries[0], dtype=F32), shape(heads, 1, entries[1], dtype=F32),
        ),
        in_specs=[OUTSIDE] * 12 + [INSIDE] * 11 + [SCALARS] * 2,
        out_specs=(INSIDE,) * 21,
        scratch_shapes=[pltpu.VMEM((2 * ROWS, w), BF16) for w in widths]
        + [pltpu.VMEM((n1, cols_a), BF16), pltpu.VMEM((act, gb2), BF16), pltpu.VMEM((n1, gmixed), BF16)]
        + [pltpu.VMEM((slots, rows, cols_a), BF16) for slots in (2 * depth, depth, depth + 1)]
        + [pltpu.VMEM((slots, rows_b, gb2), BF16) for slots in (2 * depth, depth, depth + 1)]
        + [pltpu.VMEM((4 * (depth + 1), rows, gmixed), BF16), pltpu.VMEM((2, rows, gmixed), BF16),
           pltpu.VMEM((rows, gmixed), BF16)]
        + [DMA((8,)), DMA((8,)), DMA((8,))]
        + [DMA((c,)) for c in copies] + [DMA((a,)) for a in arrivals]
        + [
            pltpu.VMEM((16, n1), F32), pltpu.VMEM((16, heads, LANES_G), F32),
            pltpu.VMEM((8, heads, LANES_L), F32), pltpu.VMEM((ROWS, n1), BF16), pltpu.VMEM((ROWS, n1), BF16),
            pltpu.VMEM((5, SMALL_ROWS, n1), F32), pltpu.VMEM((depth, SMALL_ROWS, n1), F32),
            DMA((6 + depth,)), DMA((6 + depth,)),
        ],
        compiler_params=pltpu.CompilerParams(
            vmem_limit_bytes=60 * 2**20, collective_id=1, has_side_effects=True
        ),
        name="gradient_scatter",
    )(
        *lefts, *back0[1:5], *back1[1:5], *back0[5:8], *back1[5:8],
        jnp.asarray(INDEX_G), jnp.asarray(INDEX_L), kept[0], back0[0], back1[0], *counts,
    )


def swapped(value):
    return lax.ppermute(value, "pipe", [(0, 1), (1, 0)])


def plain_scattered(kept, back0, back1, counts, tokens, entries):
    section = lax.axis_index("pipe")
    tokens_g, tokens_l = tokens

    def exchange(layer0, layer1):
        keep = jnp.where(section == 0, layer0, layer1)
        send = jnp.where(section == 0, layer1, layer0)
        return keep, swapped(send)

    lefts = [exchange(kept[i][0], kept[i][1]) for i in (1, 6, 9, 10)]
    rights = [exchange(back0[i], back1[i]) for i in (1, 2, 3, 4)]
    shares = [
        lax.psum_scatter(
            dot_rows(jnp.concatenate(a, 0), jnp.concatenate(b, 0)).astype(BF16),
            "dp", scatter_dimension=0, tiled=True,
        ).astype(F32)
        for a, b in zip(lefts, rights)
    ]
    small, tg, tl = (a + b for a, b in (exchange(back0[i], back1[i]) for i in (5, 6, 7)))
    width = small.shape[1]

    def fold(values, index, count):
        flat = jnp.transpose(values, (1, 0, 2)).reshape(values.shape[1], -1)
        high = flat.astype(BF16)
        low = (flat - high.astype(F32)).astype(BF16)
        spot = hot(jnp.asarray(index.reshape(1, -1)), count)
        sums = dot_cols(jnp.concatenate([high, low], 0), spot)
        return sums[: values.shape[1]] + sums[values.shape[1]:]

    small, tg, tl = lax.psum((small, fold(tg, INDEX_G, width), fold(tl, INDEX_L, 128)), "dp")

    def both_crops(keep, came):
        low = jnp.where(section == 0, keep, came)
        high = jnp.where(section == 0, came, keep)
        return (
            jnp.stack([low[:tokens_g], high[:tokens_g]], 1),
            jnp.stack([low[LOCAL_ROW:LOCAL_ROW + tokens_l], high[LOCAL_ROW:LOCAL_ROW + tokens_l]], 1),
        )

    out_g, out_l = both_crops(*exchange(kept[0][0], kept[0][1]))
    crop = jnp.arange(2, dtype=jnp.int32)[None, :, None]
    out_g = jnp.where(crop < counts[0][0], out_g, jnp.zeros_like(out_g))
    out_l = jnp.where(crop < counts[1][0], out_l, jnp.zeros_like(out_l))
    gin_g, gin_l = both_crops(*exchange(back0[0], back1[0]))
    hidden = back0[3].shape[1]
    rows = [small[i:i + 1] for i in range(F1B)]
    rows.append(small[F1B:F1B + hidden // width].reshape(1, hidden))
    tables = (tg[:, None, :entries[0]], tl[:, None, :entries[1]])
    return (*shares, out_g, out_l, gin_g, gin_l, *rows, *tables)


def finish_kernel(*refs):
    half = len(refs) // 2
    for source, target in zip(refs[:half], refs[half:]):
        target[...] = source[...]


def finished(arrays):
    return pl.pallas_call(
        finish_kernel,
        out_shape=tuple(shape(*a.shape, dtype=a.dtype) for a in arrays),
        in_specs=[INSIDE] * len(arrays),
        out_specs=(INSIDE,) * len(arrays),
        name="results",
    )(*arrays)


def body(
    x_global, x_local, cot_global, cot_local, global_count, local_count,
    w_qkv, w_proj, w_fc1, w_fc2,
    norm1_gain, norm1_shift, q_bias, v_bias, proj_bias, scale_attn,
    norm2_gain, norm2_shift, fc1_bias, fc2_bias, scale_mlp,
    table_global, table_local,
):
    width = x_global.shape[2]
    entries_g, heads = table_global.shape[1:]
    entries_l = table_local.shape[1]
    tokens = (x_global.shape[1], x_local.shape[1])
    own = (w_qkv[0], w_proj[0], w_fc1[0], w_fc2[0])
    vec = (norm1_gain, norm1_shift, q_bias, v_bias, proj_bias, scale_attn, norm2_gain, norm2_shift,
           fc2_bias, scale_mlp, fc1_bias)
    tables = (table_global[0].T, table_local[0].T)
    crops = tuple(jnp.transpose(a, (1, 0, 2)) for a in (x_global, x_local))
    cots = tuple(jnp.transpose(a, (1, 0, 2)) for a in (cot_global, cot_local))
    results = forward(*crops, vec, tables, own)
    other, kept, vec = results[:4], results[4:17], results[17]
    counts = (global_count, local_count)
    back1 = backward(1, (*cots, *counts), kept[0], vec, kept, heads, own, other)
    back0 = backward(0, back1[0], crops, vec, kept, heads, own, other)
    count = lax.axis_size("dp")
    given = (kept, back0, back1, counts, tokens, (entries_g, entries_l))
    if count % (2 * SIDE * SIDE) == 0 and width % (16 * count) == 0:
        results = finished(scattered(count, *given))
    else:
        results = plain_scattered(*given)
    shares, crops, small, tables = results[:4], results[4:8], results[8:19], results[19:]
    vectors = [small[i] for i in (N1G, N1S, QB, VB, PB, SA, N2G, N2S, F1B, F2B, SM)]
    return (
        *(jnp.transpose(c, (1, 0, 2))[None] for c in crops),
        *(s[None] for s in shares),
        *vectors,
        *(jnp.transpose(t, (1, 2, 0)) for t in tables),
    )


def solution(mesh):
    three, two = P("pipe", None, None), P("pipe", None)
    rows = P("dp", None, None)
    in_specs = (rows,) * 4 + (P("dp"),) * 2 + (three,) * 4 + (two,) * 11 + (three,) * 2
    crops = P("pipe", "dp", None, None)
    out_specs = (crops,) * 4 + (P("pipe", "dp", None),) * 4 + (two,) * 11 + (three,) * 2
    return jax.shard_map(body, mesh=mesh, in_specs=in_specs, out_specs=out_specs, check_vma=False)
```

```python
import functools
import jax
import jax.numpy as jnp
import numpy as np
from jax import lax
from jax.experimental import pallas as pl
from jax.experimental.pallas import tpu as pltpu
from jax.sharding import PartitionSpec as P

GRID_G = 14
GRID_L = 6
ROWS = 256
LOCAL_ROW = 208
LANES_G = 512
LANES_L = 128
FRONT_L = 51
BLOCK = 256
NEG = -1e30
eps = 1e-06
F32 = jnp.float32
BF16 = jnp.bfloat16
INV_SQRT2 = 0.7071067811865476
INV_SQRT_2PI = 0.3989422804014327
N1G, N1S, QB, VB, PB, SA, N2G, N2S, F2B, SM, F1B = range(11)


def spread_index(grid, rows, lanes, front, cls_lane):
    side = 2 * grid - 1
    entries = side * side
    index = np.full((rows, lanes), -1, np.int32)
    for q in range(grid):
        for a in range(side):
            for k in range(grid):
                index[q, front + a * grid + k] = (side - 1 - a) * side + (q - k + grid - 1)
    index[rows - 2, :] = entries
    index[rows - 2, cls_lane] = entries + 2
    index[rows - 1, :] = entries + 1
    return index


INDEX_G = spread_index(GRID_G, 16, LANES_G, 1, 0)
INDEX_L = spread_index(GRID_L, 8, LANES_L, FRONT_L, LOCAL_ROW - 128)


def dot(a, b):
    return lax.dot_general(a, b, (((1,), (0,)), ((), ())), preferred_element_type=F32)


def dot_cols(a, b):
    return lax.dot_general(a, b, (((1,), (1,)), ((), ())), preferred_element_type=F32)


def dot_rows(a, b):
    return lax.dot_general(a, b, (((0,), (0,)), ((), ())), preferred_element_type=F32)


def normalised(x):
    centered = x - jnp.mean(x, axis=-1, keepdims=True)
    rstd = lax.rsqrt(jnp.mean(centered * centered, axis=-1, keepdims=True) + eps)
    return centered * rstd, rstd


def row_steps(step, body):
    def one(i, carry):
        body(pl.ds(pl.multiple_of(i * step, step), step))
        return carry

    lax.fori_loop(0, ROWS // step, one, 0)


def build_bias(spread_g, spread_l, bias):
    for r in range(GRID_G):
        shifted = pltpu.roll(spread_g, (LANES_G - (GRID_G - 1 - r) * GRID_G) % LANES_G, 1)
        bias[pl.ds(1 + GRID_G * r, GRID_G), :] = shifted[:GRID_G, :ROWS]
    for r in range(GRID_L):
        shifted = pltpu.roll(spread_l, GRID_L * r, 1)
        bias[pl.ds(LOCAL_ROW + 1 + GRID_L * r, GRID_L), pl.ds(128, 128)] = shifted[:GRID_L, :]
    tokens_g = GRID_G * GRID_G + 1
    tokens_l = GRID_L * GRID_L + 1
    top = bias[:LOCAL_ROW, :]
    row = lax.broadcasted_iota(jnp.int32, top.shape, 0)
    col = lax.broadcasted_iota(jnp.int32, top.shape, 1)
    top = jnp.where(col == 0, spread_g[15:16, :ROWS], top)
    top = jnp.where(row == 0, spread_g[14:15, :ROWS], top)
    top = jnp.where(row >= tokens_g, 0.0, top)
    top = jnp.where(col >= tokens_g, NEG, top)
    low = bias[LOCAL_ROW:, 128:]
    row = lax.broadcasted_iota(jnp.int32, low.shape, 0)
    col = lax.broadcasted_iota(jnp.int32, low.shape, 1) - (LOCAL_ROW - 128)
    low = jnp.where(col == 0, spread_l[7:8], low)
    low = jnp.where(row == 0, spread_l[6:7], low)
    low = jnp.where(row >= tokens_l, 0.0, low)
    low = jnp.where((col >= 0) & (col < tokens_l), low, NEG)
    bottom = jnp.concatenate([jnp.full((ROWS - LOCAL_ROW, 128), NEG, F32), low], 1)
    return jnp.concatenate([top, bottom], 0)


MESH = pl.DeviceIdType.MESH
SIDE = 2
FLIGHT = 4
TABLE_ROW, TABLE_ROW_L, SMALL_ROWS = 16, 32, 48


def remote(source, target, sent, came, **device):
    return pltpu.make_async_remote_copy(
        src_ref=source, dst_ref=target, send_sem=sent, recv_sem=came,
        device_id=device, device_id_type=MESH,
    )


def hot(index_row, count):
    number = lax.broadcasted_iota(jnp.int32, (count, index_row.shape[1]), 0)
    return jnp.where(number == index_row, 1.0, 0.0).astype(BF16)


def place_crops(target, global_ref, local_ref, section, live_g=None, live_l=None):
    target[...] = jnp.zeros_like(target)
    for ref, start, live in ((global_ref, 0, live_g), (local_ref, LOCAL_ROW, live_l)):
        rows = jnp.where(section == 0, ref[:, 0, :].astype(F32), ref[:, 1, :].astype(F32))
        if live is not None:
            rows = rows * live
        target[start:start + ref.shape[0], :] = rows.astype(BF16)


def forward_kernel(
    scale, keep_both,
    xg_ref, xl_ref, vec_refs, tg_ref, tl_ref, index_g, index_l, own_qkv, own_proj, own_fc1, own_fc2,
    oth_qkv, oth_proj, oth_fc1, oth_fc2,
    out_all, n1_all, q_all, k_all, v_all, p_all, merged_all, branch_all, middle_all,
    n2_all, act_all, dact_all, branch2_all, small_out,
    w_qkv, w_proj, w_fc1, w_fc2, small_in, small, vec_all, x_in, out_ref, n1_ref, q_ref, k_ref, v_ref, p_ref,
    merged_ref, branch_ref, middle_ref, n2_ref, act_ref, dact_ref, branch2_ref,
    spread_g, spread_l, bias, own_sem, sent, came, keep_sem, store_sem, give_sent, give_came, small_sem,
):
    section = lax.axis_index("pipe")
    partner = 1 - section
    own = (own_qkv, own_proj, own_fc1, own_fc2)
    oth = (oth_qkv, oth_proj, oth_fc1, oth_fc2)
    held = (w_qkv, w_proj, w_fc1, w_fc2)
    width = x_in.shape[1]
    heads = p_ref.shape[1]
    half = SMALL_ROWS

    barrier = pltpu.get_barrier_semaphore()
    pl.semaphore_signal(barrier, inc=1, device_id={"pipe": partner}, device_id_type=MESH)
    for i in range(4):
        pltpu.make_async_copy(own[i], held[i].at[section], own_sem.at[i]).start()
    small_rows = small.at[pl.ds(pl.multiple_of(section * half, half), half), :]
    small_in[...] = jnp.zeros_like(small_in)
    row = 0
    for ref in vec_refs:
        for b in range(0, ref.shape[1], width):
            small_in[row:row + 1, :] = ref[:, b:b + width].astype(F32)
            row += 1
    small_in[TABLE_ROW:TABLE_ROW + heads, 0:tg_ref.shape[1]] = tg_ref[...].astype(F32)
    small_in[TABLE_ROW_L:TABLE_ROW_L + heads, 0:tl_ref.shape[1]] = tl_ref[...].astype(F32)
    pl.semaphore_wait(barrier, 1)
    small_copy = remote(small_in, small_rows, small_sem.at[0], small_sem.at[1], pipe=partner)
    small_copy.start()

    def weight_copy(i):
        return remote(own[i], held[i].at[section], sent.at[i], came.at[i], pipe=partner)

    for i in range(4):
        weight_copy(i).start()
    small_rows[...] = small_in[...]
    place_crops(x_in, xg_ref, xl_ref, section)
    small_copy.wait_recv()
    vec_all[...] = small[...]
    small_out[...] = vec_all[...]
    tables_g = jnp.concatenate(
        [small[TABLE_ROW:TABLE_ROW + 16, :], small[half + TABLE_ROW:half + TABLE_ROW + 16, :]], 0
    )
    tables_l = jnp.concatenate(
        [small[TABLE_ROW_L:TABLE_ROW_L + 16, :128], small[half + TABLE_ROW_L:half + TABLE_ROW_L + 16, :128]], 0
    )
    for tables, index_ref, spread, grid, cls_lane in (
        (tables_g, index_g, spread_g, GRID_G, 0), (tables_l, index_l, spread_l, GRID_L, LOCAL_ROW - 128),
    ):
        span, lanes = tables.shape[1], index_ref.shape[1]
        shifted = [tables] + [pltpu.roll(tables, span - r, 1) for r in range(1, grid)]
        found = dot(jnp.concatenate(shifted, 0).astype(BF16), hot(index_ref[0:1, :], span))
        cls = (2 * grid - 1) ** 2
        lane_all = lax.broadcasted_iota(jnp.int32, (1, lanes), 1)
        to_patch = jnp.where(lane_all == cls_lane, tables[:, cls + 2:cls + 3], tables[:, cls:cls + 1])
        to_class = jnp.broadcast_to(tables[:, cls + 1:cls + 2], to_patch.shape)
        for layer in range(2):
            for r in range(grid):
                spread[layer, :, r, :] = found[32 * r + 16 * layer:32 * r + 16 * layer + 16]
            spread[layer, :, grid, :] = to_patch[16 * layer:16 * layer + 16]
            spread[layer, :, grid + 1, :] = to_class[16 * layer:16 * layer + 16]

    slots = (
        out_ref, n1_ref, q_ref, k_ref, v_ref, p_ref, merged_ref, branch_ref, middle_ref,
        n2_ref, act_ref, dact_ref, branch2_ref,
    )
    results = (
        out_all, n1_all, q_all, k_all, v_all, p_all, merged_all, branch_all, middle_all,
        n2_all, act_all, dact_all, branch2_all,
    )
    OUT, N1, Q, K, V, PR, ME, BR, MI, N2, AC, DA, B2 = range(13)
    GIVEN = (OUT, N1, ME, N2, AC)

    def store_copy(number, layer):
        return pltpu.make_async_copy(
            slots[number].at[layer], results[number].at[layer], store_sem.at[layer, number]
        )

    def give_copy(number, layer):
        spot = number if layer == 0 else 13 + GIVEN.index(number)
        return remote(
            slots[number].at[layer], results[number].at[2], give_sent.at[spot], give_came.at[spot],
            pipe=partner,
        )

    def store(layer, *numbers):
        for number in numbers:
            store_copy(number, layer).start()
            if layer == 0 or number in GIVEN:

                @pl.when(section != layer)
                def _():
                    give_copy(number, layer).start()

    def stored(layer, *numbers):
        for number in numbers:
            store_copy(number, layer).wait()
            if layer == 0 or number in GIVEN:

                @pl.when(section != layer)
                def _():
                    give_copy(number, layer).wait_send()

    def weight(i, layer):
        @pl.when(section == layer)
        def _():
            pltpu.make_async_copy(own[i], held[i].at[section], own_sem.at[i]).wait()

        @pl.when(section != layer)
        def _():
            here = held[i].at[partner]
            remote(here, here, sent.at[i], came.at[i], pipe=partner).wait_recv()
            if layer == 1 or keep_both:
                pltpu.make_async_copy(here, oth[i], keep_sem.at[i]).start()

    lane = lax.broadcasted_iota(jnp.int32, (1, 128), 1)
    for layer in range(2):
        entering = x_in if layer == 0 else slots[OUT].at[0]
        (
            out_ref, n1_ref, q_ref, k_ref, v_ref, p_ref, merged_ref, branch_ref, middle_ref,
            n2_ref, act_ref, dact_ref, branch2_ref,
        ) = (slot.at[layer] for slot in slots)
        base = layer * half

        def vec(row):
            return vec_all[base + row:base + row + 1, :]

        def norm1(rows):
            xhat, _ = normalised(entering[rows, :].astype(F32))
            n1_ref[rows, :] = (xhat * vec(N1G) + vec(N1S)).astype(BF16)

        row_steps(32, norm1)
        store(layer, N1)
        weight(0, layer)
        n1 = n1_ref[...]
        for b in range(0, width, BLOCK):
            cols = slice(b, b + BLOCK)
            mixed = dot(n1, w_qkv[layer, :, b:b + BLOCK]) + vec(QB)[:, cols]
            q_ref[:, cols] = (mixed * scale).astype(BF16)
            k_ref[:, cols] = dot(n1, w_qkv[layer, :, width + b:width + b + BLOCK]).astype(BF16)
            mixed = dot(n1, w_qkv[layer, :, 2 * width + b:2 * width + b + BLOCK]) + vec(VB)[:, cols]
            v_ref[:, cols] = mixed.astype(BF16)
        store(layer, Q, K, V)
        for pair in range(heads // 2):
            cols = slice(pair * 128, pair * 128 + 128)
            q, k, v = q_ref[:, cols], k_ref[:, cols], v_ref[:, cols]
            result = None
            for part in range(2):
                head = 2 * pair + part
                mine = (lane < 64) if part == 0 else (lane >= 64)
                scores = dot_cols(q, jnp.where(mine, k, jnp.zeros_like(k))) + build_bias(
                    spread_g[layer, head], spread_l[layer, head], bias.at[head % 2]
                )
                expo = jnp.exp(scores - jnp.max(scores, axis=-1, keepdims=True))
                probs = expo * (1.0 / jnp.sum(expo, axis=-1, keepdims=True))
                low = probs.astype(BF16)
                p_ref[head] = low
                piece = dot(low, jnp.where(mine, v, jnp.zeros_like(v)))
                result = piece if result is None else result + piece
            merged_ref[:, cols] = result.astype(BF16)
        store(layer, PR, ME)
        weight(1, layer)
        merged = merged_ref[...]
        for b in range(0, width, BLOCK):
            cols = slice(b, b + BLOCK)
            branch = dot(merged, w_proj[layer, :, cols]) + vec(PB)[:, cols]
            branch_ref[:, cols] = branch
            middle_ref[:, cols] = entering[:, cols].astype(F32) + vec(SA)[:, cols] * branch
        store(layer, BR, MI)

        def norm2(rows):
            xhat, _ = normalised(middle_ref[rows, :])
            n2_ref[rows, :] = (xhat * vec(N2G) + vec(N2S)).astype(BF16)

        row_steps(32, norm2)
        store(layer, N2)
        weight(2, layer)
        n2 = n2_ref[...]
        for b in range(0, w_fc1.shape[2], BLOCK):
            cols = slice(b, b + BLOCK)
            part = b // width
            hidden = dot(n2, w_fc1[layer, :, cols]) + vec(F1B + part)[:, b - part * width:b - part * width + BLOCK]
            cdf = 0.5 + 0.5 * lax.erf(hidden * INV_SQRT2)
            act_ref[:, cols] = (hidden * cdf).astype(BF16)
            slope = cdf + hidden * (INV_SQRT_2PI * jnp.exp(-0.5 * hidden * hidden))
            dact_ref[:, cols] = slope.astype(BF16)
        store(layer, AC, DA)
        weight(3, layer)
        for b in range(0, width, BLOCK):
            cols = slice(b, b + BLOCK)
            branch2 = dot(act_ref[...], w_fc2[layer, :, cols]) + vec(F2B)[:, cols]
            branch2_ref[:, cols] = branch2
            out_ref[:, cols] = (middle_ref[:, cols] + vec(SM)[:, cols] * branch2).astype(BF16)
        store(layer, B2, OUT)
    stored(0, *range(13))
    stored(1, *range(13))
    for i in range(4):
        weight_copy(i).wait_send()
    small_copy.wait_send()

    def weights_kept():
        for i in range(4):
            pltpu.make_async_copy(held[i].at[partner], oth[i], keep_sem.at[i]).wait()

    @pl.when(section == 0)
    def _():
        weights_kept()
        for number in range(13):
            give_copy(number, 0).wait_recv()

    @pl.when(section != 0)
    def _():
        if keep_both:
            weights_kept()
        for number in GIVEN:
            give_copy(number, 1).wait_recv()


X, Q, K, V, PR, BR, MI, DA, B2 = range(9)


def clear(*refs):
    for ref in refs:
        ref[...] = jnp.zeros_like(ref)


def backward_steps(
    scale, vec, weight, loaded, done, g_ref, gx_ref, kept, weights, grads, sums, scratch,
):
    x_ref, q_ref, k_ref, v_ref, p_ref, branch_ref, middle_ref, dact_ref, branch2_ref = kept
    w_qkv, w_proj, w_fc1, w_fc2 = weights
    gmixed_ref, gbranch_ref, ghidden_ref, gb2_ref = grads
    small_ref, tg_ref, tl_ref = sums
    gmid, gnorm, gmerged = scratch
    width = g_ref.shape[1]
    heads = p_ref.shape[0]

    def add_small(row, values):
        small_ref[row:row + 1, :] += jnp.sum(values, axis=0, keepdims=True)

    loaded(B2)

    def scaled(rows):
        grad = g_ref[rows, :].astype(F32)
        low = (vec(SM) * grad).astype(BF16)
        gb2_ref[rows, :] = low
        add_small(SM, grad * branch2_ref[rows, :])
        add_small(F2B, low.astype(F32))

    row_steps(32, scaled)
    done(3, B2)
    weight(3)
    loaded(DA)
    gb2 = gb2_ref[...]
    for b in range(0, w_fc1.shape[1], BLOCK):
        cols = slice(b, b + BLOCK)
        part = b // width
        ghidden = (dot_cols(gb2, w_fc2[cols, :]) * dact_ref[:, cols]).astype(BF16)
        ghidden_ref[:, cols] = ghidden
        small_ref[F1B + part:F1B + part + 1, b - part * width:b - part * width + BLOCK] += jnp.sum(
            ghidden.astype(F32), axis=0, keepdims=True
        )
    done(2, DA)
    weight(2)
    for b in range(0, width, BLOCK):
        gnorm[:, b:b + BLOCK] = dot_cols(ghidden_ref[...], w_fc1[b:b + BLOCK, :])

    def norm_back(values, grad, gain):
        xhat, rstd = normalised(values)
        scaled_grad = grad * gain
        mean1 = jnp.mean(scaled_grad, axis=-1, keepdims=True)
        mean2 = jnp.mean(scaled_grad * xhat, axis=-1, keepdims=True)
        return xhat, rstd * (scaled_grad - mean1 - xhat * mean2)

    loaded(MI, BR)

    def norm2(rows):
        grad = gnorm[rows, :]
        xhat, through = norm_back(middle_ref[rows, :], grad, vec(N2G))
        grad_middle = g_ref[rows, :].astype(F32) + through
        gmid[rows, :] = grad_middle
        add_small(N2G, grad * xhat)
        add_small(N2S, grad)
        add_small(SA, grad_middle * branch_ref[rows, :])
        low = (vec(SA) * grad_middle).astype(BF16)
        gbranch_ref[rows, :] = low
        add_small(PB, low.astype(F32))

    row_steps(32, norm2)
    done(1, MI, BR)
    weight(1)
    for b in range(0, width, BLOCK):
        gmerged[:, b:b + BLOCK] = dot_cols(gbranch_ref[...], w_proj[b:b + BLOCK, :]).astype(BF16)
    lane = lax.broadcasted_iota(jnp.int32, (1, 128), 1)
    loaded(V, PR, K, Q)
    lane_all = lax.broadcasted_iota(jnp.int32, (1, ROWS), 1)
    for pair in range(heads // 2):
        cols = slice(pair * 128, pair * 128 + 128)
        q, k, v, gm = q_ref[:, cols], k_ref[:, cols], v_ref[:, cols], gmerged[:, cols]
        gq = gk = gv = 0.0
        for half in range(2):
            head = 2 * pair + half
            mine = (lane < 64) if half == 0 else (lane >= 64)

            def only(values):
                return jnp.where(mine, values, jnp.zeros_like(values))

            low = p_ref[head]
            probs = low.astype(F32)
            grad_probs = dot_cols(gm, only(v))
            total = jnp.sum(probs * grad_probs, axis=-1, keepdims=True)
            gscores = (probs * (grad_probs - total)).astype(BF16)
            gv += dot_rows(low, only(gm))
            gq += dot(gscores, only(k))
            gk += dot_rows(gscores, only(q))
            wide = gscores.astype(F32)
            gs = gnorm.at[:, pl.ds(ROWS * (head % 2), ROWS)]
            gs[...] = jnp.where((lane_all == 0) | (lane_all == LOCAL_ROW), 0.0, wide)
            acc = jnp.zeros((GRID_G, LANES_G), F32)
            for r in range(GRID_G):
                block = gs[pl.ds(1 + GRID_G * r, GRID_G), :]
                block = jnp.concatenate([block, jnp.zeros_like(block)], 1)
                acc += pltpu.roll(block, (GRID_G - 1 - r) * GRID_G, 1)
            first_row = wide[0:1, :]
            to_class = jnp.sum(wide[:LOCAL_ROW, :], axis=0, keepdims=True) - first_row
            to_class = jnp.where(lane_all == 0, to_class, 0.0)
            blank = jnp.zeros((1, LANES_G - ROWS), F32)
            tg_ref[0:GRID_G, head, :] += acc
            tg_ref[14, head:head + 1, :] += jnp.concatenate([first_row, blank], 1)
            tg_ref[15, head:head + 1, :] += jnp.concatenate([to_class, blank], 1)
            acc = jnp.zeros((GRID_L, LANES_L), F32)
            for r in range(GRID_L):
                block = gs[pl.ds(LOCAL_ROW + 1 + GRID_L * r, GRID_L), pl.ds(128, 128)]
                acc += pltpu.roll(block, (LANES_L - GRID_L * r) % LANES_L, 1)
            first_row = wide[LOCAL_ROW:LOCAL_ROW + 1, 128:]
            to_class = jnp.sum(wide[LOCAL_ROW:, 128:], axis=0, keepdims=True) - first_row
            to_class = jnp.where(lane == LOCAL_ROW - 128, to_class, 0.0)
            tl_ref[0:GRID_L, head, :] += acc
            tl_ref[6, head:head + 1, :] += first_row
            tl_ref[7, head:head + 1, :] += to_class
        gmixed_ref[:, cols] = gq.astype(BF16) * jnp.asarray(scale, BF16)
        gmixed_ref[:, slice(width + cols.start, width + cols.stop)] = gk.astype(BF16)
        gmixed_ref[:, slice(2 * width + cols.start, 2 * width + cols.stop)] = gv.astype(BF16)

    def biases(rows):
        add_small(QB, gmixed_ref[rows, :width].astype(F32))
        add_small(VB, gmixed_ref[rows, 2 * width:].astype(F32))

    done(0, V, PR, K, Q)
    row_steps(32, biases)
    weight(0)
    loaded(X)
    for b in range(0, width, BLOCK):
        gnorm[:, b:b + BLOCK] = dot_cols(gmixed_ref[...], w_qkv[b:b + BLOCK, :])

    def norm1(rows):
        grad = gnorm[rows, :]
        xhat, through = norm_back(x_ref[rows, :].astype(F32), grad, vec(N1G))
        add_small(N1G, grad * xhat)
        add_small(N1S, grad)
        gx_ref[rows, :] = (gmid[rows, :] + through).astype(BF16)

    row_steps(32, norm1)


def backward_kernel(
    layer, scale, given, vec_all,
    x_all, q_all, k_all, v_all, p_all, branch_all, middle_all, dact_all, branch2_all,
    own_qkv, own_proj, own_fc1, own_fc2, oth_qkv, oth_proj, oth_fc1, oth_fc2,
    gx_ref, gmixed_out, gbranch_out, ghidden_out, gb2_out, small_ref, tg_ref, tl_ref,
    g_ref, x_ref, q_ref, k_ref, v_ref, p_ref, branch_ref, middle_ref, dact_ref, branch2_ref,
    w_qkv, w_proj, w_fc1, w_fc2, gmixed_ref, gbranch_ref, ghidden_ref, gb2_ref,
    gmid, gnorm, gmerged, load_sem, weight_sem, store_sem,
):
    own = (own_qkv, own_proj, own_fc1, own_fc2)
    oth = (oth_qkv, oth_proj, oth_fc1, oth_fc2)
    section = lax.axis_index("pipe")
    held = (w_qkv, w_proj, w_fc1, w_fc2)
    kept = (x_ref, q_ref, k_ref, v_ref, p_ref, branch_ref, middle_ref, dact_ref, branch2_ref)
    sources = (x_all, q_all, k_all, v_all, p_all, branch_all, middle_all, dact_all, branch2_all)
    grads = (gmixed_ref, gbranch_ref, ghidden_ref, gb2_ref)
    targets = (gmixed_out, gbranch_out, ghidden_out, gb2_out)

    def load_copy(number):
        source = sources[number].at[0 if number == X else layer]
        return pltpu.make_async_copy(source, kept[number], load_sem.at[number])

    def load_weight(i):
        @pl.when(section == layer)
        def _():
            pltpu.make_async_copy(own[i], held[i], weight_sem.at[i]).start()

        @pl.when(section != layer)
        def _():
            pltpu.make_async_copy(oth[i], held[i], weight_sem.at[i]).start()

    def weight(i):
        pltpu.make_async_copy(own[i], held[i], weight_sem.at[i]).wait()

    def loaded(*numbers):
        for number in numbers:
            if layer == 1 or number != X:
                load_copy(number).wait()

    def store_copy(number):
        return pltpu.make_async_copy(grads[number], targets[number], store_sem.at[number])

    def done(number, *unused):
        store_copy(number).start()

    def vec(row):
        return vec_all[layer * SMALL_ROWS + row:layer * SMALL_ROWS + row + 1, :]

    load_copy(B2).start()
    load_weight(3)
    load_copy(DA).start()
    load_weight(2)
    for number in (MI, BR):
        load_copy(number).start()
    load_weight(1)
    for number in (V, PR, K, Q):
        load_copy(number).start()
    load_weight(0)
    clear(small_ref, tg_ref, tl_ref)
    if layer == 1:
        cg_ref, cl_ref, gcount, lcount = given
        load_copy(X).start()
        live_g = jnp.where(gcount[0] > section, 1.0, 0.0)
        live_l = jnp.where(lcount[0] > section, 1.0, 0.0)
        place_crops(g_ref, cg_ref, cl_ref, section, live_g, live_l)
    else:
        g_ref, xg_ref, xl_ref = given
        place_crops(x_ref, xg_ref, xl_ref, section)
    backward_steps(
        scale, vec, weight, loaded, done, g_ref, gx_ref, kept, held, grads,
        (small_ref, tg_ref, tl_ref), (gmid, gnorm, gmerged),
    )
    for number in range(4):
        store_copy(number).wait()


def shape(*dims, dtype=BF16):
    return jax.ShapeDtypeStruct(dims, dtype)


INSIDE = pl.BlockSpec(memory_space=pltpu.VMEM)
OUTSIDE = pl.BlockSpec(memory_space=pl.ANY)
SCALARS = pl.BlockSpec(memory_space=pltpu.SMEM)
DMA = pltpu.SemaphoreType.DMA


def forward(x_global, x_local, vec, tables, own, keep_both):
    width = x_global.shape[2]
    heads = tables[0].shape[0]
    hidden = own[2].shape[1]
    scale = (width // heads) ** (-0.5)
    kept = (
        ((ROWS, width), BF16), ((ROWS, width), BF16), ((ROWS, width), BF16), ((ROWS, width), BF16),
        ((ROWS, width), BF16), ((heads, ROWS, ROWS), BF16), ((ROWS, width), BF16),
        ((ROWS, width), F32), ((ROWS, width), F32), ((ROWS, width), BF16),
        ((ROWS, hidden), BF16), ((ROWS, hidden), BF16), ((ROWS, width), F32),
    )
    scratch = [pltpu.VMEM((2, *w.shape), BF16) for w in own]
    scratch += [pltpu.VMEM((SMALL_ROWS, width), F32)] + [pltpu.VMEM((2 * SMALL_ROWS, width), F32)] * 2
    scratch += [pltpu.VMEM((ROWS, width), BF16)]
    scratch += [pltpu.VMEM((2, *dims), kind) for dims, kind in kept]
    scratch += [
        pltpu.VMEM((2, 16, 16, LANES_G), F32), pltpu.VMEM((2, 16, 8, LANES_L), F32),
        pltpu.VMEM((2, ROWS, ROWS), F32),
        DMA((4,)), DMA((4,)), DMA((4,)), DMA((4,)), DMA((2, 13)), DMA((18,)), DMA((18,)), DMA((2,)),
    ]

    def kernel(xg, xl, *refs):
        count = len(vec)
        forward_kernel(scale, keep_both, xg, xl, refs[:count], *refs[count:])

    return pl.pallas_call(
        kernel,
        out_shape=tuple(shape(*w.shape) for w in own)
        + tuple(shape(3, *dims, dtype=kind) for dims, kind in kept)
        + (shape(2 * SMALL_ROWS, width, dtype=F32),),
        in_specs=[INSIDE] * (6 + len(vec)) + [OUTSIDE] * 4,
        out_specs=(OUTSIDE,) * 17 + (INSIDE,),
        scratch_shapes=scratch,
        compiler_params=pltpu.CompilerParams(
            vmem_limit_bytes=60 * 2**20, collective_id=2, has_side_effects=True
        ),
        name="forward_layers",
    )(x_global, x_local, *vec, *tables, jnp.asarray(INDEX_G), jnp.asarray(INDEX_L), *own)


def backward(layer, given, vec, kept, heads, own, other):
    width = vec.shape[1]
    hidden = own[2].shape[1]
    scale = (width // heads) ** (-0.5)
    first, n1, q, k, v, probs, merged, branch, middle, n2, act, dact, branch2 = kept
    count = len(given)

    def kernel(*refs):
        backward_kernel(layer, scale, refs[:count], *refs[count:])

    return pl.pallas_call(
        kernel,
        out_shape=(
            shape(ROWS, width), shape(ROWS, 3 * width), shape(ROWS, width), shape(ROWS, hidden),
            shape(ROWS, width), shape(16, width, dtype=F32),
            shape(16, 16, LANES_G, dtype=F32), shape(8, 16, LANES_L, dtype=F32),
        ),
        in_specs=[SCALARS if g.ndim == 1 else INSIDE for g in given] + [INSIDE] + [OUTSIDE] * 17,
        out_specs=(INSIDE,) + (OUTSIDE,) * 4 + (INSIDE,) * 3,
        scratch_shapes=[pltpu.VMEM((ROWS, width), BF16)] + kept_scratch(heads, width, hidden)
        + [pltpu.VMEM(w.shape, BF16) for w in own]
        + [pltpu.VMEM((ROWS, c), BF16) for c in (3 * width, width, hidden, width)]
        + work_scratch(width) + [DMA((9,)), DMA((4,)), DMA((4,))],
        compiler_params=pltpu.CompilerParams(vmem_limit_bytes=60 * 2**20),
        name="layer_backward",
    )(*given, vec, first, q, k, v, probs, branch, middle, dact, branch2, *own, *other)


def kept_scratch(heads, width, hidden):
    return [pltpu.VMEM((ROWS, width), BF16) for _ in range(4)] + [
        pltpu.VMEM((heads, ROWS, ROWS), BF16), pltpu.VMEM((ROWS, width), F32),
        pltpu.VMEM((ROWS, width), F32), pltpu.VMEM((ROWS, hidden), BF16), pltpu.VMEM((ROWS, width), F32),
    ]


def work_scratch(width):
    return [
        pltpu.VMEM((ROWS, width), F32), pltpu.VMEM((ROWS, width), F32),
        pltpu.VMEM((ROWS, width), BF16),
    ]


def add_rows(total, start, extra, count):
    def one(i, carry):
        rows = pl.ds(pl.multiple_of(start + i * 16, 16), 16)
        here = pl.ds(pl.multiple_of(i * 16, 16), 16)
        total[rows, :] = (total[rows, :].astype(F32) + extra[here, :].astype(F32)).astype(BF16)
        return carry

    lax.fori_loop(0, count // 16, one, 0)


def scatter_kernel(count, scale, *refs):
    lefts, back1, kept_all, own = refs[:4], refs[4:8], refs[8:16], refs[16:20]
    small1, tg1, tl1, index_g, index_l, outs_all, gx1, vec_all, xg_ref, xl_ref, gcount, lcount = refs[20:32]
    refs = refs[32:]
    out_qkv, out_proj, out_fc1, out_fc2, out_g, out_l, gin_g, gin_l = refs[:8]
    out_small, out_tg, out_tl = refs[8:19], *refs[19:21]
    refs = refs[21:]
    held = refs[:8]
    sum_a, sum_b, sum_c = refs[8:11]
    in_a1, in_a2, in_a3, in_b1, in_b2, in_b3, in_c1, in_c2, in_c3 = refs[11:20]
    local_sem, swap_sent, swap_came = refs[20:23]
    sent, came = refs[23:32], refs[32:41]
    small_ref, tg_ref, tl_ref, pair_small, pair_tg, pair_tl, pair_gx, gx0, sums, slots_z = refs[41:51]
    extra_sent, extra_came, load_sem, weight_sem = refs[51:55]
    kept, scratch = refs[55:64], refs[64:67]
    depth = count // (SIDE * SIDE)
    width = held[0].shape[1]
    section = lax.axis_index("pipe")
    place = lax.axis_index("dp")
    x = place % SIDE
    y = (place // SIDE) % SIDE
    z = place // (SIDE * SIDE)

    def index(zz, yy, xx):
        return (zz * SIDE + yy) * SIDE + xx

    across_x, across_y = index(z, y, 1 - x), index(z, 1 - y, x)

    barrier = pltpu.get_barrier_semaphore()
    pl.semaphore_signal(barrier, inc=1, device_id={"pipe": 1 - section}, device_id_type=MESH)
    for peer in (across_x, across_y):
        pl.semaphore_signal(barrier, inc=1, device_id={"dp": peer}, device_id_type=MESH)
    for step in range(1, depth):
        peer = index((z + step) % depth, y, x)
        pl.semaphore_signal(barrier, inc=1, device_id={"dp": peer}, device_id_type=MESH)
    pl.semaphore_wait(barrier, 3 + depth - 1)

    extras = ((small1, pair_small), (tg1, pair_tg), (tl1, pair_tl), (gx1, pair_gx))
    GX = 3

    def extra_copy(i):
        source, target = extras[i]
        return remote(source, target, extra_sent.at[i], extra_came.at[i], pipe=1 - section)

    order = (2, 1, 0, 3)

    def mine(i, crop=0):
        return held[i].at[pl.ds(crop * ROWS, ROWS), :]

    def swap_copy(i):
        return remote(back1[i], mine(4 + i, 1), swap_sent.at[i], swap_came.at[i], pipe=1 - section)

    def own_copy(i):
        if i < 4:
            return pltpu.make_async_copy(lefts[i].at[1], mine(i), local_sem.at[i])
        return pltpu.make_async_copy(back1[i - 4], mine(i), local_sem.at[i])

    def given_copy(i):
        return pltpu.make_async_copy(lefts[i].at[2], mine(i, 1), local_sem.at[8 + i])

    def left_copy(i, crop):
        return pltpu.make_async_copy(lefts[i].at[2 * crop], mine(i, crop), local_sem.at[4 * crop + i])

    def load_copy(crop, number):
        return pltpu.make_async_copy(
            kept_all[number - Q].at[2 * crop], kept[number], load_sem.at[number]
        )

    def sum_copy(i):
        return pltpu.make_async_copy(extras[i][0], (small_ref, tg_ref, tl_ref)[i], load_sem.at[i])

    hidden = held[3].shape[1]
    weights = (
        sum_c, sum_a.at[:, pl.ds(hidden, width)], sum_a.at[:, pl.ds(0, hidden)], sum_b,
    )

    def weight_copy(i):
        return pltpu.make_async_copy(own[i], weights[i], weight_sem.at[i])

    extra_copy(GX).start()

    @pl.when(section == 0)
    def _():
        for i in order:
            swap_copy(i).start()
        for i in range(GX):
            extra_copy(i).start()
        load_copy(0, B2).start()
        weight_copy(3).start()
        load_copy(0, DA).start()
        weight_copy(2).start()
        for number in (MI, BR):
            load_copy(0, number).start()
        weight_copy(1).start()
        for number in (V, PR, K, Q):
            load_copy(0, number).start()
        weight_copy(0).start()
        for i in range(4):
            left_copy(i, 0).start()
            left_copy(i, 1).start()

    @pl.when(section != 0)
    def _():
        for i in order:
            own_copy(i).start()
            given_copy(i).start()
            own_copy(4 + i).start()
        for i in range(GX):
            sum_copy(i).start()

    def first_layer(crop):
        def vec(row):
            return vec_all[row:row + 1, :]

        def weight(i):
            if crop == 0:
                weight_copy(i).wait()

        def loaded(*numbers):
            for number in numbers:
                if number != X:
                    load_copy(crop, number).wait()

        def done(unused, *numbers):
            if crop == 0:
                for number in numbers:
                    load_copy(1, number).start()

        if crop == 1:
            extra_copy(GX).wait_recv()
        x_ref = kept[0]
        clear(x_ref)
        for ref, start in ((xg_ref, 0), (xl_ref, LOCAL_ROW)):
            x_ref[start:start + ref.shape[0], :] = ref[:, crop, :]
        backward_steps(
            scale, vec, weight, loaded, done, gx1 if crop == 0 else pair_gx, gx0.at[crop], kept, weights,
            tuple(mine(4 + i, crop) for i in range(4)), (small_ref, tg_ref, tl_ref), scratch,
        )

    @pl.when(section == 0)
    def _():
        clear(small_ref, tg_ref, tl_ref)
        first_layer(0)
        first_layer(1)

    def second_sums():
        for i in range(GX):
            extra_copy(i).wait_recv()
            sum_copy(i).wait()
        small_ref[...] += pair_small[...]
        tg_ref[...] += pair_tg[...]
        tl_ref[...] += pair_tl[...]

    def swapped_outputs():
        def live(count_ref, crop):
            return jnp.where(count_ref[0] > crop, 1.0, 0.0)

        def place(crop, values, grads):
            for out, gin, start, count_ref in ((out_g, gin_g, 0, gcount), (out_l, gin_l, LOCAL_ROW, lcount)):
                rows = slice(start, start + out.shape[0])
                out[:, crop, :] = (values[rows].astype(F32) * live(count_ref, crop)).astype(BF16)
                gin[:, crop, :] = grads[rows]

        @pl.when(section == 0)
        def _():
            place(0, outs_all[0], gx0[0])
            place(1, outs_all[2], gx0[1])

        @pl.when(section != 0)
        def _():
            extra_copy(GX).wait_recv()
            place(0, outs_all[2], pair_gx[...])
            place(1, outs_all[1], gx1[...])

    def fold_back(values, index_ref, entries, grid, cls_lane):
        lanes = index_ref.shape[1]
        total = values[0:grid].reshape(grid * 16, lanes)
        high = total.astype(BF16)
        low = (total - high.astype(F32)).astype(BF16)
        found = dot_cols(jnp.concatenate([high, low], 0), hot(index_ref[0:1, :], entries))
        found = found[:grid * 16] + found[grid * 16:]
        result = found[:16]
        for r in range(1, grid):
            result = result + pltpu.roll(found[16 * r:16 * r + 16], r, 1)
        lane = lax.broadcasted_iota(jnp.int32, (1, lanes), 1)
        entry = lax.broadcasted_iota(jnp.int32, (1, entries), 1)
        cls = (2 * grid - 1) ** 2
        to_patch, to_class = values[grid], values[grid + 1]
        for spot, column in (
            (cls, jnp.sum(jnp.where(lane == cls_lane, 0.0, to_patch), axis=1, keepdims=True)),
            (cls + 1, jnp.sum(to_class, axis=1, keepdims=True)),
            (cls + 2, jnp.sum(jnp.where(lane == cls_lane, to_patch, 0.0), axis=1, keepdims=True)),
        ):
            result = result + jnp.where(entry == spot, column, 0.0)
        return result

    def small_fold():
        sums[0] = jnp.zeros((SMALL_ROWS, width), F32)
        sums[0, 0:16, :] = small_ref[...]
        sums[0, TABLE_ROW:TABLE_ROW + 16, :] = fold_back(tg_ref, index_g, width, GRID_G, 0)
        sums[0, TABLE_ROW_L:TABLE_ROW_L + 16, 0:128] = fold_back(
            tl_ref, index_l, 128, GRID_L, LOCAL_ROW - 128
        )

    def small_start():
        small_x().start()

    def small_x():
        return remote(sums.at[0], sums.at[3], extra_sent.at[5], extra_came.at[5], dp=across_x)

    def small_y():
        return remote(sums.at[1], sums.at[4], extra_sent.at[6], extra_came.at[6], dp=across_y)

    def small_z(step):
        peer = index((z + step) % depth, y, x)
        return remote(
            sums.at[2], slots_z.at[z], extra_sent.at[6 + step], extra_came.at[6 + step], dp=peer
        )

    def small_second():
        small_x().wait_recv()
        sums[1] = sums[0] + sums[3]
        small_y().start()

    def small_third():
        small_y().wait_recv()
        sums[2] = sums[1] + sums[4]
        for step in range(1, depth):
            small_z(step).start()
        slots_z[z] = sums[2]

    def small_end():
        for step in range(1, depth):
            here = slots_z.at[(z + depth - step) % depth]
            peer = index((z + step) % depth, y, x)
            remote(here, here, extra_sent.at[6 + step], extra_came.at[6 + step], dp=peer).wait_recv()
        total = slots_z[0]
        for zz in range(1, depth):
            total = total + slots_z[zz]
        row = 0
        for ref in out_small:
            for b in range(0, ref.shape[1], width):
                ref[:, b:b + width] = total[row:row + 1]
                row += 1
        for ref, start in ((out_tg, TABLE_ROW), (out_tl, TABLE_ROW_L)):
            ref[:, 0, :] = total[start:start + ref.shape[0], 0:ref.shape[2]]

    def operands(*numbers):
        @pl.when(section == 0)
        def _():
            for i in numbers:
                if i < 4:
                    left_copy(i, 0).wait()
                    left_copy(i, 1).wait()

        @pl.when(section != 0)
        def _():
            for i in numbers:
                own_copy(i).wait()
                if i < 4:
                    given_copy(i).wait()
                else:
                    swap_copy(i - 4).wait_recv()

    def when_core(number, *steps):
        @pl.when(section == number)
        def _():
            for step in steps:
                step()

    def product(left, right, total, offset):
        def one(i, carry):
            start = pl.multiple_of(i * BLOCK, BLOCK)
            rows = left[:, pl.ds(start, BLOCK)]
            for b in range(0, right.shape[1], width):
                part = dot_rows(rows, right[:, b:b + width])
                total[pl.ds(start, BLOCK), offset + b:offset + b + width] = part.astype(BF16)
            return carry

        lax.fori_loop(0, left.shape[1] // BLOCK, one, 0)

    def target(k):
        low = jnp.where(k < depth - 1 - z, depth - 1 - k, k - (depth - 1 - z))
        high = jnp.where(k < z, k, depth - 1 - (k - z))
        return jnp.where(z < depth // 2, low, high)

    targets = [target(k) for k in range(depth)]
    ups = [jnp.where(targets[k] > z, 1, 0) for k in range(depth - 1)]
    starts_line = (z == 0) | (z == depth - 1)

    def chunk(total, zz, yy, xx):
        rows = total.shape[0] // count
        return pl.ds(pl.multiple_of(index(zz, yy, xx) * rows, rows), rows)

    def accumulate(total, zz, yy, xx, extra):
        rows = total.shape[0] // count
        add_rows(total, pl.multiple_of(index(zz, yy, xx) * rows, rows), extra, rows)

    def line_copy(total, slots, group, k, c, yy, xx, width_of):
        up = ups[k]
        slot = (targets[k] + up) * width_of + c
        number = k * width_of + c
        source = total.at[chunk(total, targets[k], yy, xx), :]
        peer = index(z + 2 * up - 1, y, x)
        return slot, remote(
            source, slots.at[slot], sent[group].at[number], came[group].at[slot], dp=peer
        )

    def line_receive(total, slots, group, k, slot, yy, xx):
        here = slots.at[slot]
        peer = index(z + 1 - 2 * ups[k], y, x)
        remote(here, here, sent[group].at[0], came[group].at[slot], dp=peer).wait_recv()
        accumulate(total, targets[k], yy, xx, here)

    c_parts = ((1 - y, 1 - x), (y, 1 - x), (1 - y, x), (y, x))
    items_c = 4 * (depth - 1)

    def copy_c(n):
        return line_copy(sum_c, in_c1, 6, n // 4, n % 4, *c_parts[n % 4], 4)

    def line_c(n):
        k, c = n // 4, n % 4
        yy, xx = c_parts[c]

        @pl.when(starts_line)
        def _():
            copy_c(n)[1].wait_send()
            if n + FLIGHT < items_c:
                copy_c(n + FLIGHT)[1].start()

        @pl.when(jnp.logical_not(starts_line))
        def _():
            slot, copy = line_copy(sum_c, in_c1, 6, k, c, yy, xx, 4)
            line_receive(sum_c, in_c1, 6, k, slot, yy, xx)
            copy.start()

    def first_copy(which, i):
        yy_other = i < depth
        zz = targets[i % depth]
        if which == 0:
            where = (zz, 1 - y if yy_other else y, 1 - x)
            total, slots, peer = sum_a, in_a1, across_x
        else:
            where = (zz, 1 - y, 1 - x if yy_other else x)
            total, slots, peer = sum_b, in_b1, across_y
        source = total.at[chunk(total, *where), :]
        group = 0 if which == 0 else 3
        return remote(source, slots.at[i], sent[group].at[i], came[group].at[i], dp=peer)

    def second_copy(which, i):
        where = (targets[i], 1 - y, x) if which == 0 else (targets[i], y, 1 - x)
        total, slots, peer = (sum_a, in_a2, across_y) if which == 0 else (sum_b, in_b2, across_x)
        group = 1 if which == 0 else 4
        source = total.at[chunk(total, *where), :]
        return remote(source, slots.at[i], sent[group].at[i], came[group].at[i], dp=peer)

    def first_receive(which, i):
        first_copy(which, i).wait_recv()
        if i + FLIGHT < 2 * depth:
            first_copy(which, i + FLIGHT).start()
        zz = targets[i % depth]
        if which == 0:
            where = (zz, 1 - y if i < depth else y, x)
            accumulate(sum_a, *where, in_a1.at[i])
        else:
            where = (zz, y, 1 - x if i < depth else x)
            accumulate(sum_b, *where, in_b1.at[i])
        if i < depth:
            second_copy(which, i).start()

    def line_z(which, k):
        total, slots, group = (sum_a, in_a3, 2) if which == 0 else (sum_b, in_b3, 5)
        source = total.at[chunk(total, targets[k], y, x), :]
        peer = index(targets[k], y, x)
        return remote(source, slots.at[z], sent[group].at[k], came[group].at[z], dp=peer)

    def line(which, k):
        total, came_in = (sum_a, in_a2) if which == 0 else (sum_b, in_b2)
        second_copy(which, k).wait_recv()
        accumulate(total, targets[k], y, x, came_in.at[k])
        if k < depth - 1:
            line_z(which, k).start()

    def line_end(total, slots, group, slot_below, slot_above, add):
        @pl.when(z > 0)
        def _():
            here = slots.at[slot_below]
            peer = index(z - 1, y, x)
            remote(here, here, sent[group].at[0], came[group].at[slot_below], dp=peer).wait_recv()
            add(here)

        @pl.when(z < depth - 1)
        def _():
            here = slots.at[slot_above]
            peer = index(z + 1, y, x)
            remote(here, here, sent[group].at[0], came[group].at[slot_above], dp=peer).wait_recv()
            add(here)

    def finish(which):
        total, slots, group = (sum_a, in_a3, 2) if which == 0 else (sum_b, in_b3, 5)
        own = chunk(total, z, y, x)
        if which == 0:
            hidden = out_fc1.shape[1]
            out_fc1[...] = total[own, :hidden].astype(F32)
            out_proj[...] = total[own, hidden:].astype(F32)

            def add(here):
                out_fc1[...] += here[:, :hidden].astype(F32)
                out_proj[...] += here[:, hidden:].astype(F32)
        else:
            out_fc2[...] = total[own, :].astype(F32)

            def add(here):
                out_fc2[...] += here[...].astype(F32)

        for step in range(1, depth):
            source = (z + step) % depth
            here = slots.at[source]
            peer = index(source, y, x)
            remote(here, here, sent[group].at[0], came[group].at[source], dp=peer).wait_recv()
            add(here)

    operands(2, 6, 1, 5)
    product(held[2], held[6], sum_a, 0)
    product(held[1], held[5], sum_a, held[6].shape[1])
    for i in range(FLIGHT):
        first_copy(0, i).start()
    operands(0, 4)
    product(held[0], held[4], sum_c, 0)

    @pl.when(starts_line)
    def _():
        for n in range(min(FLIGHT, items_c)):
            copy_c(n)[1].start()

    operands(3, 7)
    product(held[3], held[7], sum_b, 0)
    for i in range(FLIGHT):
        first_copy(1, i).start()

    when_core(1, second_sums)
    small_fold()
    small_start()
    done_c = 0
    for i in range(2 * depth):
        first_receive(1, i)
        first_receive(0, i)
        while done_c < items_c * (i + 1) // (2 * depth):
            line_c(done_c)
            done_c += 1
        if i == depth - 1:
            small_second()
        if i >= depth and i < 2 * depth - 1:
            line(1, i - depth)
            line(0, i - depth)
        if i == 2 * depth - 2:
            small_third()

    def end_c(c):
        yy, xx = c_parts[c]
        line_end(
            sum_c, in_c1, 6, (z + 1) * 4 + c, z * 4 + c,
            lambda here: accumulate(sum_c, z, yy, xx, here),
        )

    def copy_c2(c):
        yy, xx = c_parts[c]
        source = sum_c.at[chunk(sum_c, z, yy, xx), :]
        return remote(source, in_c2.at[c], sent[7].at[c], came[7].at[c], dp=across_x)

    def copy_c3():
        source = sum_c.at[chunk(sum_c, z, 1 - y, x), :]
        return remote(source, in_c3, sent[8].at[0], came[8].at[0], dp=across_y)

    for c in range(2):
        end_c(c)
        copy_c2(c).start()
    end_c(2)
    end_c(3)
    copy_c2(0).wait_recv()
    accumulate(sum_c, z, 1 - y, x, in_c2.at[0])
    copy_c3().start()
    copy_c2(1).wait_recv()
    accumulate(sum_c, z, y, x, in_c2.at[1])
    swapped_outputs()
    line(1, depth - 1)
    line(0, depth - 1)
    copy_c3().wait_recv()
    out_qkv[...] = sum_c[chunk(sum_c, z, y, x), :].astype(F32) + in_c3[...].astype(F32)
    finish(1)
    finish(0)
    small_end()

    extra_copy(GX).wait_send()

    @pl.when(section == 0)
    def _():
        for i in range(GX):
            extra_copy(i).wait_send()
        for i in order:
            swap_copy(i).wait_send()

    small_x().wait_send()
    small_y().wait_send()
    for step in range(1, depth):
        small_z(step).wait_send()
    for which in range(2):
        for i in range(2 * depth):
            first_copy(which, i).wait_send()
        for i in range(depth):
            second_copy(which, i).wait_send()
        for k in range(depth - 1):
            line_z(which, k).wait_send()
    @pl.when(jnp.logical_not(starts_line))
    def _():
        for n in range(items_c):
            copy_c(n)[1].wait_send()

    copy_c2(0).wait_send()
    copy_c2(1).wait_send()
    copy_c3().wait_send()


def scattered(count, kept, back1, crops, vec, own, counts, tokens, entries):
    lefts = [kept[i] for i in (1, 6, 9, 10)]
    widths = [a.shape[2] for a in lefts] + [back1[i].shape[1] for i in (1, 2, 3, 4)]
    n1, merged, n2, act, gmixed, gbranch, ghidden, gb2 = widths
    heads = kept[5].shape[1]
    scale = (n1 // heads) ** (-0.5)
    depth = count // (SIDE * SIDE)
    rows, rows_b = n1 // count, act // count
    cols_a = ghidden + gbranch
    copies = (2 * depth, depth, depth - 1, 2 * depth, depth, depth - 1, 4 * (depth - 1), 2, 1)
    arrivals = (2 * depth, depth, depth, 2 * depth, depth, depth, 4 * (depth + 1), 2, 1)
    tokens_g, tokens_l = tokens
    return pl.pallas_call(
        functools.partial(scatter_kernel, count, scale),
        out_shape=(
            shape(rows, gmixed, dtype=F32), shape(rows, gbranch, dtype=F32),
            shape(rows, ghidden, dtype=F32), shape(rows_b, gb2, dtype=F32),
            shape(tokens_g, 2, n1), shape(tokens_l, 2, n1), shape(tokens_g, 2, n1), shape(tokens_l, 2, n1),
            *(shape(1, n1, dtype=F32) for _ in range(10)), shape(1, act, dtype=F32),
            shape(heads, 1, entries[0], dtype=F32), shape(heads, 1, entries[1], dtype=F32),
        ),
        in_specs=[OUTSIDE] * 23 + [INSIDE] * 7 + [SCALARS] * 2,
        out_specs=(INSIDE,) * 21,
        scratch_shapes=[pltpu.VMEM((2 * ROWS, w), BF16) for w in widths]
        + [pltpu.VMEM((n1, cols_a), BF16), pltpu.VMEM((act, gb2), BF16), pltpu.VMEM((n1, gmixed), BF16)]
        + [pltpu.VMEM((slots, rows, cols_a), BF16) for slots in (2 * depth, depth, depth)]
        + [pltpu.VMEM((slots, rows_b, gb2), BF16) for slots in (2 * depth, depth, depth)]
        + [pltpu.VMEM((4 * (depth + 1), rows, gmixed), BF16), pltpu.VMEM((2, rows, gmixed), BF16),
           pltpu.VMEM((rows, gmixed), BF16)]
        + [DMA((12,)), DMA((4,)), DMA((4,))]
        + [DMA((c,)) for c in copies] + [DMA((a,)) for a in arrivals]
        + 2 * [
            pltpu.VMEM((16, n1), F32), pltpu.VMEM((16, 16, LANES_G), F32),
            pltpu.VMEM((8, 16, LANES_L), F32),
        ]
        + [
            pltpu.VMEM((ROWS, n1), BF16), pltpu.VMEM((2, ROWS, n1), BF16),
            pltpu.VMEM((5, SMALL_ROWS, n1), F32), pltpu.VMEM((depth, SMALL_ROWS, n1), F32),
            DMA((6 + depth,)), DMA((6 + depth,)), DMA((9,)), DMA((4,)),
        ]
        + kept_scratch(heads, n1, act) + work_scratch(n1),
        compiler_params=pltpu.CompilerParams(
            vmem_limit_bytes=62 * 2**20, collective_id=1, has_side_effects=True
        ),
        name="first_backward_and_scatter",
    )(
        *lefts, *back1[1:5], *(kept[i] for i in (2, 3, 4, 5, 7, 8, 11, 12)), *own, *back1[5:8],
        jnp.asarray(INDEX_G), jnp.asarray(INDEX_L), kept[0], back1[0], vec, *crops, *counts,
    )


def swapped(value):
    return lax.ppermute(value, "pipe", [(0, 1), (1, 0)])


def plain_scattered(kept, back0, back1, counts, tokens, entries):
    section = lax.axis_index("pipe")
    tokens_g, tokens_l = tokens

    def exchange(layer0, layer1):
        keep = jnp.where(section == 0, layer0, layer1)
        send = jnp.where(section == 0, layer1, layer0)
        return keep, swapped(send)

    lefts = [exchange(kept[i][0], kept[i][1]) for i in (1, 6, 9, 10)]
    rights = [exchange(back0[i], back1[i]) for i in (1, 2, 3, 4)]
    shares = [
        lax.psum_scatter(
            dot_rows(jnp.concatenate(a, 0), jnp.concatenate(b, 0)).astype(BF16),
            "dp", scatter_dimension=0, tiled=True,
        ).astype(F32)
        for a, b in zip(lefts, rights)
    ]
    small, tg, tl = (a + b for a, b in (exchange(back0[i], back1[i]) for i in (5, 6, 7)))
    width = small.shape[1]

    def fold(values, index, count):
        flat = jnp.transpose(values, (1, 0, 2)).reshape(values.shape[1], -1)
        high = flat.astype(BF16)
        low = (flat - high.astype(F32)).astype(BF16)
        spot = hot(jnp.asarray(index.reshape(1, -1)), count)
        sums = dot_cols(jnp.concatenate([high, low], 0), spot)
        return sums[: values.shape[1]] + sums[values.shape[1]:]

    small, tg, tl = lax.psum((small, fold(tg, INDEX_G, width), fold(tl, INDEX_L, 128)), "dp")

    def both_crops(keep, came):
        low = jnp.where(section == 0, keep, came)
        high = jnp.where(section == 0, came, keep)
        return (
            jnp.stack([low[:tokens_g], high[:tokens_g]], 1),
            jnp.stack([low[LOCAL_ROW:LOCAL_ROW + tokens_l], high[LOCAL_ROW:LOCAL_ROW + tokens_l]], 1),
        )

    out_g, out_l = both_crops(*exchange(kept[0][0], kept[0][1]))
    crop = jnp.arange(2, dtype=jnp.int32)[None, :, None]
    out_g = jnp.where(crop < counts[0][0], out_g, jnp.zeros_like(out_g))
    out_l = jnp.where(crop < counts[1][0], out_l, jnp.zeros_like(out_l))
    gin_g, gin_l = both_crops(*exchange(back0[0], back1[0]))
    hidden = back0[3].shape[1]
    rows = [small[i:i + 1] for i in range(F1B)]
    rows.append(small[F1B:F1B + hidden // width].reshape(1, hidden))
    heads = kept[5].shape[1]
    tables = (tg[:heads, None, :entries[0]], tl[:heads, None, :entries[1]])
    return (*shares, out_g, out_l, gin_g, gin_l, *rows, *tables)


def finish_kernel(*refs):
    half = len(refs) // 2
    for source, target in zip(refs[:half], refs[half:]):
        target[...] = source[...]


def finished(arrays):
    return pl.pallas_call(
        finish_kernel,
        out_shape=tuple(shape(*a.shape, dtype=a.dtype) for a in arrays),
        in_specs=[INSIDE] * len(arrays),
        out_specs=(INSIDE,) * len(arrays),
        name="results",
    )(*arrays)


def body(
    x_global, x_local, cot_global, cot_local, global_count, local_count,
    w_qkv, w_proj, w_fc1, w_fc2,
    norm1_gain, norm1_shift, q_bias, v_bias, proj_bias, scale_attn,
    norm2_gain, norm2_shift, fc1_bias, fc2_bias, scale_mlp,
    table_global, table_local,
):
    width = x_global.shape[2]
    entries_g, heads = table_global.shape[1:]
    entries_l = table_local.shape[1]
    tokens = (x_global.shape[1], x_local.shape[1])
    own = (w_qkv[0], w_proj[0], w_fc1[0], w_fc2[0])
    vec = (norm1_gain, norm1_shift, q_bias, v_bias, proj_bias, scale_attn, norm2_gain, norm2_shift,
           fc2_bias, scale_mlp, fc1_bias)
    tables = (table_global[0].T, table_local[0].T)
    crops = tuple(jnp.transpose(a, (1, 0, 2)) for a in (x_global, x_local))
    cots = tuple(jnp.transpose(a, (1, 0, 2)) for a in (cot_global, cot_local))
    count = lax.axis_size("dp")
    whole_tiles = count % (2 * SIDE * SIDE) == 0 and width % (16 * count) == 0
    results = forward(*crops, vec, tables, own, not whole_tiles)
    other, kept, vec = results[:4], results[4:17], results[17]
    counts = (global_count, local_count)
    back1 = backward(1, (*cots, *counts), vec, kept, heads, own, other)
    entries = (entries_g, entries_l)
    if whole_tiles:
        results = finished(scattered(count, kept, back1, crops, vec, own, counts, tokens, entries))
    else:
        back0 = backward(0, (back1[0], *crops), vec, kept, heads, own, other)
        results = plain_scattered(kept, back0, back1, counts, tokens, entries)
    shares, crops, small, tables = results[:4], results[4:8], results[8:19], results[19:]
    vectors = [small[i] for i in (N1G, N1S, QB, VB, PB, SA, N2G, N2S, F1B, F2B, SM)]
    return (
        *(jnp.transpose(c, (1, 0, 2))[None] for c in crops),
        *(s[None] for s in shares),
        *vectors,
        *(jnp.transpose(t, (1, 2, 0)) for t in tables),
    )


def solution(mesh):
    three, two = P("pipe", None, None), P("pipe", None)
    rows = P("dp", None, None)
    in_specs = (rows,) * 4 + (P("dp"),) * 2 + (three,) * 4 + (two,) * 11 + (three,) * 2
    crops = P("pipe", "dp", None, None)
    out_specs = (crops,) * 4 + (P("pipe", "dp", None),) * 4 + (two,) * 11 + (three,) * 2
    return jax.shard_map(body, mesh=mesh, in_specs=in_specs, out_specs=out_specs, check_vma=False)
```

```python
import functools
import jax
import jax.numpy as jnp
import numpy as np
from jax import lax
from jax.experimental import pallas as pl
from jax.experimental.pallas import tpu as pltpu
from jax.sharding import PartitionSpec as P

GRID_G = 14
GRID_L = 6
ROWS = 256
LOCAL_ROW = 208
LANES_G = 512
LANES_L = 128
FRONT_L = 51
BLOCK = 256
NEG = -1e30
eps = 1e-06
F32 = jnp.float32
BF16 = jnp.bfloat16
INV_SQRT2 = 0.7071067811865476
INV_SQRT_2PI = 0.3989422804014327
N1G, N1S, QB, VB, PB, SA, N2G, N2S, F2B, SM, F1B = range(11)


def spread_index(grid, rows, lanes, front, cls_lane):
    side = 2 * grid - 1
    entries = side * side
    index = np.full((rows, lanes), -1, np.int32)
    for q in range(grid):
        for a in range(side):
            for k in range(grid):
                index[q, front + a * grid + k] = (side - 1 - a) * side + (q - k + grid - 1)
    index[rows - 2, :] = entries
    index[rows - 2, cls_lane] = entries + 2
    index[rows - 1, :] = entries + 1
    return index


INDEX_G = spread_index(GRID_G, 16, LANES_G, 1, 0)
INDEX_L = spread_index(GRID_L, 8, LANES_L, FRONT_L, LOCAL_ROW - 128)


def dot(a, b):
    return lax.dot_general(a, b, (((1,), (0,)), ((), ())), preferred_element_type=F32)


def dot_cols(a, b):
    return lax.dot_general(a, b, (((1,), (1,)), ((), ())), preferred_element_type=F32)


def dot_rows(a, b):
    return lax.dot_general(a, b, (((0,), (0,)), ((), ())), preferred_element_type=F32)


def normalised(x):
    centered = x - jnp.mean(x, axis=-1, keepdims=True)
    rstd = lax.rsqrt(jnp.mean(centered * centered, axis=-1, keepdims=True) + eps)
    return centered * rstd, rstd


def row_steps(step, body):
    def one(i, carry):
        body(pl.ds(pl.multiple_of(i * step, step), step))
        return carry

    lax.fori_loop(0, ROWS // step, one, 0)


def build_bias(spread_g, spread_l, bias):
    for r in range(GRID_G):
        shifted = pltpu.roll(spread_g, (LANES_G - (GRID_G - 1 - r) * GRID_G) % LANES_G, 1)
        bias[pl.ds(1 + GRID_G * r, GRID_G), :] = shifted[:GRID_G, :ROWS]
    for r in range(GRID_L):
        shifted = pltpu.roll(spread_l, GRID_L * r, 1)
        bias[pl.ds(LOCAL_ROW + 1 + GRID_L * r, GRID_L), pl.ds(128, 128)] = shifted[:GRID_L, :]
    tokens_g = GRID_G * GRID_G + 1
    tokens_l = GRID_L * GRID_L + 1
    top = bias[:LOCAL_ROW, :]
    row = lax.broadcasted_iota(jnp.int32, top.shape, 0)
    col = lax.broadcasted_iota(jnp.int32, top.shape, 1)
    top = jnp.where(col == 0, spread_g[15:16, :ROWS], top)
    top = jnp.where(row == 0, spread_g[14:15, :ROWS], top)
    top = jnp.where(row >= tokens_g, 0.0, top)
    top = jnp.where(col >= tokens_g, NEG, top)
    low = bias[LOCAL_ROW:, 128:]
    row = lax.broadcasted_iota(jnp.int32, low.shape, 0)
    col = lax.broadcasted_iota(jnp.int32, low.shape, 1) - (LOCAL_ROW - 128)
    low = jnp.where(col == 0, spread_l[7:8], low)
    low = jnp.where(row == 0, spread_l[6:7], low)
    low = jnp.where(row >= tokens_l, 0.0, low)
    low = jnp.where((col >= 0) & (col < tokens_l), low, NEG)
    bottom = jnp.concatenate([jnp.full((ROWS - LOCAL_ROW, 128), NEG, F32), low], 1)
    return jnp.concatenate([top, bottom], 0)


MESH = pl.DeviceIdType.MESH
SIDE = 2
FLIGHT = 4
TABLE_ROW, TABLE_ROW_L, SMALL_ROWS = 16, 32, 48
SUM_ROWS = 32


def remote(source, target, sent, came, **device):
    return pltpu.make_async_remote_copy(
        src_ref=source, dst_ref=target, send_sem=sent, recv_sem=came,
        device_id=device, device_id_type=MESH,
    )


def hot(index_row, count):
    number = lax.broadcasted_iota(jnp.int32, (count, index_row.shape[1]), 0)
    return jnp.where(number == index_row, 1.0, 0.0).astype(BF16)


def place_crops(target, global_ref, local_ref, section, live_g=None, live_l=None):
    target[...] = jnp.zeros_like(target)
    for ref, start, live in ((global_ref, 0, live_g), (local_ref, LOCAL_ROW, live_l)):
        rows = jnp.where(section == 0, ref[:, 0, :].astype(F32), ref[:, 1, :].astype(F32))
        if live is not None:
            rows = rows * live
        target[start:start + ref.shape[0], :] = rows.astype(BF16)


def forward_kernel(
    scale, keep_both,
    xg_ref, xl_ref, vec_refs, tg_ref, tl_ref, index_g, index_l, own_qkv, own_proj, own_fc1, own_fc2,
    oth_qkv, oth_proj, oth_fc1, oth_fc2,
    out_all, n1_all, q_all, k_all, v_all, p_all, merged_all, branch_all, middle_all,
    n2_all, act_all, dact_all, branch2_all, small_out,
    w_qkv, w_proj, w_fc1, w_fc2, small_in, small, vec_all, x_in, out_ref, n1_ref, q_ref, k_ref, v_ref, p_ref,
    merged_ref, branch_ref, middle_ref, n2_ref, act_ref, dact_ref, branch2_ref,
    spread_g, spread_l, bias, own_sem, sent, came, keep_sem, store_sem, give_sent, give_came, small_sem,
):
    section = lax.axis_index("pipe")
    partner = 1 - section
    own = (own_qkv, own_proj, own_fc1, own_fc2)
    oth = (oth_qkv, oth_proj, oth_fc1, oth_fc2)
    held = (w_qkv, w_proj, w_fc1, w_fc2)
    width = x_in.shape[1]
    heads = p_ref.shape[1]
    half = SMALL_ROWS

    barrier = pltpu.get_barrier_semaphore()
    pl.semaphore_signal(barrier, inc=1, device_id={"pipe": partner}, device_id_type=MESH)
    for i in range(4):
        pltpu.make_async_copy(own[i], held[i].at[section], own_sem.at[i]).start()
    small_rows = small.at[pl.ds(pl.multiple_of(section * half, half), half), :]
    small_in[...] = jnp.zeros_like(small_in)
    row = 0
    for ref in vec_refs:
        for b in range(0, ref.shape[1], width):
            small_in[row:row + 1, :] = ref[:, b:b + width].astype(F32)
            row += 1
    small_in[TABLE_ROW:TABLE_ROW + heads, 0:tg_ref.shape[1]] = tg_ref[...].astype(F32)
    small_in[TABLE_ROW_L:TABLE_ROW_L + heads, 0:tl_ref.shape[1]] = tl_ref[...].astype(F32)
    pl.semaphore_wait(barrier, 1)
    small_copy = remote(small_in, small_rows, small_sem.at[0], small_sem.at[1], pipe=partner)
    small_copy.start()

    def weight_copy(i):
        return remote(own[i], held[i].at[section], sent.at[i], came.at[i], pipe=partner)

    for i in range(4):
        weight_copy(i).start()
    small_rows[...] = small_in[...]
    place_crops(x_in, xg_ref, xl_ref, section)
    small_copy.wait_recv()
    vec_all[...] = small[...]
    small_out[...] = vec_all[...]
    tables_g = jnp.concatenate(
        [small[TABLE_ROW:TABLE_ROW + 16, :], small[half + TABLE_ROW:half + TABLE_ROW + 16, :]], 0
    )
    tables_l = jnp.concatenate(
        [small[TABLE_ROW_L:TABLE_ROW_L + 16, :128], small[half + TABLE_ROW_L:half + TABLE_ROW_L + 16, :128]], 0
    )
    for tables, index_ref, spread, grid, cls_lane in (
        (tables_g, index_g, spread_g, GRID_G, 0), (tables_l, index_l, spread_l, GRID_L, LOCAL_ROW - 128),
    ):
        span, lanes = tables.shape[1], index_ref.shape[1]
        shifted = [tables] + [pltpu.roll(tables, span - r, 1) for r in range(1, grid)]
        found = dot(jnp.concatenate(shifted, 0).astype(BF16), hot(index_ref[0:1, :], span))
        cls = (2 * grid - 1) ** 2
        lane_all = lax.broadcasted_iota(jnp.int32, (1, lanes), 1)
        to_patch = jnp.where(lane_all == cls_lane, tables[:, cls + 2:cls + 3], tables[:, cls:cls + 1])
        to_class = jnp.broadcast_to(tables[:, cls + 1:cls + 2], to_patch.shape)
        for layer in range(2):
            for r in range(grid):
                spread[layer, :, r, :] = found[32 * r + 16 * layer:32 * r + 16 * layer + 16]
            spread[layer, :, grid, :] = to_patch[16 * layer:16 * layer + 16]
            spread[layer, :, grid + 1, :] = to_class[16 * layer:16 * layer + 16]

    slots = (
        out_ref, n1_ref, q_ref, k_ref, v_ref, p_ref, merged_ref, branch_ref, middle_ref,
        n2_ref, act_ref, dact_ref, branch2_ref,
    )
    results = (
        out_all, n1_all, q_all, k_all, v_all, p_all, merged_all, branch_all, middle_all,
        n2_all, act_all, dact_all, branch2_all,
    )
    OUT, N1, Q, K, V, PR, ME, BR, MI, N2, AC, DA, B2 = range(13)
    GIVEN = (OUT, N1, ME, N2, AC)

    def store_copy(number, layer):
        return pltpu.make_async_copy(
            slots[number].at[layer], results[number].at[layer], store_sem.at[layer, number]
        )

    def give_copy(number, layer):
        spot = number if layer == 0 else 13 + GIVEN.index(number)
        return remote(
            slots[number].at[layer], results[number].at[2], give_sent.at[spot], give_came.at[spot],
            pipe=partner,
        )

    def store(layer, *numbers):
        for number in numbers:
            store_copy(number, layer).start()
            if layer == 0 or number in GIVEN:

                @pl.when(section != layer)
                def _():
                    give_copy(number, layer).start()

    def stored(layer, *numbers):
        for number in numbers:
            store_copy(number, layer).wait()
            if layer == 0 or number in GIVEN:

                @pl.when(section != layer)
                def _():
                    give_copy(number, layer).wait_send()

    def weight(i, layer):
        @pl.when(section == layer)
        def _():
            pltpu.make_async_copy(own[i], held[i].at[section], own_sem.at[i]).wait()

        @pl.when(section != layer)
        def _():
            here = held[i].at[partner]
            remote(here, here, sent.at[i], came.at[i], pipe=partner).wait_recv()
            if layer == 1 or keep_both:
                pltpu.make_async_copy(here, oth[i], keep_sem.at[i]).start()

    lane = lax.broadcasted_iota(jnp.int32, (1, 128), 1)
    for layer in range(2):
        entering = x_in if layer == 0 else slots[OUT].at[0]
        (
            out_ref, n1_ref, q_ref, k_ref, v_ref, p_ref, merged_ref, branch_ref, middle_ref,
            n2_ref, act_ref, dact_ref, branch2_ref,
        ) = (slot.at[layer] for slot in slots)
        base = layer * half

        def vec(row):
            return vec_all[base + row:base + row + 1, :]

        def norm1(rows):
            xhat, _ = normalised(entering[rows, :].astype(F32))
            n1_ref[rows, :] = (xhat * vec(N1G) + vec(N1S)).astype(BF16)

        row_steps(128, norm1)
        store(layer, N1)
        weight(0, layer)
        n1 = n1_ref[...]
        for b in range(0, width, BLOCK):
            cols = slice(b, b + BLOCK)
            mixed = dot(n1, w_qkv[layer, :, b:b + BLOCK]) + vec(QB)[:, cols]
            q_ref[:, cols] = (mixed * scale).astype(BF16)
            k_ref[:, cols] = dot(n1, w_qkv[layer, :, width + b:width + b + BLOCK]).astype(BF16)
            mixed = dot(n1, w_qkv[layer, :, 2 * width + b:2 * width + b + BLOCK]) + vec(VB)[:, cols]
            v_ref[:, cols] = mixed.astype(BF16)
        store(layer, Q, K, V)
        for pair in range(heads // 2):
            cols = slice(pair * 128, pair * 128 + 128)
            q, k, v = q_ref[:, cols], k_ref[:, cols], v_ref[:, cols]
            result = None
            for part in range(2):
                head = 2 * pair + part
                mine = (lane < 64) if part == 0 else (lane >= 64)
                scores = dot_cols(q, jnp.where(mine, k, jnp.zeros_like(k))) + build_bias(
                    spread_g[layer, head], spread_l[layer, head], bias.at[head % 2]
                )
                expo = jnp.exp(scores - jnp.max(scores, axis=-1, keepdims=True))
                probs = expo * (1.0 / jnp.sum(expo, axis=-1, keepdims=True))
                low = probs.astype(BF16)
                p_ref[head] = low
                piece = dot(low, jnp.where(mine, v, jnp.zeros_like(v)))
                result = piece if result is None else result + piece
            merged_ref[:, cols] = result.astype(BF16)
        store(layer, PR, ME)
        weight(1, layer)
        merged = merged_ref[...]
        for b in range(0, width, BLOCK):
            cols = slice(b, b + BLOCK)
            branch = dot(merged, w_proj[layer, :, cols]) + vec(PB)[:, cols]
            branch_ref[:, cols] = branch
            middle_ref[:, cols] = entering[:, cols].astype(F32) + vec(SA)[:, cols] * branch
        store(layer, BR, MI)

        def norm2(rows):
            xhat, _ = normalised(middle_ref[rows, :])
            n2_ref[rows, :] = (xhat * vec(N2G) + vec(N2S)).astype(BF16)

        row_steps(128, norm2)
        store(layer, N2)
        weight(2, layer)
        n2 = n2_ref[...]
        for b in range(0, w_fc1.shape[2], BLOCK):
            cols = slice(b, b + BLOCK)
            part = b // width
            hidden = dot(n2, w_fc1[layer, :, cols]) + vec(F1B + part)[:, b - part * width:b - part * width + BLOCK]
            cdf = 0.5 + 0.5 * lax.erf(hidden * INV_SQRT2)
            act_ref[:, cols] = (hidden * cdf).astype(BF16)
            slope = cdf + hidden * (INV_SQRT_2PI * jnp.exp(-0.5 * hidden * hidden))
            dact_ref[:, cols] = slope.astype(BF16)
        store(layer, AC, DA)
        weight(3, layer)
        for b in range(0, width, BLOCK):
            cols = slice(b, b + BLOCK)
            branch2 = dot(act_ref[...], w_fc2[layer, :, cols]) + vec(F2B)[:, cols]
            branch2_ref[:, cols] = branch2
            out_ref[:, cols] = (middle_ref[:, cols] + vec(SM)[:, cols] * branch2).astype(BF16)
        store(layer, B2, OUT)
    stored(0, *range(13))
    stored(1, *range(13))
    for i in range(4):
        weight_copy(i).wait_send()
    small_copy.wait_send()

    def weights_kept():
        for i in range(4):
            pltpu.make_async_copy(held[i].at[partner], oth[i], keep_sem.at[i]).wait()

    @pl.when(section == 0)
    def _():
        weights_kept()
        for number in range(13):
            give_copy(number, 0).wait_recv()

    @pl.when(section != 0)
    def _():
        if keep_both:
            weights_kept()
        for number in GIVEN:
            give_copy(number, 1).wait_recv()


X, Q, K, V, PR, BR, MI, DA, B2 = range(9)


def clear(*refs):
    for ref in refs:
        ref[...] = jnp.zeros_like(ref)


def backward_steps(
    scale, vec, weight, loaded, done, g_ref, gx_ref, kept, weights, grads, sums, scratch,
):
    x_ref, q_ref, k_ref, v_ref, p_ref, branch_ref, middle_ref, dact_ref, branch2_ref = kept
    w_qkv, w_proj, w_fc1, w_fc2 = weights
    gmixed_ref, gbranch_ref, ghidden_ref, gb2_ref = grads
    small_ref, tg_ref, tl_ref = sums
    gmid, gnorm, gmerged = scratch
    width = g_ref.shape[1]
    heads = p_ref.shape[0]

    def add_small(row, values):
        small_ref[row:row + 1, :] += jnp.sum(values, axis=0, keepdims=True)

    loaded(B2)

    def scaled(rows):
        grad = g_ref[rows, :].astype(F32)
        low = (vec(SM) * grad).astype(BF16)
        gb2_ref[rows, :] = low
        add_small(SM, grad * branch2_ref[rows, :])
        add_small(F2B, low.astype(F32))

    row_steps(128, scaled)
    done(3, B2)
    weight(3)
    loaded(DA)
    gb2 = gb2_ref[...]
    for b in range(0, w_fc1.shape[1], BLOCK):
        cols = slice(b, b + BLOCK)
        part = b // width
        ghidden = (dot_cols(gb2, w_fc2[cols, :]) * dact_ref[:, cols]).astype(BF16)
        ghidden_ref[:, cols] = ghidden
        small_ref[F1B + part:F1B + part + 1, b - part * width:b - part * width + BLOCK] += jnp.sum(
            ghidden.astype(F32), axis=0, keepdims=True
        )
    done(2, DA)
    weight(2)
    for b in range(0, width, BLOCK):
        gnorm[:, b:b + BLOCK] = dot_cols(ghidden_ref[...], w_fc1[b:b + BLOCK, :])

    def norm_back(values, grad, gain):
        xhat, rstd = normalised(values)
        scaled_grad = grad * gain
        mean1 = jnp.mean(scaled_grad, axis=-1, keepdims=True)
        mean2 = jnp.mean(scaled_grad * xhat, axis=-1, keepdims=True)
        return xhat, rstd * (scaled_grad - mean1 - xhat * mean2)

    loaded(MI, BR)

    def norm2(rows):
        grad = gnorm[rows, :]
        xhat, through = norm_back(middle_ref[rows, :], grad, vec(N2G))
        grad_middle = g_ref[rows, :].astype(F32) + through
        gmid[rows, :] = grad_middle
        add_small(N2G, grad * xhat)
        add_small(N2S, grad)
        add_small(SA, grad_middle * branch_ref[rows, :])
        low = (vec(SA) * grad_middle).astype(BF16)
        gbranch_ref[rows, :] = low
        add_small(PB, low.astype(F32))

    row_steps(128, norm2)
    done(1, MI, BR)
    weight(1)
    for b in range(0, width, BLOCK):
        gmerged[:, b:b + BLOCK] = dot_cols(gbranch_ref[...], w_proj[b:b + BLOCK, :]).astype(BF16)
    lane = lax.broadcasted_iota(jnp.int32, (1, 128), 1)
    loaded(V, PR, K, Q)
    lane_all = lax.broadcasted_iota(jnp.int32, (1, ROWS), 1)
    for pair in range(heads // 2):
        cols = slice(pair * 128, pair * 128 + 128)
        q, k, v, gm = q_ref[:, cols], k_ref[:, cols], v_ref[:, cols], gmerged[:, cols]
        gq = gk = gv = 0.0
        for half in range(2):
            head = 2 * pair + half
            mine = (lane < 64) if half == 0 else (lane >= 64)

            def only(values):
                return jnp.where(mine, values, jnp.zeros_like(values))

            low = p_ref[head]
            probs = low.astype(F32)
            grad_probs = dot_cols(gm, only(v))
            total = jnp.sum(probs * grad_probs, axis=-1, keepdims=True)
            gscores = (probs * (grad_probs - total)).astype(BF16)
            gv += dot_rows(low, only(gm))
            gq += dot(gscores, only(k))
            gk += dot_rows(gscores, only(q))
            wide = gscores.astype(F32)
            gs = gnorm.at[:, pl.ds(ROWS * (head % 2), ROWS)]
            gs[...] = jnp.where((lane_all == 0) | (lane_all == LOCAL_ROW), 0.0, wide)
            acc = jnp.zeros((GRID_G, LANES_G), F32)
            for r in range(GRID_G):
                block = gs[pl.ds(1 + GRID_G * r, GRID_G), :]
                block = jnp.concatenate([block, jnp.zeros_like(block)], 1)
                acc += pltpu.roll(block, (GRID_G - 1 - r) * GRID_G, 1)
            first_row = wide[0:1, :]
            to_class = jnp.sum(wide[:LOCAL_ROW, :], axis=0, keepdims=True) - first_row
            to_class = jnp.where(lane_all == 0, to_class, 0.0)
            blank = jnp.zeros((1, LANES_G - ROWS), F32)
            tg_ref[0:GRID_G, head, :] += acc
            tg_ref[14, head:head + 1, :] += jnp.concatenate([first_row, blank], 1)
            tg_ref[15, head:head + 1, :] += jnp.concatenate([to_class, blank], 1)
            acc = jnp.zeros((GRID_L, LANES_L), F32)
            for r in range(GRID_L):
                block = gs[pl.ds(LOCAL_ROW + 1 + GRID_L * r, GRID_L), pl.ds(128, 128)]
                acc += pltpu.roll(block, (LANES_L - GRID_L * r) % LANES_L, 1)
            first_row = wide[LOCAL_ROW:LOCAL_ROW + 1, 128:]
            to_class = jnp.sum(wide[LOCAL_ROW:, 128:], axis=0, keepdims=True) - first_row
            to_class = jnp.where(lane == LOCAL_ROW - 128, to_class, 0.0)
            tl_ref[0:GRID_L, head, :] += acc
            tl_ref[6, head:head + 1, :] += first_row
            tl_ref[7, head:head + 1, :] += to_class
        gmixed_ref[:, cols] = gq.astype(BF16) * jnp.asarray(scale, BF16)
        gmixed_ref[:, slice(width + cols.start, width + cols.stop)] = gk.astype(BF16)
        gmixed_ref[:, slice(2 * width + cols.start, 2 * width + cols.stop)] = gv.astype(BF16)

    def biases(rows):
        add_small(QB, gmixed_ref[rows, :width].astype(F32))
        add_small(VB, gmixed_ref[rows, 2 * width:].astype(F32))

    done(0, V, PR, K, Q)
    row_steps(128, biases)
    weight(0)
    loaded(X)
    for b in range(0, width, BLOCK):
        gnorm[:, b:b + BLOCK] = dot_cols(gmixed_ref[...], w_qkv[b:b + BLOCK, :])

    def norm1(rows):
        grad = gnorm[rows, :]
        xhat, through = norm_back(x_ref[rows, :].astype(F32), grad, vec(N1G))
        add_small(N1G, grad * xhat)
        add_small(N1S, grad)
        gx_ref[rows, :] = (gmid[rows, :] + through).astype(BF16)

    row_steps(128, norm1)


def backward_kernel(
    layer, scale, given, vec_all,
    x_all, q_all, k_all, v_all, p_all, branch_all, middle_all, dact_all, branch2_all,
    own_qkv, own_proj, own_fc1, own_fc2, oth_qkv, oth_proj, oth_fc1, oth_fc2,
    gx_ref, gmixed_out, gbranch_out, ghidden_out, gb2_out, small_ref, tg_ref, tl_ref,
    g_ref, x_ref, q_ref, k_ref, v_ref, p_ref, branch_ref, middle_ref, dact_ref, branch2_ref,
    w_qkv, w_proj, w_fc1, w_fc2, gmixed_ref, gbranch_ref, ghidden_ref, gb2_ref,
    gmid, gnorm, gmerged, load_sem, weight_sem, store_sem,
):
    own = (own_qkv, own_proj, own_fc1, own_fc2)
    oth = (oth_qkv, oth_proj, oth_fc1, oth_fc2)
    section = lax.axis_index("pipe")
    held = (w_qkv, w_proj, w_fc1, w_fc2)
    kept = (x_ref, q_ref, k_ref, v_ref, p_ref, branch_ref, middle_ref, dact_ref, branch2_ref)
    sources = (x_all, q_all, k_all, v_all, p_all, branch_all, middle_all, dact_all, branch2_all)
    grads = (gmixed_ref, gbranch_ref, ghidden_ref, gb2_ref)
    targets = (gmixed_out, gbranch_out, ghidden_out, gb2_out)

    def load_copy(number):
        source = sources[number].at[0 if number == X else layer]
        return pltpu.make_async_copy(source, kept[number], load_sem.at[number])

    def load_weight(i):
        @pl.when(section == layer)
        def _():
            pltpu.make_async_copy(own[i], held[i], weight_sem.at[i]).start()

        @pl.when(section != layer)
        def _():
            pltpu.make_async_copy(oth[i], held[i], weight_sem.at[i]).start()

    def weight(i):
        pltpu.make_async_copy(own[i], held[i], weight_sem.at[i]).wait()

    def loaded(*numbers):
        for number in numbers:
            if layer == 1 or number != X:
                load_copy(number).wait()

    def store_copy(number):
        return pltpu.make_async_copy(grads[number], targets[number], store_sem.at[number])

    def done(number, *unused):
        store_copy(number).start()

    def vec(row):
        return vec_all[layer * SMALL_ROWS + row:layer * SMALL_ROWS + row + 1, :]

    load_copy(B2).start()
    load_weight(3)
    load_copy(DA).start()
    load_weight(2)
    for number in (MI, BR):
        load_copy(number).start()
    load_weight(1)
    for number in (V, PR, K, Q):
        load_copy(number).start()
    load_weight(0)
    clear(small_ref, tg_ref, tl_ref)
    if layer == 1:
        cg_ref, cl_ref, gcount, lcount = given
        load_copy(X).start()
        live_g = jnp.where(gcount[0] > section, 1.0, 0.0)
        live_l = jnp.where(lcount[0] > section, 1.0, 0.0)
        place_crops(g_ref, cg_ref, cl_ref, section, live_g, live_l)
    else:
        g_ref, xg_ref, xl_ref = given
        place_crops(x_ref, xg_ref, xl_ref, section)
    backward_steps(
        scale, vec, weight, loaded, done, g_ref, gx_ref, kept, held, grads,
        (small_ref, tg_ref, tl_ref), (gmid, gnorm, gmerged),
    )
    for number in range(4):
        store_copy(number).wait()


def shape(*dims, dtype=BF16):
    return jax.ShapeDtypeStruct(dims, dtype)


INSIDE = pl.BlockSpec(memory_space=pltpu.VMEM)
OUTSIDE = pl.BlockSpec(memory_space=pl.ANY)
SCALARS = pl.BlockSpec(memory_space=pltpu.SMEM)
DMA = pltpu.SemaphoreType.DMA


def forward(x_global, x_local, vec, tables, own, keep_both):
    width = x_global.shape[2]
    heads = tables[0].shape[0]
    hidden = own[2].shape[1]
    scale = (width // heads) ** (-0.5)
    kept = (
        ((ROWS, width), BF16), ((ROWS, width), BF16), ((ROWS, width), BF16), ((ROWS, width), BF16),
        ((ROWS, width), BF16), ((heads, ROWS, ROWS), BF16), ((ROWS, width), BF16),
        ((ROWS, width), F32), ((ROWS, width), F32), ((ROWS, width), BF16),
        ((ROWS, hidden), BF16), ((ROWS, hidden), BF16), ((ROWS, width), F32),
    )
    scratch = [pltpu.VMEM((2, *w.shape), BF16) for w in own]
    scratch += [pltpu.VMEM((SMALL_ROWS, width), F32)] + [pltpu.VMEM((2 * SMALL_ROWS, width), F32)] * 2
    scratch += [pltpu.VMEM((ROWS, width), BF16)]
    scratch += [pltpu.VMEM((2, *dims), kind) for dims, kind in kept]
    scratch += [
        pltpu.VMEM((2, 16, 16, LANES_G), F32), pltpu.VMEM((2, 16, 8, LANES_L), F32),
        pltpu.VMEM((2, ROWS, ROWS), F32),
        DMA((4,)), DMA((4,)), DMA((4,)), DMA((4,)), DMA((2, 13)), DMA((18,)), DMA((18,)), DMA((2,)),
    ]

    def kernel(xg, xl, *refs):
        count = len(vec)
        forward_kernel(scale, keep_both, xg, xl, refs[:count], *refs[count:])

    return pl.pallas_call(
        kernel,
        out_shape=tuple(shape(*w.shape) for w in own)
        + tuple(shape(3, *dims, dtype=kind) for dims, kind in kept)
        + (shape(2 * SMALL_ROWS, width, dtype=F32),),
        in_specs=[INSIDE] * (6 + len(vec)) + [OUTSIDE] * 4,
        out_specs=(OUTSIDE,) * 17 + (INSIDE,),
        scratch_shapes=scratch,
        compiler_params=pltpu.CompilerParams(
            vmem_limit_bytes=60 * 2**20, collective_id=2, has_side_effects=True
        ),
        name="forward_layers",
    )(x_global, x_local, *vec, *tables, jnp.asarray(INDEX_G), jnp.asarray(INDEX_L), *own)


def backward(layer, given, vec, kept, heads, own, other):
    width = vec.shape[1]
    hidden = own[2].shape[1]
    scale = (width // heads) ** (-0.5)
    first, n1, q, k, v, probs, merged, branch, middle, n2, act, dact, branch2 = kept
    count = len(given)

    def kernel(*refs):
        backward_kernel(layer, scale, refs[:count], *refs[count:])

    return pl.pallas_call(
        kernel,
        out_shape=(
            shape(ROWS, width), shape(ROWS, 3 * width), shape(ROWS, width), shape(ROWS, hidden),
            shape(ROWS, width), shape(16, width, dtype=F32),
            shape(16, 16, LANES_G, dtype=F32), shape(8, 16, LANES_L, dtype=F32),
        ),
        in_specs=[SCALARS if g.ndim == 1 else INSIDE for g in given] + [INSIDE] + [OUTSIDE] * 17,
        out_specs=(INSIDE,) + (OUTSIDE,) * 4 + (INSIDE,) * 3,
        scratch_shapes=[pltpu.VMEM((ROWS, width), BF16)] + kept_scratch(heads, width, hidden)
        + [pltpu.VMEM(w.shape, BF16) for w in own]
        + [pltpu.VMEM((ROWS, c), BF16) for c in (3 * width, width, hidden, width)]
        + work_scratch(width) + [DMA((9,)), DMA((4,)), DMA((4,))],
        compiler_params=pltpu.CompilerParams(vmem_limit_bytes=60 * 2**20),
        name="layer_backward",
    )(*given, vec, first, q, k, v, probs, branch, middle, dact, branch2, *own, *other)


def kept_scratch(heads, width, hidden):
    return [pltpu.VMEM((ROWS, width), BF16) for _ in range(4)] + [
        pltpu.VMEM((heads, ROWS, ROWS), BF16), pltpu.VMEM((ROWS, width), F32),
        pltpu.VMEM((ROWS, width), F32), pltpu.VMEM((ROWS, hidden), BF16), pltpu.VMEM((ROWS, width), F32),
    ]


def work_scratch(width):
    return [
        pltpu.VMEM((ROWS, width), F32), pltpu.VMEM((ROWS, width), F32),
        pltpu.VMEM((ROWS, width), BF16),
    ]


def add_rows(total, start, extra, count):
    def one(i, carry):
        rows = pl.ds(pl.multiple_of(start + i * 16, 16), 16)
        here = pl.ds(pl.multiple_of(i * 16, 16), 16)
        total[rows, :] = (total[rows, :].astype(F32) + extra[here, :].astype(F32)).astype(BF16)
        return carry

    lax.fori_loop(0, count // 16, one, 0)


def scatter_kernel(count, scale, *refs):
    lefts, back1, kept_all, own = refs[:4], refs[4:8], refs[8:16], refs[16:20]
    small1, tg1, tl1, index_g, index_l, outs_all, gx1, vec_all, xg_ref, xl_ref, gcount, lcount = refs[20:32]
    refs = refs[32:]
    out_qkv, out_proj, out_fc1, out_fc2, out_g, out_l, gin_g, gin_l = refs[:8]
    out_small, out_tg, out_tl = refs[8:19], *refs[19:21]
    refs = refs[21:]
    held = refs[:8]
    sum_a, sum_b, sum_c = refs[8:11]
    in_a1, in_a2, in_a3, in_b1, in_b2, in_b3, in_c1, in_c2, in_c3 = refs[11:20]
    local_sem, swap_sent, swap_came = refs[20:23]
    sent, came = refs[23:32], refs[32:41]
    small_ref, tg_ref, tl_ref, pair_small, pair_tg, pair_tl, pair_gx, gx0, sums = refs[41:50]
    extra_sent, extra_came, load_sem, weight_sem = refs[50:54]
    kept, scratch = refs[54:63], refs[63:66]
    depth = count // (SIDE * SIDE)
    width = held[0].shape[1]
    section = lax.axis_index("pipe")
    place = lax.axis_index("dp")
    x = place % SIDE
    y = (place // SIDE) % SIDE
    z = place // (SIDE * SIDE)

    def index(zz, yy, xx):
        return (zz * SIDE + yy) * SIDE + xx

    across_x, across_y = index(z, y, 1 - x), index(z, 1 - y, x)

    barrier = pltpu.get_barrier_semaphore()
    pl.semaphore_signal(barrier, inc=1, device_id={"pipe": 1 - section}, device_id_type=MESH)
    for peer in (across_x, across_y):
        pl.semaphore_signal(barrier, inc=1, device_id={"dp": peer}, device_id_type=MESH)
    for step in range(1, depth):
        peer = index((z + step) % depth, y, x)
        pl.semaphore_signal(barrier, inc=1, device_id={"dp": peer}, device_id_type=MESH)
    pl.semaphore_wait(barrier, 3 + depth - 1)

    extras = ((small1, pair_small), (tg1, pair_tg), (tl1, pair_tl), (gx1, pair_gx))
    GX = 3

    def extra_copy(i):
        source, target = extras[i]
        return remote(source, target, extra_sent.at[i], extra_came.at[i], pipe=1 - section)

    order = (2, 1, 0, 3)

    def mine(i, crop=0):
        return held[i].at[pl.ds(crop * ROWS, ROWS), :]

    def swap_copy(i):
        return remote(back1[i], mine(4 + i, 1), swap_sent.at[i], swap_came.at[i], pipe=1 - section)

    def own_copy(i):
        if i < 4:
            return pltpu.make_async_copy(lefts[i].at[1], mine(i), local_sem.at[i])
        return pltpu.make_async_copy(back1[i - 4], mine(i), local_sem.at[i])

    def given_copy(i):
        return pltpu.make_async_copy(lefts[i].at[2], mine(i, 1), local_sem.at[8 + i])

    def left_copy(i, crop):
        return pltpu.make_async_copy(lefts[i].at[2 * crop], mine(i, crop), local_sem.at[4 * crop + i])

    def load_copy(crop, number):
        return pltpu.make_async_copy(
            kept_all[number - Q].at[2 * crop], kept[number], load_sem.at[number]
        )

    def sum_copy(i):
        return pltpu.make_async_copy(extras[i][0], (small_ref, tg_ref, tl_ref)[i], load_sem.at[i])

    hidden = held[3].shape[1]
    weights = (
        sum_c, sum_a.at[:, pl.ds(hidden, width)], sum_a.at[:, pl.ds(0, hidden)], sum_b,
    )

    def weight_copy(i):
        return pltpu.make_async_copy(own[i], weights[i], weight_sem.at[i])

    extra_copy(GX).start()

    @pl.when(section == 0)
    def _():
        for i in order:
            swap_copy(i).start()
        for i in range(GX):
            extra_copy(i).start()
        load_copy(0, B2).start()
        weight_copy(3).start()
        load_copy(0, DA).start()
        weight_copy(2).start()
        for number in (MI, BR):
            load_copy(0, number).start()
        weight_copy(1).start()
        for number in (V, PR, K, Q):
            load_copy(0, number).start()
        weight_copy(0).start()
        for i in range(4):
            left_copy(i, 0).start()
            left_copy(i, 1).start()

    @pl.when(section != 0)
    def _():
        for i in order:
            own_copy(i).start()
            given_copy(i).start()
            own_copy(4 + i).start()
        for i in range(GX):
            sum_copy(i).start()

    def first_layer(crop):
        def vec(row):
            return vec_all[row:row + 1, :]

        def weight(i):
            if crop == 0:
                weight_copy(i).wait()

        def loaded(*numbers):
            for number in numbers:
                if number != X:
                    load_copy(crop, number).wait()

        def done(unused, *numbers):
            if crop == 0:
                for number in numbers:
                    load_copy(1, number).start()

        if crop == 1:
            extra_copy(GX).wait_recv()
        x_ref = kept[0]
        clear(x_ref)
        for ref, start in ((xg_ref, 0), (xl_ref, LOCAL_ROW)):
            x_ref[start:start + ref.shape[0], :] = ref[:, crop, :]
        backward_steps(
            scale, vec, weight, loaded, done, gx1 if crop == 0 else pair_gx, gx0.at[crop], kept, weights,
            tuple(mine(4 + i, crop) for i in range(4)), (small_ref, tg_ref, tl_ref), scratch,
        )

    @pl.when(section == 0)
    def _():
        clear(small_ref, tg_ref, tl_ref)
        first_layer(0)
        first_layer(1)

    def second_sums():
        for i in range(GX):
            extra_copy(i).wait_recv()
            sum_copy(i).wait()
        small_ref[...] += pair_small[...]
        tg_ref[...] += pair_tg[...]
        tl_ref[...] += pair_tl[...]

    def swapped_outputs():
        def live(count_ref, crop):
            return jnp.where(count_ref[0] > crop, 1.0, 0.0)

        def place(crop, values, grads):
            for out, gin, start, count_ref in ((out_g, gin_g, 0, gcount), (out_l, gin_l, LOCAL_ROW, lcount)):
                rows = slice(start, start + out.shape[0])
                out[:, crop, :] = (values[rows].astype(F32) * live(count_ref, crop)).astype(BF16)
                gin[:, crop, :] = grads[rows]

        @pl.when(section == 0)
        def _():
            place(0, outs_all[0], gx0[0])
            place(1, outs_all[2], gx0[1])

        @pl.when(section != 0)
        def _():
            extra_copy(GX).wait_recv()
            place(0, outs_all[2], pair_gx[...])
            place(1, outs_all[1], gx1[...])

    def fold_back(values, index_ref, entries, grid, cls_lane):
        lanes = index_ref.shape[1]
        total = values[0:grid].reshape(grid * 16, lanes)
        high = total.astype(BF16)
        low = (total - high.astype(F32)).astype(BF16)
        found = dot_cols(jnp.concatenate([high, low], 0), hot(index_ref[0:1, :], entries))
        found = found[:grid * 16] + found[grid * 16:]
        result = found[:16]
        for r in range(1, grid):
            result = result + pltpu.roll(found[16 * r:16 * r + 16], r, 1)
        lane = lax.broadcasted_iota(jnp.int32, (1, lanes), 1)
        entry = lax.broadcasted_iota(jnp.int32, (1, entries), 1)
        cls = (2 * grid - 1) ** 2
        to_patch, to_class = values[grid], values[grid + 1]
        for spot, column in (
            (cls, jnp.sum(jnp.where(lane == cls_lane, 0.0, to_patch), axis=1, keepdims=True)),
            (cls + 1, jnp.sum(to_class, axis=1, keepdims=True)),
            (cls + 2, jnp.sum(jnp.where(lane == cls_lane, to_patch, 0.0), axis=1, keepdims=True)),
        ):
            result = result + jnp.where(entry == spot, column, 0.0)
        return result

    levels = (depth - 1).bit_length()
    hops = [across_x, across_y]
    for level in range(levels):
        step = 1 << level
        hops.append(index(z + step * (1 - 2 * ((z // step) % 2)), y, x))
    used = max(ref.shape[1] for ref in out_small) // width + len(out_small) - 1
    per_row = width // 128

    def small_fold():
        sums[0] = jnp.zeros((SUM_ROWS, width), F32)
        sums[0, 0:used, :] = small_ref[0:used, :]
        sums[0, TABLE_ROW:TABLE_ROW + 16, :] = fold_back(tg_ref, index_g, width, GRID_G, 0)
        local = fold_back(tl_ref, index_l, 128, GRID_L, LOCAL_ROW - 128)
        for head in range(out_tl.shape[0]):
            row, column = used + head // per_row, head % per_row * 128
            sums[0, row:row + 1, column:column + 128] = local[head:head + 1]

    def small_hop(stage):
        return remote(
            sums.at[stage], sums.at[len(hops) + 1 + stage],
            extra_sent.at[4 + stage], extra_came.at[4 + stage], dp=hops[stage],
        )

    def small_start():
        small_hop(0).start()

    def small_step(stage):
        small_hop(stage).wait_recv()
        sums[stage + 1] = sums[stage] + sums[len(hops) + 1 + stage]
        if stage + 1 < len(hops):
            small_hop(stage + 1).start()

    def small_end():
        total = sums[len(hops)]
        row = 0
        for ref in out_small:
            for b in range(0, ref.shape[1], width):
                ref[:, b:b + width] = total[row:row + 1]
                row += 1
        out_tg[:, 0, :] = total[TABLE_ROW:TABLE_ROW + out_tg.shape[0], 0:out_tg.shape[2]]
        for head in range(out_tl.shape[0]):
            row, column = used + head // per_row, head % per_row * 128
            out_tl[head] = total[row:row + 1, column:column + out_tl.shape[2]]

    def operands(*numbers):
        @pl.when(section == 0)
        def _():
            for i in numbers:
                if i < 4:
                    left_copy(i, 0).wait()
                    left_copy(i, 1).wait()

        @pl.when(section != 0)
        def _():
            for i in numbers:
                own_copy(i).wait()
                if i < 4:
                    given_copy(i).wait()
                else:
                    swap_copy(i - 4).wait_recv()

    def when_core(number, *steps):
        @pl.when(section == number)
        def _():
            for step in steps:
                step()

    def product(left, right, total, offset):
        def one(i, carry):
            start = pl.multiple_of(i * BLOCK, BLOCK)
            rows = left[:, pl.ds(start, BLOCK)].T
            for b in range(0, right.shape[1], width):
                part = dot(rows, right[:, b:b + width])
                total[pl.ds(start, BLOCK), offset + b:offset + b + width] = part.astype(BF16)
            return carry

        lax.fori_loop(0, left.shape[1] // BLOCK, one, 0)

    def target(k):
        low = jnp.where(k < depth - 1 - z, depth - 1 - k, k - (depth - 1 - z))
        high = jnp.where(k < z, k, depth - 1 - (k - z))
        return jnp.where(z < depth // 2, low, high)

    targets = [target(k) for k in range(depth)]
    ups = [jnp.where(targets[k] > z, 1, 0) for k in range(depth - 1)]
    starts_line = (z == 0) | (z == depth - 1)

    def chunk(total, zz, yy, xx):
        rows = total.shape[0] // count
        return pl.ds(pl.multiple_of(index(zz, yy, xx) * rows, rows), rows)

    def accumulate(total, zz, yy, xx, extra):
        rows = total.shape[0] // count
        add_rows(total, pl.multiple_of(index(zz, yy, xx) * rows, rows), extra, rows)

    def line_copy(total, slots, group, k, c, yy, xx, width_of):
        up = ups[k]
        slot = (targets[k] + up) * width_of + c
        number = k * width_of + c
        source = total.at[chunk(total, targets[k], yy, xx), :]
        peer = index(z + 2 * up - 1, y, x)
        return slot, remote(
            source, slots.at[slot], sent[group].at[number], came[group].at[slot], dp=peer
        )

    def line_receive(total, slots, group, k, slot, yy, xx):
        here = slots.at[slot]
        peer = index(z + 1 - 2 * ups[k], y, x)
        remote(here, here, sent[group].at[0], came[group].at[slot], dp=peer).wait_recv()
        accumulate(total, targets[k], yy, xx, here)

    c_parts = ((1 - y, 1 - x), (y, 1 - x), (1 - y, x), (y, x))
    items_c = 4 * (depth - 1)

    def copy_c(n):
        return line_copy(sum_c, in_c1, 6, n // 4, n % 4, *c_parts[n % 4], 4)

    def line_c(n):
        k, c = n // 4, n % 4
        yy, xx = c_parts[c]

        @pl.when(starts_line)
        def _():
            copy_c(n)[1].wait_send()
            if n + FLIGHT < items_c:
                copy_c(n + FLIGHT)[1].start()

        @pl.when(jnp.logical_not(starts_line))
        def _():
            slot, copy = line_copy(sum_c, in_c1, 6, k, c, yy, xx, 4)
            line_receive(sum_c, in_c1, 6, k, slot, yy, xx)
            copy.start()

    def first_copy(which, i):
        yy_other = i % 2 == 0
        zz = targets[i // 2]
        if which == 0:
            where = (zz, 1 - y if yy_other else y, 1 - x)
            total, slots, peer = sum_a, in_a1, across_x
        else:
            where = (zz, 1 - y, 1 - x if yy_other else x)
            total, slots, peer = sum_b, in_b1, across_y
        source = total.at[chunk(total, *where), :]
        group = 0 if which == 0 else 3
        return remote(source, slots.at[i], sent[group].at[i], came[group].at[i], dp=peer)

    def second_copy(which, i):
        where = (targets[i], 1 - y, x) if which == 0 else (targets[i], y, 1 - x)
        total, slots, peer = (sum_a, in_a2, across_y) if which == 0 else (sum_b, in_b2, across_x)
        group = 1 if which == 0 else 4
        source = total.at[chunk(total, *where), :]
        return remote(source, slots.at[i], sent[group].at[i], came[group].at[i], dp=peer)

    def first_receive(which, i):
        first_copy(which, i).wait_recv()
        if i + FLIGHT < 2 * depth:
            first_copy(which, i + FLIGHT).start()
        zz = targets[i // 2]
        if which == 0:
            where = (zz, 1 - y if i % 2 == 0 else y, x)
            accumulate(sum_a, *where, in_a1.at[i])
        else:
            where = (zz, y, 1 - x if i % 2 == 0 else x)
            accumulate(sum_b, *where, in_b1.at[i])
        if i % 2 == 0:
            second_copy(which, i // 2).start()

    def line_z(which, k):
        total, slots, group = (sum_a, in_a3, 2) if which == 0 else (sum_b, in_b3, 5)
        source = total.at[chunk(total, targets[k], y, x), :]
        peer = index(targets[k], y, x)
        return remote(source, slots.at[z], sent[group].at[k], came[group].at[z], dp=peer)

    def line(which, k):
        total, came_in = (sum_a, in_a2) if which == 0 else (sum_b, in_b2)
        second_copy(which, k).wait_recv()
        accumulate(total, targets[k], y, x, came_in.at[k])
        if k < depth - 1:
            line_z(which, k).start()

    def line_end(total, slots, group, slot_below, slot_above, add):
        @pl.when(z > 0)
        def _():
            here = slots.at[slot_below]
            peer = index(z - 1, y, x)
            remote(here, here, sent[group].at[0], came[group].at[slot_below], dp=peer).wait_recv()
            add(here)

        @pl.when(z < depth - 1)
        def _():
            here = slots.at[slot_above]
            peer = index(z + 1, y, x)
            remote(here, here, sent[group].at[0], came[group].at[slot_above], dp=peer).wait_recv()
            add(here)

    def finish(which):
        total, slots, group = (sum_a, in_a3, 2) if which == 0 else (sum_b, in_b3, 5)
        own = chunk(total, z, y, x)
        if which == 0:
            hidden = out_fc1.shape[1]
            out_fc1[...] = total[own, :hidden].astype(F32)
            out_proj[...] = total[own, hidden:].astype(F32)

            def add(here):
                out_fc1[...] += here[:, :hidden].astype(F32)
                out_proj[...] += here[:, hidden:].astype(F32)
        else:
            out_fc2[...] = total[own, :].astype(F32)

            def add(here):
                out_fc2[...] += here[...].astype(F32)

        for step in range(1, depth):
            source = (z + step) % depth
            here = slots.at[source]
            peer = index(source, y, x)
            remote(here, here, sent[group].at[0], came[group].at[source], dp=peer).wait_recv()
            add(here)

    operands(2, 6, 1, 5)
    product(held[2], held[6], sum_a, 0)
    product(held[1], held[5], sum_a, held[6].shape[1])
    for i in range(FLIGHT):
        first_copy(0, i).start()
    operands(0, 4)
    product(held[0], held[4], sum_c, 0)

    @pl.when(starts_line)
    def _():
        for n in range(min(FLIGHT, items_c)):
            copy_c(n)[1].start()

    operands(3, 7)
    product(held[3], held[7], sum_b, 0)
    for i in range(FLIGHT):
        first_copy(1, i).start()

    when_core(1, second_sums)
    small_fold()
    small_start()
    done_c = 0
    for i in range(2 * depth):
        first_receive(1, i)
        first_receive(0, i)
        while done_c < items_c * (i + 1) // (2 * depth):
            line_c(done_c)
            done_c += 1
        if i >= 2 and i % 2 == 0 and i // 2 - 1 < len(hops) - 1:
            small_step(i // 2 - 1)
        if i % 2 == 1 and i > 1:
            line(1, i // 2 - 1)
            line(0, i // 2 - 1)

    def end_c(c):
        yy, xx = c_parts[c]
        line_end(
            sum_c, in_c1, 6, (z + 1) * 4 + c, z * 4 + c,
            lambda here: accumulate(sum_c, z, yy, xx, here),
        )

    def copy_c2(c):
        yy, xx = c_parts[c]
        source = sum_c.at[chunk(sum_c, z, yy, xx), :]
        return remote(source, in_c2.at[c], sent[7].at[c], came[7].at[c], dp=across_x)

    def copy_c3():
        source = sum_c.at[chunk(sum_c, z, 1 - y, x), :]
        return remote(source, in_c3, sent[8].at[0], came[8].at[0], dp=across_y)

    for c in range(2):
        end_c(c)
        copy_c2(c).start()
    end_c(2)
    end_c(3)
    copy_c2(0).wait_recv()
    accumulate(sum_c, z, 1 - y, x, in_c2.at[0])
    copy_c3().start()
    copy_c2(1).wait_recv()
    accumulate(sum_c, z, y, x, in_c2.at[1])
    swapped_outputs()
    for stage in range(depth - 1, len(hops)):
        small_step(stage)
    line(1, depth - 1)
    line(0, depth - 1)
    copy_c3().wait_recv()
    out_qkv[...] = sum_c[chunk(sum_c, z, y, x), :].astype(F32) + in_c3[...].astype(F32)
    finish(1)
    finish(0)
    small_end()

    extra_copy(GX).wait_send()

    @pl.when(section == 0)
    def _():
        for i in range(GX):
            extra_copy(i).wait_send()
        for i in order:
            swap_copy(i).wait_send()

    for stage in range(len(hops)):
        small_hop(stage).wait_send()
    for which in range(2):
        for i in range(2 * depth):
            first_copy(which, i).wait_send()
        for i in range(depth):
            second_copy(which, i).wait_send()
        for k in range(depth - 1):
            line_z(which, k).wait_send()
    @pl.when(jnp.logical_not(starts_line))
    def _():
        for n in range(items_c):
            copy_c(n)[1].wait_send()

    copy_c2(0).wait_send()
    copy_c2(1).wait_send()
    copy_c3().wait_send()


def scattered(count, kept, back1, crops, vec, own, counts, tokens, entries):
    lefts = [kept[i] for i in (1, 6, 9, 10)]
    widths = [a.shape[2] for a in lefts] + [back1[i].shape[1] for i in (1, 2, 3, 4)]
    n1, merged, n2, act, gmixed, gbranch, ghidden, gb2 = widths
    heads = kept[5].shape[1]
    scale = (n1 // heads) ** (-0.5)
    depth = count // (SIDE * SIDE)
    rows, rows_b = n1 // count, act // count
    cols_a = ghidden + gbranch
    copies = (2 * depth, depth, depth - 1, 2 * depth, depth, depth - 1, 4 * (depth - 1), 2, 1)
    arrivals = (2 * depth, depth, depth, 2 * depth, depth, depth, 4 * (depth + 1), 2, 1)
    tokens_g, tokens_l = tokens
    return pl.pallas_call(
        functools.partial(scatter_kernel, count, scale),
        out_shape=(
            shape(rows, gmixed, dtype=F32), shape(rows, gbranch, dtype=F32),
            shape(rows, ghidden, dtype=F32), shape(rows_b, gb2, dtype=F32),
            shape(tokens_g, 2, n1), shape(tokens_l, 2, n1), shape(tokens_g, 2, n1), shape(tokens_l, 2, n1),
            *(shape(1, n1, dtype=F32) for _ in range(10)), shape(1, act, dtype=F32),
            shape(heads, 1, entries[0], dtype=F32), shape(heads, 1, entries[1], dtype=F32),
        ),
        in_specs=[OUTSIDE] * 23 + [INSIDE] * 7 + [SCALARS] * 2,
        out_specs=(INSIDE,) * 21,
        scratch_shapes=[pltpu.VMEM((2 * ROWS, w), BF16) for w in widths]
        + [pltpu.VMEM((n1, cols_a), BF16), pltpu.VMEM((act, gb2), BF16), pltpu.VMEM((n1, gmixed), BF16)]
        + [pltpu.VMEM((slots, rows, cols_a), BF16) for slots in (2 * depth, depth, depth)]
        + [pltpu.VMEM((slots, rows_b, gb2), BF16) for slots in (2 * depth, depth, depth)]
        + [pltpu.VMEM((4 * (depth + 1), rows, gmixed), BF16), pltpu.VMEM((2, rows, gmixed), BF16),
           pltpu.VMEM((rows, gmixed), BF16)]
        + [DMA((12,)), DMA((4,)), DMA((4,))]
        + [DMA((c,)) for c in copies] + [DMA((a,)) for a in arrivals]
        + 2 * [
            pltpu.VMEM((16, n1), F32), pltpu.VMEM((16, 16, LANES_G), F32),
            pltpu.VMEM((8, 16, LANES_L), F32),
        ]
        + [
            pltpu.VMEM((ROWS, n1), BF16), pltpu.VMEM((2, ROWS, n1), BF16),
            pltpu.VMEM((2 * (2 + (depth - 1).bit_length()) + 1, SUM_ROWS, n1), F32),
            DMA((8 + depth,)), DMA((8 + depth,)), DMA((9,)), DMA((4,)),
        ]
        + kept_scratch(heads, n1, act) + work_scratch(n1),
        compiler_params=pltpu.CompilerParams(
            vmem_limit_bytes=62 * 2**20, collective_id=1, has_side_effects=True
        ),
        name="first_backward_and_scatter",
    )(
        *lefts, *back1[1:5], *(kept[i] for i in (2, 3, 4, 5, 7, 8, 11, 12)), *own, *back1[5:8],
        jnp.asarray(INDEX_G), jnp.asarray(INDEX_L), kept[0], back1[0], vec, *crops, *counts,
    )


def swapped(value):
    return lax.ppermute(value, "pipe", [(0, 1), (1, 0)])


def plain_scattered(kept, back0, back1, counts, tokens, entries):
    section = lax.axis_index("pipe")
    tokens_g, tokens_l = tokens

    def exchange(layer0, layer1):
        keep = jnp.where(section == 0, layer0, layer1)
        send = jnp.where(section == 0, layer1, layer0)
        return keep, swapped(send)

    lefts = [exchange(kept[i][0], kept[i][1]) for i in (1, 6, 9, 10)]
    rights = [exchange(back0[i], back1[i]) for i in (1, 2, 3, 4)]
    shares = [
        lax.psum_scatter(
            dot_rows(jnp.concatenate(a, 0), jnp.concatenate(b, 0)).astype(BF16),
            "dp", scatter_dimension=0, tiled=True,
        ).astype(F32)
        for a, b in zip(lefts, rights)
    ]
    small, tg, tl = (a + b for a, b in (exchange(back0[i], back1[i]) for i in (5, 6, 7)))
    width = small.shape[1]

    def fold(values, index, count):
        flat = jnp.transpose(values, (1, 0, 2)).reshape(values.shape[1], -1)
        high = flat.astype(BF16)
        low = (flat - high.astype(F32)).astype(BF16)
        spot = hot(jnp.asarray(index.reshape(1, -1)), count)
        sums = dot_cols(jnp.concatenate([high, low], 0), spot)
        return sums[: values.shape[1]] + sums[values.shape[1]:]

    small, tg, tl = lax.psum((small, fold(tg, INDEX_G, width), fold(tl, INDEX_L, 128)), "dp")

    def both_crops(keep, came):
        low = jnp.where(section == 0, keep, came)
        high = jnp.where(section == 0, came, keep)
        return (
            jnp.stack([low[:tokens_g], high[:tokens_g]], 1),
            jnp.stack([low[LOCAL_ROW:LOCAL_ROW + tokens_l], high[LOCAL_ROW:LOCAL_ROW + tokens_l]], 1),
        )

    out_g, out_l = both_crops(*exchange(kept[0][0], kept[0][1]))
    crop = jnp.arange(2, dtype=jnp.int32)[None, :, None]
    out_g = jnp.where(crop < counts[0][0], out_g, jnp.zeros_like(out_g))
    out_l = jnp.where(crop < counts[1][0], out_l, jnp.zeros_like(out_l))
    gin_g, gin_l = both_crops(*exchange(back0[0], back1[0]))
    hidden = back0[3].shape[1]
    rows = [small[i:i + 1] for i in range(F1B)]
    rows.append(small[F1B:F1B + hidden // width].reshape(1, hidden))
    heads = kept[5].shape[1]
    tables = (tg[:heads, None, :entries[0]], tl[:heads, None, :entries[1]])
    return (*shares, out_g, out_l, gin_g, gin_l, *rows, *tables)


def finish_kernel(*refs):
    half = len(refs) // 2
    for source, target in zip(refs[:half], refs[half:]):
        target[...] = source[...]


def finished(arrays):
    return pl.pallas_call(
        finish_kernel,
        out_shape=tuple(shape(*a.shape, dtype=a.dtype) for a in arrays),
        in_specs=[INSIDE] * len(arrays),
        out_specs=(INSIDE,) * len(arrays),
        name="results",
    )(*arrays)


def body(
    x_global, x_local, cot_global, cot_local, global_count, local_count,
    w_qkv, w_proj, w_fc1, w_fc2,
    norm1_gain, norm1_shift, q_bias, v_bias, proj_bias, scale_attn,
    norm2_gain, norm2_shift, fc1_bias, fc2_bias, scale_mlp,
    table_global, table_local,
):
    width = x_global.shape[2]
    entries_g, heads = table_global.shape[1:]
    entries_l = table_local.shape[1]
    tokens = (x_global.shape[1], x_local.shape[1])
    own = (w_qkv[0], w_proj[0], w_fc1[0], w_fc2[0])
    vec = (norm1_gain, norm1_shift, q_bias, v_bias, proj_bias, scale_attn, norm2_gain, norm2_shift,
           fc2_bias, scale_mlp, fc1_bias)
    tables = (table_global[0].T, table_local[0].T)
    crops = tuple(jnp.transpose(a, (1, 0, 2)) for a in (x_global, x_local))
    cots = tuple(jnp.transpose(a, (1, 0, 2)) for a in (cot_global, cot_local))
    count = lax.axis_size("dp")
    depth = count // (SIDE * SIDE)
    whole_tiles = depth > 1 and count % depth == 0 and depth & (depth - 1) == 0 and width % (16 * count) == 0
    results = forward(*crops, vec, tables, own, not whole_tiles)
    other, kept, vec = results[:4], results[4:17], results[17]
    counts = (global_count, local_count)
    back1 = backward(1, (*cots, *counts), vec, kept, heads, own, other)
    entries = (entries_g, entries_l)
    if whole_tiles:
        results = finished(scattered(count, kept, back1, crops, vec, own, counts, tokens, entries))
    else:
        back0 = backward(0, (back1[0], *crops), vec, kept, heads, own, other)
        results = plain_scattered(kept, back0, back1, counts, tokens, entries)
    shares, crops, small, tables = results[:4], results[4:8], results[8:19], results[19:]
    vectors = [small[i] for i in (N1G, N1S, QB, VB, PB, SA, N2G, N2S, F1B, F2B, SM)]
    return (
        *(jnp.transpose(c, (1, 0, 2))[None] for c in crops),
        *(s[None] for s in shares),
        *vectors,
        *(jnp.transpose(t, (1, 2, 0)) for t in tables),
    )


def solution(mesh):
    three, two = P("pipe", None, None), P("pipe", None)
    rows = P("dp", None, None)
    in_specs = (rows,) * 4 + (P("dp"),) * 2 + (three,) * 4 + (two,) * 11 + (three,) * 2
    crops = P("pipe", "dp", None, None)
    out_specs = (crops,) * 4 + (P("pipe", "dp", None),) * 4 + (two,) * 11 + (three,) * 2
    return jax.shard_map(body, mesh=mesh, in_specs=in_specs, out_specs=out_specs, check_vma=False)
```

```python
import functools
import jax
import jax.numpy as jnp
import numpy as np
from jax import lax
from jax.experimental import pallas as pl
from jax.experimental.pallas import tpu as pltpu
from jax.sharding import PartitionSpec as P

GRID_G = 14
GRID_L = 6
ROWS = 256
LOCAL_ROW = 208
LANES_G = 512
LANES_L = 128
FRONT_L = 51
BLOCK = 256
NEG = -1e30
eps = 1e-06
F32 = jnp.float32
BF16 = jnp.bfloat16
INV_SQRT2 = 0.7071067811865476
INV_SQRT_2PI = 0.3989422804014327
N1G, N1S, QB, VB, PB, SA, N2G, N2S, F2B, SM, F1B = range(11)


def spread_index(grid, rows, lanes, front, cls_lane):
    side = 2 * grid - 1
    entries = side * side
    index = np.full((rows, lanes), -1, np.int32)
    for q in range(grid):
        for a in range(side):
            for k in range(grid):
                index[q, front + a * grid + k] = (side - 1 - a) * side + (q - k + grid - 1)
    index[rows - 2, :] = entries
    index[rows - 2, cls_lane] = entries + 2
    index[rows - 1, :] = entries + 1
    return index


INDEX_G = spread_index(GRID_G, 16, LANES_G, 1, 0)
INDEX_L = spread_index(GRID_L, 8, LANES_L, FRONT_L, LOCAL_ROW - 128)


def dot(a, b):
    return lax.dot_general(a, b, (((1,), (0,)), ((), ())), preferred_element_type=F32)


def dot_cols(a, b):
    return lax.dot_general(a, b, (((1,), (1,)), ((), ())), preferred_element_type=F32)


def dot_rows(a, b):
    return lax.dot_general(a, b, (((0,), (0,)), ((), ())), preferred_element_type=F32)


def normalised(x):
    centered = x - jnp.mean(x, axis=-1, keepdims=True)
    rstd = lax.rsqrt(jnp.mean(centered * centered, axis=-1, keepdims=True) + eps)
    return centered * rstd, rstd


def row_steps(step, body):
    def one(i, carry):
        body(pl.ds(pl.multiple_of(i * step, step), step))
        return carry

    lax.fori_loop(0, ROWS // step, one, 0)


def build_bias(spread_g, spread_l, bias):
    for r in range(GRID_G):
        shifted = pltpu.roll(spread_g, (LANES_G - (GRID_G - 1 - r) * GRID_G) % LANES_G, 1)
        bias[pl.ds(1 + GRID_G * r, GRID_G), :] = shifted[:GRID_G, :ROWS]
    for r in range(GRID_L):
        shifted = pltpu.roll(spread_l, GRID_L * r, 1)
        bias[pl.ds(LOCAL_ROW + 1 + GRID_L * r, GRID_L), pl.ds(128, 128)] = shifted[:GRID_L, :]
    tokens_g = GRID_G * GRID_G + 1
    tokens_l = GRID_L * GRID_L + 1
    top = bias[:LOCAL_ROW, :]
    row = lax.broadcasted_iota(jnp.int32, top.shape, 0)
    col = lax.broadcasted_iota(jnp.int32, top.shape, 1)
    top = jnp.where(col == 0, spread_g[15:16, :ROWS], top)
    top = jnp.where(row == 0, spread_g[14:15, :ROWS], top)
    top = jnp.where(row >= tokens_g, 0.0, top)
    top = jnp.where(col >= tokens_g, NEG, top)
    low = bias[LOCAL_ROW:, 128:]
    row = lax.broadcasted_iota(jnp.int32, low.shape, 0)
    col = lax.broadcasted_iota(jnp.int32, low.shape, 1) - (LOCAL_ROW - 128)
    low = jnp.where(col == 0, spread_l[7:8], low)
    low = jnp.where(row == 0, spread_l[6:7], low)
    low = jnp.where(row >= tokens_l, 0.0, low)
    low = jnp.where((col >= 0) & (col < tokens_l), low, NEG)
    bottom = jnp.concatenate([jnp.full((ROWS - LOCAL_ROW, 128), NEG, F32), low], 1)
    return jnp.concatenate([top, bottom], 0)


MESH = pl.DeviceIdType.MESH
SIDE = 2
FLIGHT = 4
TABLE_ROW, TABLE_ROW_L, SMALL_ROWS = 16, 32, 48
SUM_ROWS = 32


def remote(source, target, sent, came, **device):
    return pltpu.make_async_remote_copy(
        src_ref=source, dst_ref=target, send_sem=sent, recv_sem=came,
        device_id=device, device_id_type=MESH,
    )


def hot(index_row, count):
    number = lax.broadcasted_iota(jnp.int32, (count, index_row.shape[1]), 0)
    return jnp.where(number == index_row, 1.0, 0.0).astype(BF16)


def place_crops(target, global_ref, local_ref, section, live_g=None, live_l=None):
    target[...] = jnp.zeros_like(target)
    for ref, start, live in ((global_ref, 0, live_g), (local_ref, LOCAL_ROW, live_l)):
        rows = jnp.where(section == 0, ref[:, 0, :].astype(F32), ref[:, 1, :].astype(F32))
        if live is not None:
            rows = rows * live
        target[start:start + ref.shape[0], :] = rows.astype(BF16)


def forward_kernel(
    scale, keep_both,
    xg_ref, xl_ref, vec_refs, tg_ref, tl_ref, index_g, index_l, own_qkv, own_proj, own_fc1, own_fc2,
    oth_qkv, oth_proj, oth_fc1, oth_fc2,
    out_all, n1_all, q_all, k_all, v_all, p_all, merged_all, branch_all, middle_all,
    n2_all, act_all, dact_all, branch2_all, small_out,
    w_qkv, w_proj, w_fc1, w_fc2, small_in, small, vec_all, x_in, out_ref, n1_ref, q_ref, k_ref, v_ref, p_ref,
    merged_ref, branch_ref, middle_ref, n2_ref, act_ref, dact_ref, branch2_ref,
    spread_g, spread_l, bias, own_sem, sent, came, keep_sem, store_sem, give_sent, give_came, small_sem,
):
    section = lax.axis_index("pipe")
    partner = 1 - section
    own = (own_qkv, own_proj, own_fc1, own_fc2)
    oth = (oth_qkv, oth_proj, oth_fc1, oth_fc2)
    held = (w_qkv, w_proj, w_fc1, w_fc2)
    width = x_in.shape[1]
    heads = p_ref.shape[1]
    half = SMALL_ROWS

    barrier = pltpu.get_barrier_semaphore()
    pl.semaphore_signal(barrier, inc=1, device_id={"pipe": partner}, device_id_type=MESH)
    for i in range(4):
        pltpu.make_async_copy(own[i], held[i].at[section], own_sem.at[i]).start()
    small_rows = small.at[pl.ds(pl.multiple_of(section * half, half), half), :]
    small_in[...] = jnp.zeros_like(small_in)
    row = 0
    for ref in vec_refs:
        for b in range(0, ref.shape[1], width):
            small_in[row:row + 1, :] = ref[:, b:b + width].astype(F32)
            row += 1
    small_in[TABLE_ROW:TABLE_ROW + heads, 0:tg_ref.shape[1]] = tg_ref[...].astype(F32)
    small_in[TABLE_ROW_L:TABLE_ROW_L + heads, 0:tl_ref.shape[1]] = tl_ref[...].astype(F32)
    pl.semaphore_wait(barrier, 1)
    small_copy = remote(small_in, small_rows, small_sem.at[0], small_sem.at[1], pipe=partner)
    small_copy.start()

    def weight_copy(i):
        return remote(own[i], held[i].at[section], sent.at[i], came.at[i], pipe=partner)

    for i in range(4):
        weight_copy(i).start()
    small_rows[...] = small_in[...]
    place_crops(x_in, xg_ref, xl_ref, section)
    small_copy.wait_recv()
    vec_all[...] = small[...]
    small_out[...] = vec_all[...]
    tables_g = jnp.concatenate(
        [small[TABLE_ROW:TABLE_ROW + 16, :], small[half + TABLE_ROW:half + TABLE_ROW + 16, :]], 0
    )
    tables_l = jnp.concatenate(
        [small[TABLE_ROW_L:TABLE_ROW_L + 16, :128], small[half + TABLE_ROW_L:half + TABLE_ROW_L + 16, :128]], 0
    )
    for tables, index_ref, spread, grid, cls_lane in (
        (tables_g, index_g, spread_g, GRID_G, 0), (tables_l, index_l, spread_l, GRID_L, LOCAL_ROW - 128),
    ):
        span, lanes = tables.shape[1], index_ref.shape[1]
        shifted = [tables] + [pltpu.roll(tables, span - r, 1) for r in range(1, grid)]
        found = dot(jnp.concatenate(shifted, 0).astype(BF16), hot(index_ref[0:1, :], span))
        cls = (2 * grid - 1) ** 2
        lane_all = lax.broadcasted_iota(jnp.int32, (1, lanes), 1)
        to_patch = jnp.where(lane_all == cls_lane, tables[:, cls + 2:cls + 3], tables[:, cls:cls + 1])
        to_class = jnp.broadcast_to(tables[:, cls + 1:cls + 2], to_patch.shape)
        for layer in range(2):
            for r in range(grid):
                spread[layer, :, r, :] = found[32 * r + 16 * layer:32 * r + 16 * layer + 16]
            spread[layer, :, grid, :] = to_patch[16 * layer:16 * layer + 16]
            spread[layer, :, grid + 1, :] = to_class[16 * layer:16 * layer + 16]

    slots = (
        out_ref, n1_ref, q_ref, k_ref, v_ref, p_ref, merged_ref, branch_ref, middle_ref,
        n2_ref, act_ref, dact_ref, branch2_ref,
    )
    results = (
        out_all, n1_all, q_all, k_all, v_all, p_all, merged_all, branch_all, middle_all,
        n2_all, act_all, dact_all, branch2_all,
    )
    OUT, N1, Q, K, V, PR, ME, BR, MI, N2, AC, DA, B2 = range(13)
    GIVEN = (OUT, N1, ME, N2, AC)

    def store_copy(number, layer):
        return pltpu.make_async_copy(
            slots[number].at[layer], results[number].at[layer], store_sem.at[layer, number]
        )

    def give_copy(number, layer):
        spot = number if layer == 0 else 13 + GIVEN.index(number)
        return remote(
            slots[number].at[layer], results[number].at[2], give_sent.at[spot], give_came.at[spot],
            pipe=partner,
        )

    def store(layer, *numbers):
        for number in numbers:
            store_copy(number, layer).start()
            if layer == 0 or number in GIVEN:

                @pl.when(section != layer)
                def _():
                    give_copy(number, layer).start()

    def stored(layer, *numbers):
        for number in numbers:
            store_copy(number, layer).wait()
            if layer == 0 or number in GIVEN:

                @pl.when(section != layer)
                def _():
                    give_copy(number, layer).wait_send()

    def weight(i, layer):
        @pl.when(section == layer)
        def _():
            pltpu.make_async_copy(own[i], held[i].at[section], own_sem.at[i]).wait()

        @pl.when(section != layer)
        def _():
            here = held[i].at[partner]
            remote(here, here, sent.at[i], came.at[i], pipe=partner).wait_recv()
            if layer == 1 or keep_both:
                pltpu.make_async_copy(here, oth[i], keep_sem.at[i]).start()

    lane = lax.broadcasted_iota(jnp.int32, (1, 128), 1)
    for layer in range(2):
        entering = x_in if layer == 0 else slots[OUT].at[0]
        (
            out_ref, n1_ref, q_ref, k_ref, v_ref, p_ref, merged_ref, branch_ref, middle_ref,
            n2_ref, act_ref, dact_ref, branch2_ref,
        ) = (slot.at[layer] for slot in slots)
        base = layer * half

        def vec(row):
            return vec_all[base + row:base + row + 1, :]

        def norm1(rows):
            xhat, _ = normalised(entering[rows, :].astype(F32))
            n1_ref[rows, :] = (xhat * vec(N1G) + vec(N1S)).astype(BF16)

        row_steps(128, norm1)
        store(layer, N1)
        weight(0, layer)
        n1 = n1_ref[...]
        for b in range(0, width, BLOCK):
            cols = slice(b, b + BLOCK)
            mixed = dot(n1, w_qkv[layer, :, b:b + BLOCK]) + vec(QB)[:, cols]
            q_ref[:, cols] = (mixed * scale).astype(BF16)
            k_ref[:, cols] = dot(n1, w_qkv[layer, :, width + b:width + b + BLOCK]).astype(BF16)
            mixed = dot(n1, w_qkv[layer, :, 2 * width + b:2 * width + b + BLOCK]) + vec(VB)[:, cols]
            v_ref[:, cols] = mixed.astype(BF16)
        store(layer, Q, K, V)
        for pair in range(heads // 2):
            cols = slice(pair * 128, pair * 128 + 128)
            q, k, v = q_ref[:, cols], k_ref[:, cols], v_ref[:, cols]
            result = None
            for part in range(2):
                head = 2 * pair + part
                mine = (lane < 64) if part == 0 else (lane >= 64)
                scores = dot_cols(q, jnp.where(mine, k, jnp.zeros_like(k))) + build_bias(
                    spread_g[layer, head], spread_l[layer, head], bias.at[head % 2]
                )
                expo = jnp.exp(scores - jnp.max(scores, axis=-1, keepdims=True))
                probs = expo * (1.0 / jnp.sum(expo, axis=-1, keepdims=True))
                low = probs.astype(BF16)
                p_ref[head] = low
                piece = dot(low, jnp.where(mine, v, jnp.zeros_like(v)))
                result = piece if result is None else result + piece
            merged_ref[:, cols] = result.astype(BF16)
        store(layer, PR, ME)
        weight(1, layer)
        merged = merged_ref[...]
        for b in range(0, width, BLOCK):
            cols = slice(b, b + BLOCK)
            branch = dot(merged, w_proj[layer, :, cols]) + vec(PB)[:, cols]
            branch_ref[:, cols] = branch.astype(BF16)
            middle_ref[:, cols] = entering[:, cols].astype(F32) + vec(SA)[:, cols] * branch
        store(layer, BR, MI)

        def norm2(rows):
            xhat, _ = normalised(middle_ref[rows, :])
            n2_ref[rows, :] = (xhat * vec(N2G) + vec(N2S)).astype(BF16)

        row_steps(128, norm2)
        store(layer, N2)
        weight(2, layer)
        n2 = n2_ref[...]
        for b in range(0, w_fc1.shape[2], BLOCK):
            cols = slice(b, b + BLOCK)
            part = b // width
            hidden = dot(n2, w_fc1[layer, :, cols]) + vec(F1B + part)[:, b - part * width:b - part * width + BLOCK]
            cdf = 0.5 + 0.5 * lax.erf(hidden * INV_SQRT2)
            act_ref[:, cols] = (hidden * cdf).astype(BF16)
            slope = cdf + hidden * (INV_SQRT_2PI * jnp.exp(-0.5 * hidden * hidden))
            dact_ref[:, cols] = slope.astype(BF16)
        store(layer, AC, DA)
        weight(3, layer)
        for b in range(0, width, BLOCK):
            cols = slice(b, b + BLOCK)
            branch2 = dot(act_ref[...], w_fc2[layer, :, cols]) + vec(F2B)[:, cols]
            branch2_ref[:, cols] = branch2.astype(BF16)
            out_ref[:, cols] = (middle_ref[:, cols] + vec(SM)[:, cols] * branch2).astype(BF16)
        store(layer, B2, OUT)
    stored(0, *range(13))
    stored(1, *range(13))
    for i in range(4):
        weight_copy(i).wait_send()
    small_copy.wait_send()

    def weights_kept():
        for i in range(4):
            pltpu.make_async_copy(held[i].at[partner], oth[i], keep_sem.at[i]).wait()

    @pl.when(section == 0)
    def _():
        weights_kept()
        for number in range(13):
            give_copy(number, 0).wait_recv()

    @pl.when(section != 0)
    def _():
        if keep_both:
            weights_kept()
        for number in GIVEN:
            give_copy(number, 1).wait_recv()


X, Q, K, V, PR, BR, MI, DA, B2 = range(9)


def clear(*refs):
    for ref in refs:
        ref[...] = jnp.zeros_like(ref)


def backward_steps(
    scale, vec, weight, loaded, done, g_ref, gx_ref, kept, weights, grads, sums, scratch,
):
    x_ref, q_ref, k_ref, v_ref, p_ref, branch_ref, middle_ref, dact_ref, branch2_ref = kept
    w_qkv, w_proj, w_fc1, w_fc2 = weights
    gmixed_ref, gbranch_ref, ghidden_ref, gb2_ref = grads
    small_ref, tg_ref, tl_ref = sums
    gmid, gnorm, gmerged = scratch
    width = g_ref.shape[1]
    heads = p_ref.shape[0]

    def add_small(row, values):
        small_ref[row:row + 1, :] += jnp.sum(values, axis=0, keepdims=True)

    loaded(B2)

    def scaled(rows):
        grad = g_ref[rows, :].astype(F32)
        low = (vec(SM) * grad).astype(BF16)
        gb2_ref[rows, :] = low
        add_small(SM, grad * branch2_ref[rows, :].astype(F32))
        add_small(F2B, low.astype(F32))

    row_steps(128, scaled)
    done(3, B2)
    weight(3)
    loaded(DA)
    gb2 = gb2_ref[...]
    for b in range(0, w_fc1.shape[1], BLOCK):
        cols = slice(b, b + BLOCK)
        part = b // width
        ghidden = (dot_cols(gb2, w_fc2[cols, :]) * dact_ref[:, cols]).astype(BF16)
        ghidden_ref[:, cols] = ghidden
        small_ref[F1B + part:F1B + part + 1, b - part * width:b - part * width + BLOCK] += jnp.sum(
            ghidden.astype(F32), axis=0, keepdims=True
        )
    done(2, DA)
    weight(2)
    for b in range(0, width, BLOCK):
        gnorm[:, b:b + BLOCK] = dot_cols(ghidden_ref[...], w_fc1[b:b + BLOCK, :])

    def norm_back(values, grad, gain):
        xhat, rstd = normalised(values)
        scaled_grad = grad * gain
        mean1 = jnp.mean(scaled_grad, axis=-1, keepdims=True)
        mean2 = jnp.mean(scaled_grad * xhat, axis=-1, keepdims=True)
        return xhat, rstd * (scaled_grad - mean1 - xhat * mean2)

    loaded(MI, BR)

    def norm2(rows):
        grad = gnorm[rows, :]
        xhat, through = norm_back(middle_ref[rows, :], grad, vec(N2G))
        grad_middle = g_ref[rows, :].astype(F32) + through
        gmid[rows, :] = grad_middle
        add_small(N2G, grad * xhat)
        add_small(N2S, grad)
        add_small(SA, grad_middle * branch_ref[rows, :].astype(F32))
        low = (vec(SA) * grad_middle).astype(BF16)
        gbranch_ref[rows, :] = low
        add_small(PB, low.astype(F32))

    row_steps(128, norm2)
    done(1, MI, BR)
    weight(1)
    for b in range(0, width, BLOCK):
        gmerged[:, b:b + BLOCK] = dot_cols(gbranch_ref[...], w_proj[b:b + BLOCK, :]).astype(BF16)
    lane = lax.broadcasted_iota(jnp.int32, (1, 128), 1)
    loaded(V, PR, K, Q)
    lane_all = lax.broadcasted_iota(jnp.int32, (1, ROWS), 1)
    for pair in range(heads // 2):
        cols = slice(pair * 128, pair * 128 + 128)
        q, k, v, gm = q_ref[:, cols], k_ref[:, cols], v_ref[:, cols], gmerged[:, cols]
        gq = gk = gv = 0.0
        for half in range(2):
            head = 2 * pair + half
            mine = (lane < 64) if half == 0 else (lane >= 64)

            def only(values):
                return jnp.where(mine, values, jnp.zeros_like(values))

            low = p_ref[head]
            probs = low.astype(F32)
            grad_probs = dot_cols(gm, only(v))
            total = jnp.sum(probs * grad_probs, axis=-1, keepdims=True)
            gscores = (probs * (grad_probs - total)).astype(BF16)
            gv += dot_rows(low, only(gm))
            gq += dot(gscores, only(k))
            gk += dot_rows(gscores, only(q))
            wide = gscores.astype(F32)
            gs = gnorm.at[:, pl.ds(ROWS * (head % 2), ROWS)]
            gs[...] = jnp.where((lane_all == 0) | (lane_all == LOCAL_ROW), 0.0, wide)
            acc = jnp.zeros((GRID_G, LANES_G), F32)
            for r in range(GRID_G):
                block = gs[pl.ds(1 + GRID_G * r, GRID_G), :]
                block = jnp.concatenate([block, jnp.zeros_like(block)], 1)
                acc += pltpu.roll(block, (GRID_G - 1 - r) * GRID_G, 1)
            first_row = wide[0:1, :]
            to_class = jnp.sum(wide[:LOCAL_ROW, :], axis=0, keepdims=True) - first_row
            to_class = jnp.where(lane_all == 0, to_class, 0.0)
            blank = jnp.zeros((1, LANES_G - ROWS), F32)
            tg_ref[0:GRID_G, head, :] += acc
            tg_ref[14, head:head + 1, :] += jnp.concatenate([first_row, blank], 1)
            tg_ref[15, head:head + 1, :] += jnp.concatenate([to_class, blank], 1)
            acc = jnp.zeros((GRID_L, LANES_L), F32)
            for r in range(GRID_L):
                block = gs[pl.ds(LOCAL_ROW + 1 + GRID_L * r, GRID_L), pl.ds(128, 128)]
                acc += pltpu.roll(block, (LANES_L - GRID_L * r) % LANES_L, 1)
            first_row = wide[LOCAL_ROW:LOCAL_ROW + 1, 128:]
            to_class = jnp.sum(wide[LOCAL_ROW:, 128:], axis=0, keepdims=True) - first_row
            to_class = jnp.where(lane == LOCAL_ROW - 128, to_class, 0.0)
            tl_ref[0:GRID_L, head, :] += acc
            tl_ref[6, head:head + 1, :] += first_row
            tl_ref[7, head:head + 1, :] += to_class
        gmixed_ref[:, cols] = gq.astype(BF16) * jnp.asarray(scale, BF16)
        gmixed_ref[:, slice(width + cols.start, width + cols.stop)] = gk.astype(BF16)
        gmixed_ref[:, slice(2 * width + cols.start, 2 * width + cols.stop)] = gv.astype(BF16)

    def biases(rows):
        add_small(QB, gmixed_ref[rows, :width].astype(F32))
        add_small(VB, gmixed_ref[rows, 2 * width:].astype(F32))

    done(0, V, PR, K, Q)
    row_steps(128, biases)
    weight(0)
    loaded(X)
    for b in range(0, width, BLOCK):
        gnorm[:, b:b + BLOCK] = dot_cols(gmixed_ref[...], w_qkv[b:b + BLOCK, :])

    def norm1(rows):
        grad = gnorm[rows, :]
        xhat, through = norm_back(x_ref[rows, :].astype(F32), grad, vec(N1G))
        add_small(N1G, grad * xhat)
        add_small(N1S, grad)
        gx_ref[rows, :] = (gmid[rows, :] + through).astype(BF16)

    row_steps(128, norm1)


def backward_kernel(
    layer, scale, given, vec_all,
    x_all, q_all, k_all, v_all, p_all, branch_all, middle_all, dact_all, branch2_all,
    own_qkv, own_proj, own_fc1, own_fc2, oth_qkv, oth_proj, oth_fc1, oth_fc2,
    gx_ref, gmixed_out, gbranch_out, ghidden_out, gb2_out, small_ref, tg_ref, tl_ref,
    g_ref, x_ref, q_ref, k_ref, v_ref, p_ref, branch_ref, middle_ref, dact_ref, branch2_ref,
    w_qkv, w_proj, w_fc1, w_fc2, gmixed_ref, gbranch_ref, ghidden_ref, gb2_ref,
    gmid, gnorm, gmerged, load_sem, weight_sem, store_sem,
):
    own = (own_qkv, own_proj, own_fc1, own_fc2)
    oth = (oth_qkv, oth_proj, oth_fc1, oth_fc2)
    section = lax.axis_index("pipe")
    held = (w_qkv, w_proj, w_fc1, w_fc2)
    kept = (x_ref, q_ref, k_ref, v_ref, p_ref, branch_ref, middle_ref, dact_ref, branch2_ref)
    sources = (x_all, q_all, k_all, v_all, p_all, branch_all, middle_all, dact_all, branch2_all)
    grads = (gmixed_ref, gbranch_ref, ghidden_ref, gb2_ref)
    targets = (gmixed_out, gbranch_out, ghidden_out, gb2_out)

    def load_copy(number):
        source = sources[number].at[0 if number == X else layer]
        return pltpu.make_async_copy(source, kept[number], load_sem.at[number])

    def load_weight(i):
        @pl.when(section == layer)
        def _():
            pltpu.make_async_copy(own[i], held[i], weight_sem.at[i]).start()

        @pl.when(section != layer)
        def _():
            pltpu.make_async_copy(oth[i], held[i], weight_sem.at[i]).start()

    def weight(i):
        pltpu.make_async_copy(own[i], held[i], weight_sem.at[i]).wait()

    def loaded(*numbers):
        for number in numbers:
            if layer == 1 or number != X:
                load_copy(number).wait()

    def store_copy(number):
        return pltpu.make_async_copy(grads[number], targets[number], store_sem.at[number])

    def done(number, *unused):
        store_copy(number).start()

    def vec(row):
        return vec_all[layer * SMALL_ROWS + row:layer * SMALL_ROWS + row + 1, :]

    load_copy(B2).start()
    load_weight(3)
    load_copy(DA).start()
    load_weight(2)
    for number in (MI, BR):
        load_copy(number).start()
    load_weight(1)
    for number in (V, PR, K, Q):
        load_copy(number).start()
    load_weight(0)
    clear(small_ref, tg_ref, tl_ref)
    if layer == 1:
        cg_ref, cl_ref, gcount, lcount = given
        load_copy(X).start()
        live_g = jnp.where(gcount[0] > section, 1.0, 0.0)
        live_l = jnp.where(lcount[0] > section, 1.0, 0.0)
        place_crops(g_ref, cg_ref, cl_ref, section, live_g, live_l)
    else:
        g_ref, xg_ref, xl_ref = given
        place_crops(x_ref, xg_ref, xl_ref, section)
    backward_steps(
        scale, vec, weight, loaded, done, g_ref, gx_ref, kept, held, grads,
        (small_ref, tg_ref, tl_ref), (gmid, gnorm, gmerged),
    )
    for number in range(4):
        store_copy(number).wait()


def shape(*dims, dtype=BF16):
    return jax.ShapeDtypeStruct(dims, dtype)


INSIDE = pl.BlockSpec(memory_space=pltpu.VMEM)
OUTSIDE = pl.BlockSpec(memory_space=pl.ANY)
SCALARS = pl.BlockSpec(memory_space=pltpu.SMEM)
DMA = pltpu.SemaphoreType.DMA


def forward(x_global, x_local, vec, tables, own, keep_both):
    width = x_global.shape[2]
    heads = tables[0].shape[0]
    hidden = own[2].shape[1]
    scale = (width // heads) ** (-0.5)
    kept = (
        ((ROWS, width), BF16), ((ROWS, width), BF16), ((ROWS, width), BF16), ((ROWS, width), BF16),
        ((ROWS, width), BF16), ((heads, ROWS, ROWS), BF16), ((ROWS, width), BF16),
        ((ROWS, width), BF16), ((ROWS, width), F32), ((ROWS, width), BF16),
        ((ROWS, hidden), BF16), ((ROWS, hidden), BF16), ((ROWS, width), BF16),
    )
    scratch = [pltpu.VMEM((2, *w.shape), BF16) for w in own]
    scratch += [pltpu.VMEM((SMALL_ROWS, width), F32)] + [pltpu.VMEM((2 * SMALL_ROWS, width), F32)] * 2
    scratch += [pltpu.VMEM((ROWS, width), BF16)]
    scratch += [pltpu.VMEM((2, *dims), kind) for dims, kind in kept]
    scratch += [
        pltpu.VMEM((2, 16, 16, LANES_G), F32), pltpu.VMEM((2, 16, 8, LANES_L), F32),
        pltpu.VMEM((2, ROWS, ROWS), F32),
        DMA((4,)), DMA((4,)), DMA((4,)), DMA((4,)), DMA((2, 13)), DMA((18,)), DMA((18,)), DMA((2,)),
    ]

    def kernel(xg, xl, *refs):
        count = len(vec)
        forward_kernel(scale, keep_both, xg, xl, refs[:count], *refs[count:])

    return pl.pallas_call(
        kernel,
        out_shape=tuple(shape(*w.shape) for w in own)
        + tuple(shape(3, *dims, dtype=kind) for dims, kind in kept)
        + (shape(2 * SMALL_ROWS, width, dtype=F32),),
        in_specs=[INSIDE] * (6 + len(vec)) + [OUTSIDE] * 4,
        out_specs=(OUTSIDE,) * 17 + (INSIDE,),
        scratch_shapes=scratch,
        compiler_params=pltpu.CompilerParams(
            vmem_limit_bytes=60 * 2**20, collective_id=2, has_side_effects=True
        ),
        name="forward_layers",
    )(x_global, x_local, *vec, *tables, jnp.asarray(INDEX_G), jnp.asarray(INDEX_L), *own)


def backward(layer, given, vec, kept, heads, own, other):
    width = vec.shape[1]
    hidden = own[2].shape[1]
    scale = (width // heads) ** (-0.5)
    first, n1, q, k, v, probs, merged, branch, middle, n2, act, dact, branch2 = kept
    count = len(given)

    def kernel(*refs):
        backward_kernel(layer, scale, refs[:count], *refs[count:])

    return pl.pallas_call(
        kernel,
        out_shape=(
            shape(ROWS, width), shape(ROWS, 3 * width), shape(ROWS, width), shape(ROWS, hidden),
            shape(ROWS, width), shape(16, width, dtype=F32),
            shape(16, 16, LANES_G, dtype=F32), shape(8, 16, LANES_L, dtype=F32),
        ),
        in_specs=[SCALARS if g.ndim == 1 else INSIDE for g in given] + [INSIDE] + [OUTSIDE] * 17,
        out_specs=(INSIDE,) + (OUTSIDE,) * 4 + (INSIDE,) * 3,
        scratch_shapes=[pltpu.VMEM((ROWS, width), BF16)] + kept_scratch(heads, width, hidden)
        + [pltpu.VMEM(w.shape, BF16) for w in own]
        + [pltpu.VMEM((ROWS, c), BF16) for c in (3 * width, width, hidden, width)]
        + work_scratch(width) + [DMA((9,)), DMA((4,)), DMA((4,))],
        compiler_params=pltpu.CompilerParams(vmem_limit_bytes=60 * 2**20),
        name="layer_backward",
    )(*given, vec, first, q, k, v, probs, branch, middle, dact, branch2, *own, *other)


def kept_scratch(heads, width, hidden):
    return [pltpu.VMEM((ROWS, width), BF16) for _ in range(4)] + [
        pltpu.VMEM((heads, ROWS, ROWS), BF16), pltpu.VMEM((ROWS, width), BF16),
        pltpu.VMEM((ROWS, width), F32), pltpu.VMEM((ROWS, hidden), BF16), pltpu.VMEM((ROWS, width), BF16),
    ]


def work_scratch(width):
    return [
        pltpu.VMEM((ROWS, width), F32), pltpu.VMEM((ROWS, width), F32),
        pltpu.VMEM((ROWS, width), BF16),
    ]


def add_rows(total, start, extra, count):
    def one(i, carry):
        rows = pl.ds(pl.multiple_of(start + i * 16, 16), 16)
        here = pl.ds(pl.multiple_of(i * 16, 16), 16)
        total[rows, :] = (total[rows, :].astype(F32) + extra[here, :].astype(F32)).astype(BF16)
        return carry

    lax.fori_loop(0, count // 16, one, 0)


def scatter_kernel(count, scale, *refs):
    lefts, back1, kept_all, own = refs[:4], refs[4:8], refs[8:16], refs[16:20]
    small1, tg1, tl1, index_g, index_l, outs_all, gx1, vec_all, xg_ref, xl_ref, gcount, lcount = refs[20:32]
    refs = refs[32:]
    out_qkv, out_proj, out_fc1, out_fc2, out_g, out_l, gin_g, gin_l = refs[:8]
    out_small, out_tg, out_tl = refs[8:19], *refs[19:21]
    refs = refs[21:]
    held = refs[:8]
    sum_a, sum_b, sum_c = refs[8:11]
    in_a1, in_a2, in_a3, in_b1, in_b2, in_b3, in_c1, in_c2, in_c3 = refs[11:20]
    local_sem, swap_sent, swap_came = refs[20:23]
    sent, came = refs[23:32], refs[32:41]
    small_ref, tg_ref, tl_ref, pair_small, pair_tg, pair_tl, pair_gx, gx0, sums = refs[41:50]
    extra_sent, extra_came, load_sem, weight_sem = refs[50:54]
    kept, scratch = refs[54:63], refs[63:66]
    depth = count // (SIDE * SIDE)
    width = held[0].shape[1]
    section = lax.axis_index("pipe")
    place = lax.axis_index("dp")
    x = place % SIDE
    y = (place // SIDE) % SIDE
    z = place // (SIDE * SIDE)

    def index(zz, yy, xx):
        return (zz * SIDE + yy) * SIDE + xx

    across_x, across_y = index(z, y, 1 - x), index(z, 1 - y, x)

    barrier = pltpu.get_barrier_semaphore()
    pl.semaphore_signal(barrier, inc=1, device_id={"pipe": 1 - section}, device_id_type=MESH)
    for peer in (across_x, across_y):
        pl.semaphore_signal(barrier, inc=1, device_id={"dp": peer}, device_id_type=MESH)
    for step in range(1, depth):
        peer = index((z + step) % depth, y, x)
        pl.semaphore_signal(barrier, inc=1, device_id={"dp": peer}, device_id_type=MESH)
    pl.semaphore_wait(barrier, 3 + depth - 1)

    extras = ((small1, pair_small), (tg1, pair_tg), (tl1, pair_tl), (gx1, pair_gx))
    GX = 3

    def extra_copy(i):
        source, target = extras[i]
        return remote(source, target, extra_sent.at[i], extra_came.at[i], pipe=1 - section)

    order = (2, 1, 0, 3)

    def mine(i, crop=0):
        return held[i].at[pl.ds(crop * ROWS, ROWS), :]

    def swap_copy(i):
        return remote(back1[i], mine(4 + i, 1), swap_sent.at[i], swap_came.at[i], pipe=1 - section)

    def own_copy(i):
        if i < 4:
            return pltpu.make_async_copy(lefts[i].at[1], mine(i), local_sem.at[i])
        return pltpu.make_async_copy(back1[i - 4], mine(i), local_sem.at[i])

    def given_copy(i):
        return pltpu.make_async_copy(lefts[i].at[2], mine(i, 1), local_sem.at[8 + i])

    def left_copy(i, crop):
        return pltpu.make_async_copy(lefts[i].at[2 * crop], mine(i, crop), local_sem.at[4 * crop + i])

    def load_copy(crop, number):
        return pltpu.make_async_copy(
            kept_all[number - Q].at[2 * crop], kept[number], load_sem.at[number]
        )

    def sum_copy(i):
        return pltpu.make_async_copy(extras[i][0], (small_ref, tg_ref, tl_ref)[i], load_sem.at[i])

    hidden = held[3].shape[1]
    weights = (
        sum_c, sum_a.at[:, pl.ds(hidden, width)], sum_a.at[:, pl.ds(0, hidden)], sum_b,
    )

    def weight_copy(i):
        return pltpu.make_async_copy(own[i], weights[i], weight_sem.at[i])

    extra_copy(GX).start()

    @pl.when(section == 0)
    def _():
        for i in order:
            swap_copy(i).start()
        for i in range(GX):
            extra_copy(i).start()
        load_copy(0, B2).start()
        weight_copy(3).start()
        load_copy(0, DA).start()
        weight_copy(2).start()
        for number in (MI, BR):
            load_copy(0, number).start()
        weight_copy(1).start()
        for number in (V, PR, K, Q):
            load_copy(0, number).start()
        weight_copy(0).start()
        for i in range(4):
            left_copy(i, 0).start()
            left_copy(i, 1).start()

    @pl.when(section != 0)
    def _():
        for i in order:
            own_copy(i).start()
            given_copy(i).start()
            own_copy(4 + i).start()
        for i in range(GX):
            sum_copy(i).start()

    def first_layer(crop):
        def vec(row):
            return vec_all[row:row + 1, :]

        def weight(i):
            if crop == 0:
                weight_copy(i).wait()

        def loaded(*numbers):
            for number in numbers:
                if number != X:
                    load_copy(crop, number).wait()

        def done(unused, *numbers):
            if crop == 0:
                for number in numbers:
                    load_copy(1, number).start()

        if crop == 1:
            extra_copy(GX).wait_recv()
        x_ref = kept[0]
        clear(x_ref)
        for ref, start in ((xg_ref, 0), (xl_ref, LOCAL_ROW)):
            x_ref[start:start + ref.shape[0], :] = ref[:, crop, :]
        backward_steps(
            scale, vec, weight, loaded, done, gx1 if crop == 0 else pair_gx, gx0.at[crop], kept, weights,
            tuple(mine(4 + i, crop) for i in range(4)), (small_ref, tg_ref, tl_ref), scratch,
        )

    @pl.when(section == 0)
    def _():
        clear(small_ref, tg_ref, tl_ref)
        first_layer(0)
        first_layer(1)

    def second_sums():
        for i in range(GX):
            extra_copy(i).wait_recv()
            sum_copy(i).wait()
        small_ref[...] += pair_small[...]
        tg_ref[...] += pair_tg[...]
        tl_ref[...] += pair_tl[...]

    def swapped_outputs():
        def live(count_ref, crop):
            return jnp.where(count_ref[0] > crop, 1.0, 0.0)

        def place(crop, values, grads):
            for out, gin, start, count_ref in ((out_g, gin_g, 0, gcount), (out_l, gin_l, LOCAL_ROW, lcount)):
                rows = slice(start, start + out.shape[0])
                out[:, crop, :] = (values[rows].astype(F32) * live(count_ref, crop)).astype(BF16)
                gin[:, crop, :] = grads[rows]

        @pl.when(section == 0)
        def _():
            place(0, outs_all[0], gx0[0])
            place(1, outs_all[2], gx0[1])

        @pl.when(section != 0)
        def _():
            extra_copy(GX).wait_recv()
            place(0, outs_all[2], pair_gx[...])
            place(1, outs_all[1], gx1[...])

    def fold_back(values, index_ref, entries, grid, cls_lane):
        lanes = index_ref.shape[1]
        total = values[0:grid].reshape(grid * 16, lanes)
        high = total.astype(BF16)
        low = (total - high.astype(F32)).astype(BF16)
        found = dot_cols(jnp.concatenate([high, low], 0), hot(index_ref[0:1, :], entries))
        found = found[:grid * 16] + found[grid * 16:]
        result = found[:16]
        for r in range(1, grid):
            result = result + pltpu.roll(found[16 * r:16 * r + 16], r, 1)
        lane = lax.broadcasted_iota(jnp.int32, (1, lanes), 1)
        entry = lax.broadcasted_iota(jnp.int32, (1, entries), 1)
        cls = (2 * grid - 1) ** 2
        to_patch, to_class = values[grid], values[grid + 1]
        for spot, column in (
            (cls, jnp.sum(jnp.where(lane == cls_lane, 0.0, to_patch), axis=1, keepdims=True)),
            (cls + 1, jnp.sum(to_class, axis=1, keepdims=True)),
            (cls + 2, jnp.sum(jnp.where(lane == cls_lane, to_patch, 0.0), axis=1, keepdims=True)),
        ):
            result = result + jnp.where(entry == spot, column, 0.0)
        return result

    levels = (depth - 1).bit_length()
    hops = [across_x, across_y]
    for level in range(levels):
        step = 1 << level
        hops.append(index(z + step * (1 - 2 * ((z // step) % 2)), y, x))
    used = max(ref.shape[1] for ref in out_small) // width + len(out_small) - 1
    per_row = width // 128

    def small_fold():
        sums[0] = jnp.zeros((SUM_ROWS, width), F32)
        sums[0, 0:used, :] = small_ref[0:used, :]
        sums[0, TABLE_ROW:TABLE_ROW + 16, :] = fold_back(tg_ref, index_g, width, GRID_G, 0)
        local = fold_back(tl_ref, index_l, 128, GRID_L, LOCAL_ROW - 128)
        for head in range(out_tl.shape[0]):
            row, column = used + head // per_row, head % per_row * 128
            sums[0, row:row + 1, column:column + 128] = local[head:head + 1]

    def small_hop(stage):
        return remote(
            sums.at[stage], sums.at[len(hops) + 1 + stage],
            extra_sent.at[4 + stage], extra_came.at[4 + stage], dp=hops[stage],
        )

    def small_start():
        small_hop(0).start()

    def small_step(stage):
        small_hop(stage).wait_recv()
        sums[stage + 1] = sums[stage] + sums[len(hops) + 1 + stage]
        if stage + 1 < len(hops):
            small_hop(stage + 1).start()

    def small_end():
        total = sums[len(hops)]
        row = 0
        for ref in out_small:
            for b in range(0, ref.shape[1], width):
                ref[:, b:b + width] = total[row:row + 1]
                row += 1
        out_tg[:, 0, :] = total[TABLE_ROW:TABLE_ROW + out_tg.shape[0], 0:out_tg.shape[2]]
        for head in range(out_tl.shape[0]):
            row, column = used + head // per_row, head % per_row * 128
            out_tl[head] = total[row:row + 1, column:column + out_tl.shape[2]]

    def operands(*numbers):
        @pl.when(section == 0)
        def _():
            for i in numbers:
                if i < 4:
                    left_copy(i, 0).wait()
                    left_copy(i, 1).wait()

        @pl.when(section != 0)
        def _():
            for i in numbers:
                own_copy(i).wait()
                if i < 4:
                    given_copy(i).wait()
                else:
                    swap_copy(i - 4).wait_recv()

    def when_core(number, *steps):
        @pl.when(section == number)
        def _():
            for step in steps:
                step()

    def product(left, right, total, offset):
        def one(i, carry):
            start = pl.multiple_of(i * BLOCK, BLOCK)
            rows = left[:, pl.ds(start, BLOCK)].T
            for b in range(0, right.shape[1], width):
                part = dot(rows, right[:, b:b + width])
                total[pl.ds(start, BLOCK), offset + b:offset + b + width] = part.astype(BF16)
            return carry

        lax.fori_loop(0, left.shape[1] // BLOCK, one, 0)

    def target(k):
        low = jnp.where(k < depth - 1 - z, depth - 1 - k, k - (depth - 1 - z))
        high = jnp.where(k < z, k, depth - 1 - (k - z))
        return jnp.where(z < depth // 2, low, high)

    targets = [target(k) for k in range(depth)]
    ups = [jnp.where(targets[k] > z, 1, 0) for k in range(depth - 1)]
    starts_line = (z == 0) | (z == depth - 1)

    def chunk(total, zz, yy, xx):
        rows = total.shape[0] // count
        return pl.ds(pl.multiple_of(index(zz, yy, xx) * rows, rows), rows)

    def accumulate(total, zz, yy, xx, extra):
        rows = total.shape[0] // count
        add_rows(total, pl.multiple_of(index(zz, yy, xx) * rows, rows), extra, rows)

    def line_copy(total, slots, group, k, c, yy, xx, width_of):
        up = ups[k]
        slot = (targets[k] + up) * width_of + c
        number = k * width_of + c
        source = total.at[chunk(total, targets[k], yy, xx), :]
        peer = index(z + 2 * up - 1, y, x)
        return slot, remote(
            source, slots.at[slot], sent[group].at[number], came[group].at[slot], dp=peer
        )

    def line_receive(total, slots, group, k, slot, yy, xx):
        here = slots.at[slot]
        peer = index(z + 1 - 2 * ups[k], y, x)
        remote(here, here, sent[group].at[0], came[group].at[slot], dp=peer).wait_recv()
        accumulate(total, targets[k], yy, xx, here)

    c_parts = ((1 - y, 1 - x), (y, 1 - x), (1 - y, x), (y, x))
    items_c = 4 * (depth - 1)

    def copy_c(n):
        return line_copy(sum_c, in_c1, 6, n // 4, n % 4, *c_parts[n % 4], 4)

    def line_c(n):
        k, c = n // 4, n % 4
        yy, xx = c_parts[c]

        @pl.when(starts_line)
        def _():
            copy_c(n)[1].wait_send()
            if n + FLIGHT < items_c:
                copy_c(n + FLIGHT)[1].start()

        @pl.when(jnp.logical_not(starts_line))
        def _():
            slot, copy = line_copy(sum_c, in_c1, 6, k, c, yy, xx, 4)
            line_receive(sum_c, in_c1, 6, k, slot, yy, xx)
            copy.start()

    def first_copy(which, i):
        yy_other = i % 2 == 0
        zz = targets[i // 2]
        if which == 0:
            where = (zz, 1 - y if yy_other else y, 1 - x)
            total, slots, peer = sum_a, in_a1, across_x
        else:
            where = (zz, 1 - y, 1 - x if yy_other else x)
            total, slots, peer = sum_b, in_b1, across_y
        source = total.at[chunk(total, *where), :]
        group = 0 if which == 0 else 3
        return remote(source, slots.at[i], sent[group].at[i], came[group].at[i], dp=peer)

    def second_copy(which, i):
        where = (targets[i], 1 - y, x) if which == 0 else (targets[i], y, 1 - x)
        total, slots, peer = (sum_a, in_a2, across_y) if which == 0 else (sum_b, in_b2, across_x)
        group = 1 if which == 0 else 4
        source = total.at[chunk(total, *where), :]
        return remote(source, slots.at[i], sent[group].at[i], came[group].at[i], dp=peer)

    def first_receive(which, i):
        first_copy(which, i).wait_recv()
        if i + FLIGHT < 2 * depth:
            first_copy(which, i + FLIGHT).start()
        zz = targets[i // 2]
        if which == 0:
            where = (zz, 1 - y if i % 2 == 0 else y, x)
            accumulate(sum_a, *where, in_a1.at[i])
        else:
            where = (zz, y, 1 - x if i % 2 == 0 else x)
            accumulate(sum_b, *where, in_b1.at[i])
        if i % 2 == 0:
            second_copy(which, i // 2).start()

    def line_z(which, k):
        total, slots, group = (sum_a, in_a3, 2) if which == 0 else (sum_b, in_b3, 5)
        source = total.at[chunk(total, targets[k], y, x), :]
        peer = index(targets[k], y, x)
        return remote(source, slots.at[z], sent[group].at[k], came[group].at[z], dp=peer)

    def line(which, k):
        total, came_in = (sum_a, in_a2) if which == 0 else (sum_b, in_b2)
        second_copy(which, k).wait_recv()
        accumulate(total, targets[k], y, x, came_in.at[k])
        if k < depth - 1:
            line_z(which, k).start()

    def line_end(total, slots, group, slot_below, slot_above, add):
        @pl.when(z > 0)
        def _():
            here = slots.at[slot_below]
            peer = index(z - 1, y, x)
            remote(here, here, sent[group].at[0], came[group].at[slot_below], dp=peer).wait_recv()
            add(here)

        @pl.when(z < depth - 1)
        def _():
            here = slots.at[slot_above]
            peer = index(z + 1, y, x)
            remote(here, here, sent[group].at[0], came[group].at[slot_above], dp=peer).wait_recv()
            add(here)

    def finish(which):
        total, slots, group = (sum_a, in_a3, 2) if which == 0 else (sum_b, in_b3, 5)
        own = chunk(total, z, y, x)
        if which == 0:
            hidden = out_fc1.shape[1]
            out_fc1[...] = total[own, :hidden].astype(F32)
            out_proj[...] = total[own, hidden:].astype(F32)

            def add(here):
                out_fc1[...] += here[:, :hidden].astype(F32)
                out_proj[...] += here[:, hidden:].astype(F32)
        else:
            out_fc2[...] = total[own, :].astype(F32)

            def add(here):
                out_fc2[...] += here[...].astype(F32)

        for step in range(1, depth):
            source = (z + step) % depth
            here = slots.at[source]
            peer = index(source, y, x)
            remote(here, here, sent[group].at[0], came[group].at[source], dp=peer).wait_recv()
            add(here)

    operands(2, 6, 1, 5)
    product(held[2], held[6], sum_a, 0)
    product(held[1], held[5], sum_a, held[6].shape[1])
    for i in range(FLIGHT):
        first_copy(0, i).start()
    operands(0, 4)
    product(held[0], held[4], sum_c, 0)

    @pl.when(starts_line)
    def _():
        for n in range(min(FLIGHT, items_c)):
            copy_c(n)[1].start()

    operands(3, 7)
    product(held[3], held[7], sum_b, 0)
    for i in range(FLIGHT):
        first_copy(1, i).start()

    when_core(1, second_sums)
    small_fold()
    small_start()
    done_c = 0
    for i in range(2 * depth):
        first_receive(1, i)
        first_receive(0, i)
        while done_c < items_c * (i + 1) // (2 * depth):
            line_c(done_c)
            done_c += 1
        if i >= 2 and i % 2 == 0 and i // 2 - 1 < len(hops) - 1:
            small_step(i // 2 - 1)
        if i % 2 == 1 and i > 1:
            line(1, i // 2 - 1)
            line(0, i // 2 - 1)

    def end_c(c):
        yy, xx = c_parts[c]
        line_end(
            sum_c, in_c1, 6, (z + 1) * 4 + c, z * 4 + c,
            lambda here: accumulate(sum_c, z, yy, xx, here),
        )

    def copy_c2(c):
        yy, xx = c_parts[c]
        source = sum_c.at[chunk(sum_c, z, yy, xx), :]
        return remote(source, in_c2.at[c], sent[7].at[c], came[7].at[c], dp=across_x)

    def copy_c3():
        source = sum_c.at[chunk(sum_c, z, 1 - y, x), :]
        return remote(source, in_c3, sent[8].at[0], came[8].at[0], dp=across_y)

    for c in range(2):
        end_c(c)
        copy_c2(c).start()
    end_c(2)
    end_c(3)
    copy_c2(0).wait_recv()
    accumulate(sum_c, z, 1 - y, x, in_c2.at[0])
    copy_c3().start()
    copy_c2(1).wait_recv()
    accumulate(sum_c, z, y, x, in_c2.at[1])
    swapped_outputs()
    for stage in range(depth - 1, len(hops)):
        small_step(stage)
    line(1, depth - 1)
    line(0, depth - 1)
    copy_c3().wait_recv()
    out_qkv[...] = sum_c[chunk(sum_c, z, y, x), :].astype(F32) + in_c3[...].astype(F32)
    finish(1)
    finish(0)
    small_end()

    extra_copy(GX).wait_send()

    @pl.when(section == 0)
    def _():
        for i in range(GX):
            extra_copy(i).wait_send()
        for i in order:
            swap_copy(i).wait_send()

    for stage in range(len(hops)):
        small_hop(stage).wait_send()
    for which in range(2):
        for i in range(2 * depth):
            first_copy(which, i).wait_send()
        for i in range(depth):
            second_copy(which, i).wait_send()
        for k in range(depth - 1):
            line_z(which, k).wait_send()
    @pl.when(jnp.logical_not(starts_line))
    def _():
        for n in range(items_c):
            copy_c(n)[1].wait_send()

    copy_c2(0).wait_send()
    copy_c2(1).wait_send()
    copy_c3().wait_send()


def scattered(count, kept, back1, crops, vec, own, counts, tokens, entries):
    lefts = [kept[i] for i in (1, 6, 9, 10)]
    widths = [a.shape[2] for a in lefts] + [back1[i].shape[1] for i in (1, 2, 3, 4)]
    n1, merged, n2, act, gmixed, gbranch, ghidden, gb2 = widths
    heads = kept[5].shape[1]
    scale = (n1 // heads) ** (-0.5)
    depth = count // (SIDE * SIDE)
    rows, rows_b = n1 // count, act // count
    cols_a = ghidden + gbranch
    copies = (2 * depth, depth, depth - 1, 2 * depth, depth, depth - 1, 4 * (depth - 1), 2, 1)
    arrivals = (2 * depth, depth, depth, 2 * depth, depth, depth, 4 * (depth + 1), 2, 1)
    tokens_g, tokens_l = tokens
    return pl.pallas_call(
        functools.partial(scatter_kernel, count, scale),
        out_shape=(
            shape(rows, gmixed, dtype=F32), shape(rows, gbranch, dtype=F32),
            shape(rows, ghidden, dtype=F32), shape(rows_b, gb2, dtype=F32),
            shape(tokens_g, 2, n1), shape(tokens_l, 2, n1), shape(tokens_g, 2, n1), shape(tokens_l, 2, n1),
            *(shape(1, n1, dtype=F32) for _ in range(10)), shape(1, act, dtype=F32),
            shape(heads, 1, entries[0], dtype=F32), shape(heads, 1, entries[1], dtype=F32),
        ),
        in_specs=[OUTSIDE] * 23 + [INSIDE] * 7 + [SCALARS] * 2,
        out_specs=(INSIDE,) * 21,
        scratch_shapes=[pltpu.VMEM((2 * ROWS, w), BF16) for w in widths]
        + [pltpu.VMEM((n1, cols_a), BF16), pltpu.VMEM((act, gb2), BF16), pltpu.VMEM((n1, gmixed), BF16)]
        + [pltpu.VMEM((slots, rows, cols_a), BF16) for slots in (2 * depth, depth, depth)]
        + [pltpu.VMEM((slots, rows_b, gb2), BF16) for slots in (2 * depth, depth, depth)]
        + [pltpu.VMEM((4 * (depth + 1), rows, gmixed), BF16), pltpu.VMEM((2, rows, gmixed), BF16),
           pltpu.VMEM((rows, gmixed), BF16)]
        + [DMA((12,)), DMA((4,)), DMA((4,))]
        + [DMA((c,)) for c in copies] + [DMA((a,)) for a in arrivals]
        + 2 * [
            pltpu.VMEM((16, n1), F32), pltpu.VMEM((16, 16, LANES_G), F32),
            pltpu.VMEM((8, 16, LANES_L), F32),
        ]
        + [
            pltpu.VMEM((ROWS, n1), BF16), pltpu.VMEM((2, ROWS, n1), BF16),
            pltpu.VMEM((2 * (2 + (depth - 1).bit_length()) + 1, SUM_ROWS, n1), F32),
            DMA((8 + depth,)), DMA((8 + depth,)), DMA((9,)), DMA((4,)),
        ]
        + kept_scratch(heads, n1, act) + work_scratch(n1),
        compiler_params=pltpu.CompilerParams(
            vmem_limit_bytes=62 * 2**20, collective_id=1, has_side_effects=True
        ),
        name="first_backward_and_scatter",
    )(
        *lefts, *back1[1:5], *(kept[i] for i in (2, 3, 4, 5, 7, 8, 11, 12)), *own, *back1[5:8],
        jnp.asarray(INDEX_G), jnp.asarray(INDEX_L), kept[0], back1[0], vec, *crops, *counts,
    )


def swapped(value):
    return lax.ppermute(value, "pipe", [(0, 1), (1, 0)])


def plain_scattered(kept, back0, back1, counts, tokens, entries):
    section = lax.axis_index("pipe")
    tokens_g, tokens_l = tokens

    def exchange(layer0, layer1):
        keep = jnp.where(section == 0, layer0, layer1)
        send = jnp.where(section == 0, layer1, layer0)
        return keep, swapped(send)

    lefts = [exchange(kept[i][0], kept[i][1]) for i in (1, 6, 9, 10)]
    rights = [exchange(back0[i], back1[i]) for i in (1, 2, 3, 4)]
    shares = [
        lax.psum_scatter(
            dot_rows(jnp.concatenate(a, 0), jnp.concatenate(b, 0)).astype(BF16),
            "dp", scatter_dimension=0, tiled=True,
        ).astype(F32)
        for a, b in zip(lefts, rights)
    ]
    small, tg, tl = (a + b for a, b in (exchange(back0[i], back1[i]) for i in (5, 6, 7)))
    width = small.shape[1]

    def fold(values, index, count):
        flat = jnp.transpose(values, (1, 0, 2)).reshape(values.shape[1], -1)
        high = flat.astype(BF16)
        low = (flat - high.astype(F32)).astype(BF16)
        spot = hot(jnp.asarray(index.reshape(1, -1)), count)
        sums = dot_cols(jnp.concatenate([high, low], 0), spot)
        return sums[: values.shape[1]] + sums[values.shape[1]:]

    small, tg, tl = lax.psum((small, fold(tg, INDEX_G, width), fold(tl, INDEX_L, 128)), "dp")

    def both_crops(keep, came):
        low = jnp.where(section == 0, keep, came)
        high = jnp.where(section == 0, came, keep)
        return (
            jnp.stack([low[:tokens_g], high[:tokens_g]], 1),
            jnp.stack([low[LOCAL_ROW:LOCAL_ROW + tokens_l], high[LOCAL_ROW:LOCAL_ROW + tokens_l]], 1),
        )

    out_g, out_l = both_crops(*exchange(kept[0][0], kept[0][1]))
    crop = jnp.arange(2, dtype=jnp.int32)[None, :, None]
    out_g = jnp.where(crop < counts[0][0], out_g, jnp.zeros_like(out_g))
    out_l = jnp.where(crop < counts[1][0], out_l, jnp.zeros_like(out_l))
    gin_g, gin_l = both_crops(*exchange(back0[0], back1[0]))
    hidden = back0[3].shape[1]
    rows = [small[i:i + 1] for i in range(F1B)]
    rows.append(small[F1B:F1B + hidden // width].reshape(1, hidden))
    heads = kept[5].shape[1]
    tables = (tg[:heads, None, :entries[0]], tl[:heads, None, :entries[1]])
    return (*shares, out_g, out_l, gin_g, gin_l, *rows, *tables)


def finish_kernel(*refs):
    half = len(refs) // 2
    for source, target in zip(refs[:half], refs[half:]):
        target[...] = source[...]


def finished(arrays):
    return pl.pallas_call(
        finish_kernel,
        out_shape=tuple(shape(*a.shape, dtype=a.dtype) for a in arrays),
        in_specs=[INSIDE] * len(arrays),
        out_specs=(INSIDE,) * len(arrays),
        name="results",
    )(*arrays)


def body(
    x_global, x_local, cot_global, cot_local, global_count, local_count,
    w_qkv, w_proj, w_fc1, w_fc2,
    norm1_gain, norm1_shift, q_bias, v_bias, proj_bias, scale_attn,
    norm2_gain, norm2_shift, fc1_bias, fc2_bias, scale_mlp,
    table_global, table_local,
):
    width = x_global.shape[2]
    entries_g, heads = table_global.shape[1:]
    entries_l = table_local.shape[1]
    tokens = (x_global.shape[1], x_local.shape[1])
    own = (w_qkv[0], w_proj[0], w_fc1[0], w_fc2[0])
    vec = (norm1_gain, norm1_shift, q_bias, v_bias, proj_bias, scale_attn, norm2_gain, norm2_shift,
           fc2_bias, scale_mlp, fc1_bias)
    tables = (table_global[0].T, table_local[0].T)
    crops = tuple(jnp.transpose(a, (1, 0, 2)) for a in (x_global, x_local))
    cots = tuple(jnp.transpose(a, (1, 0, 2)) for a in (cot_global, cot_local))
    count = lax.axis_size("dp")
    depth = count // (SIDE * SIDE)
    whole_tiles = depth > 1 and count % depth == 0 and depth & (depth - 1) == 0 and width % (16 * count) == 0
    results = forward(*crops, vec, tables, own, not whole_tiles)
    other, kept, vec = results[:4], results[4:17], results[17]
    counts = (global_count, local_count)
    back1 = backward(1, (*cots, *counts), vec, kept, heads, own, other)
    entries = (entries_g, entries_l)
    if whole_tiles:
        results = finished(scattered(count, kept, back1, crops, vec, own, counts, tokens, entries))
    else:
        back0 = backward(0, (back1[0], *crops), vec, kept, heads, own, other)
        results = plain_scattered(kept, back0, back1, counts, tokens, entries)
    shares, crops, small, tables = results[:4], results[4:8], results[8:19], results[19:]
    vectors = [small[i] for i in (N1G, N1S, QB, VB, PB, SA, N2G, N2S, F1B, F2B, SM)]
    return (
        *(jnp.transpose(c, (1, 0, 2))[None] for c in crops),
        *(s[None] for s in shares),
        *vectors,
        *(jnp.transpose(t, (1, 2, 0)) for t in tables),
    )


def solution(mesh):
    three, two = P("pipe", None, None), P("pipe", None)
    rows = P("dp", None, None)
    in_specs = (rows,) * 4 + (P("dp"),) * 2 + (three,) * 4 + (two,) * 11 + (three,) * 2
    crops = P("pipe", "dp", None, None)
    out_specs = (crops,) * 4 + (P("pipe", "dp", None),) * 4 + (two,) * 11 + (three,) * 2
    return jax.shard_map(body, mesh=mesh, in_specs=in_specs, out_specs=out_specs, check_vma=False)
```

```python
import functools
import jax
import jax.numpy as jnp
import numpy as np
from jax import lax
from jax.experimental import pallas as pl
from jax.experimental.pallas import tpu as pltpu
from jax.sharding import PartitionSpec as P

GRID_G = 14
GRID_L = 6
ROWS = 256
LOCAL_ROW = 208
LANES_G = 512
LANES_L = 128
FRONT_L = 51
BLOCK = 256
NEG = -1e30
eps = 1e-06
F32 = jnp.float32
BF16 = jnp.bfloat16
INV_SQRT2 = 0.7071067811865476
INV_SQRT_2PI = 0.3989422804014327
N1G, N1S, QB, VB, PB, SA, N2G, N2S, F2B, SM, F1B = range(11)


def spread_index(grid, rows, lanes, front, cls_lane):
    side = 2 * grid - 1
    entries = side * side
    index = np.full((rows, lanes), -1, np.int32)
    for q in range(grid):
        for a in range(side):
            for k in range(grid):
                index[q, front + a * grid + k] = (side - 1 - a) * side + (q - k + grid - 1)
    index[rows - 2, :] = entries
    index[rows - 2, cls_lane] = entries + 2
    index[rows - 1, :] = entries + 1
    return index


INDEX_G = spread_index(GRID_G, 16, LANES_G, 1, 0)
INDEX_L = spread_index(GRID_L, 8, LANES_L, FRONT_L, LOCAL_ROW - 128)


def dot(a, b):
    return lax.dot_general(a, b, (((1,), (0,)), ((), ())), preferred_element_type=F32)


def dot_cols(a, b):
    return lax.dot_general(a, b, (((1,), (1,)), ((), ())), preferred_element_type=F32)


def dot_rows(a, b):
    return lax.dot_general(a, b, (((0,), (0,)), ((), ())), preferred_element_type=F32)


def normalised(x):
    centered = x - jnp.mean(x, axis=-1, keepdims=True)
    rstd = lax.rsqrt(jnp.mean(centered * centered, axis=-1, keepdims=True) + eps)
    return centered * rstd, rstd


def row_steps(step, body):
    def one(i, carry):
        body(pl.ds(pl.multiple_of(i * step, step), step))
        return carry

    lax.fori_loop(0, ROWS // step, one, 0)


def build_bias(spread_g, spread_l, bias):
    for r in range(GRID_G):
        shifted = pltpu.roll(spread_g, (LANES_G - (GRID_G - 1 - r) * GRID_G) % LANES_G, 1)
        bias[pl.ds(1 + GRID_G * r, GRID_G), :] = shifted[:GRID_G, :ROWS]
    for r in range(GRID_L):
        shifted = pltpu.roll(spread_l, GRID_L * r, 1)
        bias[pl.ds(LOCAL_ROW + 1 + GRID_L * r, GRID_L), pl.ds(128, 128)] = shifted[:GRID_L, :]
    tokens_g = GRID_G * GRID_G + 1
    tokens_l = GRID_L * GRID_L + 1
    top = bias[:LOCAL_ROW, :]
    row = lax.broadcasted_iota(jnp.int32, top.shape, 0)
    col = lax.broadcasted_iota(jnp.int32, top.shape, 1)
    top = jnp.where(col == 0, spread_g[15:16, :ROWS], top)
    top = jnp.where(row == 0, spread_g[14:15, :ROWS], top)
    top = jnp.where(row >= tokens_g, 0.0, top)
    top = jnp.where(col >= tokens_g, NEG, top)
    low = bias[LOCAL_ROW:, 128:]
    row = lax.broadcasted_iota(jnp.int32, low.shape, 0)
    col = lax.broadcasted_iota(jnp.int32, low.shape, 1) - (LOCAL_ROW - 128)
    low = jnp.where(col == 0, spread_l[7:8], low)
    low = jnp.where(row == 0, spread_l[6:7], low)
    low = jnp.where(row >= tokens_l, 0.0, low)
    low = jnp.where((col >= 0) & (col < tokens_l), low, NEG)
    bottom = jnp.concatenate([jnp.full((ROWS - LOCAL_ROW, 128), NEG, F32), low], 1)
    return jnp.concatenate([top, bottom], 0)


MESH = pl.DeviceIdType.MESH
SIDE = 2
FLIGHT = 4
TABLE_ROW, TABLE_ROW_L, SMALL_ROWS = 16, 32, 48
SUM_ROWS = 32


def remote(source, target, sent, came, **device):
    return pltpu.make_async_remote_copy(
        src_ref=source, dst_ref=target, send_sem=sent, recv_sem=came,
        device_id=device, device_id_type=MESH,
    )


def hot(index_row, count):
    number = lax.broadcasted_iota(jnp.int32, (count, index_row.shape[1]), 0)
    return jnp.where(number == index_row, 1.0, 0.0).astype(BF16)


def place_crops(target, global_ref, local_ref, section, live_g=None, live_l=None):
    target[...] = jnp.zeros_like(target)
    for ref, start, live in ((global_ref, 0, live_g), (local_ref, LOCAL_ROW, live_l)):
        rows = jnp.where(section == 0, ref[:, 0, :].astype(F32), ref[:, 1, :].astype(F32))
        if live is not None:
            rows = rows * live
        target[start:start + ref.shape[0], :] = rows.astype(BF16)


def forward_kernel(
    scale, keep_both,
    xg_ref, xl_ref, vec_refs, tg_ref, tl_ref, index_g, index_l, own_qkv, own_proj, own_fc1, own_fc2,
    oth_qkv, oth_proj, oth_fc1, oth_fc2,
    out_all, n1_all, q_all, k_all, v_all, p_all, merged_all, branch_all, middle_all,
    n2_all, act_all, dact_all, branch2_all, small_out,
    w_qkv, w_proj, w_fc1, w_fc2, small_in, small, vec_all, x_in, out_ref, n1_ref, q_ref, k_ref, v_ref, p_ref,
    merged_ref, branch_ref, middle_ref, n2_ref, act_ref, dact_ref, branch2_ref,
    spread_g, spread_l, bias, own_sem, sent, came, keep_sem, store_sem, give_sent, give_came, small_sem,
):
    section = lax.axis_index("pipe")
    partner = 1 - section
    own = (own_qkv, own_proj, own_fc1, own_fc2)
    oth = (oth_qkv, oth_proj, oth_fc1, oth_fc2)
    held = (w_qkv, w_proj, w_fc1, w_fc2)
    width = x_in.shape[1]
    heads = p_ref.shape[1]
    half = SMALL_ROWS

    barrier = pltpu.get_barrier_semaphore()
    pl.semaphore_signal(barrier, inc=1, device_id={"pipe": partner}, device_id_type=MESH)
    for i in range(4):
        pltpu.make_async_copy(own[i], held[i].at[section], own_sem.at[i]).start()
    small_rows = small.at[pl.ds(pl.multiple_of(section * half, half), half), :]
    small_in[...] = jnp.zeros_like(small_in)
    row = 0
    for ref in vec_refs:
        for b in range(0, ref.shape[1], width):
            small_in[row:row + 1, :] = ref[:, b:b + width].astype(F32)
            row += 1
    small_in[TABLE_ROW:TABLE_ROW + heads, 0:tg_ref.shape[1]] = tg_ref[...].astype(F32)
    small_in[TABLE_ROW_L:TABLE_ROW_L + heads, 0:tl_ref.shape[1]] = tl_ref[...].astype(F32)
    pl.semaphore_wait(barrier, 1)
    small_copy = remote(small_in, small_rows, small_sem.at[0], small_sem.at[1], pipe=partner)
    small_copy.start()

    def weight_copy(i):
        return remote(own[i], held[i].at[section], sent.at[i], came.at[i], pipe=partner)

    for i in range(4):
        weight_copy(i).start()
    small_rows[...] = small_in[...]
    place_crops(x_in, xg_ref, xl_ref, section)
    small_copy.wait_recv()
    vec_all[...] = small[...]
    small_out[...] = vec_all[...]
    tables_g = jnp.concatenate(
        [small[TABLE_ROW:TABLE_ROW + 16, :], small[half + TABLE_ROW:half + TABLE_ROW + 16, :]], 0
    )
    tables_l = jnp.concatenate(
        [small[TABLE_ROW_L:TABLE_ROW_L + 16, :128], small[half + TABLE_ROW_L:half + TABLE_ROW_L + 16, :128]], 0
    )
    for tables, index_ref, spread, grid, cls_lane in (
        (tables_g, index_g, spread_g, GRID_G, 0), (tables_l, index_l, spread_l, GRID_L, LOCAL_ROW - 128),
    ):
        span, lanes = tables.shape[1], index_ref.shape[1]
        shifted = [tables] + [pltpu.roll(tables, span - r, 1) for r in range(1, grid)]
        found = dot(jnp.concatenate(shifted, 0).astype(BF16), hot(index_ref[0:1, :], span))
        cls = (2 * grid - 1) ** 2
        lane_all = lax.broadcasted_iota(jnp.int32, (1, lanes), 1)
        to_patch = jnp.where(lane_all == cls_lane, tables[:, cls + 2:cls + 3], tables[:, cls:cls + 1])
        to_class = jnp.broadcast_to(tables[:, cls + 1:cls + 2], to_patch.shape)
        for layer in range(2):
            for r in range(grid):
                spread[layer, :, r, :] = found[32 * r + 16 * layer:32 * r + 16 * layer + 16]
            spread[layer, :, grid, :] = to_patch[16 * layer:16 * layer + 16]
            spread[layer, :, grid + 1, :] = to_class[16 * layer:16 * layer + 16]

    slots = (
        out_ref, n1_ref, q_ref, k_ref, v_ref, p_ref, merged_ref, branch_ref, middle_ref,
        n2_ref, act_ref, dact_ref, branch2_ref,
    )
    results = (
        out_all, n1_all, q_all, k_all, v_all, p_all, merged_all, branch_all, middle_all,
        n2_all, act_all, dact_all, branch2_all,
    )
    OUT, N1, Q, K, V, PR, ME, BR, MI, N2, AC, DA, B2 = range(13)
    GIVEN = (OUT, N1, ME, N2, AC)

    def store_copy(number, layer):
        return pltpu.make_async_copy(
            slots[number].at[layer], results[number].at[layer], store_sem.at[layer, number]
        )

    def give_copy(number, layer):
        spot = number if layer == 0 else 13 + GIVEN.index(number)
        return remote(
            slots[number].at[layer], results[number].at[2], give_sent.at[spot], give_came.at[spot],
            pipe=partner,
        )

    def store(layer, *numbers):
        for number in numbers:
            store_copy(number, layer).start()
            if layer == 0 or number in GIVEN:

                @pl.when(section != layer)
                def _():
                    give_copy(number, layer).start()

    def stored(layer, *numbers):
        for number in numbers:
            store_copy(number, layer).wait()
            if layer == 0 or number in GIVEN:

                @pl.when(section != layer)
                def _():
                    give_copy(number, layer).wait_send()

    def weight(i, layer):
        @pl.when(section == layer)
        def _():
            pltpu.make_async_copy(own[i], held[i].at[section], own_sem.at[i]).wait()

        @pl.when(section != layer)
        def _():
            here = held[i].at[partner]
            remote(here, here, sent.at[i], came.at[i], pipe=partner).wait_recv()
            if layer == 1 or keep_both:
                pltpu.make_async_copy(here, oth[i], keep_sem.at[i]).start()

    lane = lax.broadcasted_iota(jnp.int32, (1, 128), 1)
    for layer in range(2):
        entering = x_in if layer == 0 else slots[OUT].at[0]
        (
            out_ref, n1_ref, q_ref, k_ref, v_ref, p_ref, merged_ref, branch_ref, middle_ref,
            n2_ref, act_ref, dact_ref, branch2_ref,
        ) = (slot.at[layer] for slot in slots)
        base = layer * half

        def vec(row):
            return vec_all[base + row:base + row + 1, :]

        def norm1(rows):
            xhat, _ = normalised(entering[rows, :].astype(F32))
            n1_ref[rows, :] = (xhat * vec(N1G) + vec(N1S)).astype(BF16)

        row_steps(256, norm1)
        store(layer, N1)
        weight(0, layer)
        n1 = n1_ref[...]
        for b in range(0, width, BLOCK):
            cols = slice(b, b + BLOCK)
            mixed = dot(n1, w_qkv[layer, :, b:b + BLOCK]) + vec(QB)[:, cols]
            q_ref[:, cols] = (mixed * scale).astype(BF16)
            k_ref[:, cols] = dot(n1, w_qkv[layer, :, width + b:width + b + BLOCK]).astype(BF16)
            mixed = dot(n1, w_qkv[layer, :, 2 * width + b:2 * width + b + BLOCK]) + vec(VB)[:, cols]
            v_ref[:, cols] = mixed.astype(BF16)
        store(layer, Q, K, V)
        for pair in range(heads // 2):
            cols = slice(pair * 128, pair * 128 + 128)
            q, k, v = q_ref[:, cols], k_ref[:, cols], v_ref[:, cols]
            result = None
            for part in range(2):
                head = 2 * pair + part
                mine = (lane < 64) if part == 0 else (lane >= 64)
                scores = dot_cols(q, jnp.where(mine, k, jnp.zeros_like(k))) + build_bias(
                    spread_g[layer, head], spread_l[layer, head], bias.at[head % 2]
                )
                expo = jnp.exp(scores - jnp.max(scores, axis=-1, keepdims=True))
                probs = expo * (1.0 / jnp.sum(expo, axis=-1, keepdims=True))
                low = probs.astype(BF16)
                p_ref[head] = low
                piece = dot(low, jnp.where(mine, v, jnp.zeros_like(v)))
                result = piece if result is None else result + piece
            merged_ref[:, cols] = result.astype(BF16)
        store(layer, PR, ME)
        weight(1, layer)
        merged = merged_ref[...]
        for b in range(0, width, BLOCK):
            cols = slice(b, b + BLOCK)
            branch = dot(merged, w_proj[layer, :, cols]) + vec(PB)[:, cols]
            branch_ref[:, cols] = branch.astype(BF16)
            middle_ref[:, cols] = entering[:, cols].astype(F32) + vec(SA)[:, cols] * branch
        store(layer, BR, MI)

        def norm2(rows):
            xhat, _ = normalised(middle_ref[rows, :])
            n2_ref[rows, :] = (xhat * vec(N2G) + vec(N2S)).astype(BF16)

        row_steps(256, norm2)
        store(layer, N2)
        weight(2, layer)
        n2 = n2_ref[...]
        for b in range(0, w_fc1.shape[2], BLOCK):
            cols = slice(b, b + BLOCK)
            part = b // width
            hidden = dot(n2, w_fc1[layer, :, cols]) + vec(F1B + part)[:, b - part * width:b - part * width + BLOCK]
            cdf = 0.5 + 0.5 * lax.erf(hidden * INV_SQRT2)
            act_ref[:, cols] = (hidden * cdf).astype(BF16)
            slope = cdf + hidden * (INV_SQRT_2PI * jnp.exp(-0.5 * hidden * hidden))
            dact_ref[:, cols] = slope.astype(BF16)
        store(layer, AC, DA)
        weight(3, layer)
        for b in range(0, width, BLOCK):
            cols = slice(b, b + BLOCK)
            branch2 = dot(act_ref[...], w_fc2[layer, :, cols]) + vec(F2B)[:, cols]
            branch2_ref[:, cols] = branch2.astype(BF16)
            out_ref[:, cols] = (middle_ref[:, cols] + vec(SM)[:, cols] * branch2).astype(BF16)
        store(layer, B2, OUT)
    stored(0, *range(13))
    stored(1, *range(13))
    for i in range(4):
        weight_copy(i).wait_send()
    small_copy.wait_send()

    def weights_kept():
        for i in range(4):
            pltpu.make_async_copy(held[i].at[partner], oth[i], keep_sem.at[i]).wait()

    @pl.when(section == 0)
    def _():
        weights_kept()
        for number in range(13):
            give_copy(number, 0).wait_recv()

    @pl.when(section != 0)
    def _():
        if keep_both:
            weights_kept()
        for number in GIVEN:
            give_copy(number, 1).wait_recv()


X, Q, K, V, PR, BR, MI, DA, B2 = range(9)


def clear(*refs):
    for ref in refs:
        ref[...] = jnp.zeros_like(ref)


def backward_steps(
    scale, vec, weight, loaded, done, g_ref, gx_ref, kept, weights, grads, sums, scratch,
):
    x_ref, q_ref, k_ref, v_ref, p_ref, branch_ref, middle_ref, dact_ref, branch2_ref = kept
    w_qkv, w_proj, w_fc1, w_fc2 = weights
    gmixed_ref, gbranch_ref, ghidden_ref, gb2_ref = grads
    small_ref, tg_ref, tl_ref = sums
    gmid, gnorm, gmerged = scratch
    width = g_ref.shape[1]
    heads = p_ref.shape[0]

    def add_small(row, values):
        small_ref[row:row + 1, :] += jnp.sum(values, axis=0, keepdims=True)

    loaded(B2)

    def scaled(rows):
        grad = g_ref[rows, :].astype(F32)
        low = (vec(SM) * grad).astype(BF16)
        gb2_ref[rows, :] = low
        add_small(SM, grad * branch2_ref[rows, :].astype(F32))
        add_small(F2B, low.astype(F32))

    row_steps(256, scaled)
    done(3, B2)
    weight(3)
    loaded(DA)
    gb2 = gb2_ref[...]
    for b in range(0, w_fc1.shape[1], BLOCK):
        cols = slice(b, b + BLOCK)
        part = b // width
        ghidden = (dot_cols(gb2, w_fc2[cols, :]) * dact_ref[:, cols]).astype(BF16)
        ghidden_ref[:, cols] = ghidden
        small_ref[F1B + part:F1B + part + 1, b - part * width:b - part * width + BLOCK] += jnp.sum(
            ghidden.astype(F32), axis=0, keepdims=True
        )
    done(2, DA)
    weight(2)
    for b in range(0, width, BLOCK):
        gnorm[:, b:b + BLOCK] = dot_cols(ghidden_ref[...], w_fc1[b:b + BLOCK, :])

    def norm_back(values, grad, gain):
        xhat, rstd = normalised(values)
        scaled_grad = grad * gain
        mean1 = jnp.mean(scaled_grad, axis=-1, keepdims=True)
        mean2 = jnp.mean(scaled_grad * xhat, axis=-1, keepdims=True)
        return xhat, rstd * (scaled_grad - mean1 - xhat * mean2)

    loaded(MI, BR)

    def norm2(rows):
        grad = gnorm[rows, :]
        xhat, through = norm_back(middle_ref[rows, :], grad, vec(N2G))
        grad_middle = g_ref[rows, :].astype(F32) + through
        gmid[rows, :] = grad_middle
        add_small(N2G, grad * xhat)
        add_small(N2S, grad)
        add_small(SA, grad_middle * branch_ref[rows, :].astype(F32))
        low = (vec(SA) * grad_middle).astype(BF16)
        gbranch_ref[rows, :] = low
        add_small(PB, low.astype(F32))

    row_steps(256, norm2)
    done(1, MI, BR)
    weight(1)
    for b in range(0, width, BLOCK):
        gmerged[:, b:b + BLOCK] = dot_cols(gbranch_ref[...], w_proj[b:b + BLOCK, :]).astype(BF16)
    lane = lax.broadcasted_iota(jnp.int32, (1, 128), 1)
    loaded(V, PR, K, Q)
    lane_all = lax.broadcasted_iota(jnp.int32, (1, ROWS), 1)
    for pair in range(heads // 2):
        cols = slice(pair * 128, pair * 128 + 128)
        q, k, v, gm = q_ref[:, cols], k_ref[:, cols], v_ref[:, cols], gmerged[:, cols]
        gq = gk = gv = 0.0
        for half in range(2):
            head = 2 * pair + half
            mine = (lane < 64) if half == 0 else (lane >= 64)

            def only(values):
                return jnp.where(mine, values, jnp.zeros_like(values))

            low = p_ref[head]
            probs = low.astype(F32)
            grad_probs = dot_cols(gm, only(v))
            total = jnp.sum(probs * grad_probs, axis=-1, keepdims=True)
            gscores = (probs * (grad_probs - total)).astype(BF16)
            gv += dot_rows(low, only(gm))
            gq += dot(gscores, only(k))
            gk += dot_rows(gscores, only(q))
            wide = gscores.astype(F32)
            gs = gnorm.at[:, pl.ds(ROWS * (head % 2), ROWS)]
            gs[...] = jnp.where((lane_all == 0) | (lane_all == LOCAL_ROW), 0.0, wide)
            acc = jnp.zeros((GRID_G, LANES_G), F32)
            for r in range(GRID_G):
                block = gs[pl.ds(1 + GRID_G * r, GRID_G), :]
                block = jnp.concatenate([block, jnp.zeros_like(block)], 1)
                acc += pltpu.roll(block, (GRID_G - 1 - r) * GRID_G, 1)
            first_row = wide[0:1, :]
            to_class = jnp.sum(wide[:LOCAL_ROW, :], axis=0, keepdims=True) - first_row
            to_class = jnp.where(lane_all == 0, to_class, 0.0)
            blank = jnp.zeros((1, LANES_G - ROWS), F32)
            tg_ref[0:GRID_G, head, :] += acc
            tg_ref[14, head:head + 1, :] += jnp.concatenate([first_row, blank], 1)
            tg_ref[15, head:head + 1, :] += jnp.concatenate([to_class, blank], 1)
            acc = jnp.zeros((GRID_L, LANES_L), F32)
            for r in range(GRID_L):
                block = gs[pl.ds(LOCAL_ROW + 1 + GRID_L * r, GRID_L), pl.ds(128, 128)]
                acc += pltpu.roll(block, (LANES_L - GRID_L * r) % LANES_L, 1)
            first_row = wide[LOCAL_ROW:LOCAL_ROW + 1, 128:]
            to_class = jnp.sum(wide[LOCAL_ROW:, 128:], axis=0, keepdims=True) - first_row
            to_class = jnp.where(lane == LOCAL_ROW - 128, to_class, 0.0)
            tl_ref[0:GRID_L, head, :] += acc
            tl_ref[6, head:head + 1, :] += first_row
            tl_ref[7, head:head + 1, :] += to_class
        gmixed_ref[:, cols] = gq.astype(BF16) * jnp.asarray(scale, BF16)
        gmixed_ref[:, slice(width + cols.start, width + cols.stop)] = gk.astype(BF16)
        gmixed_ref[:, slice(2 * width + cols.start, 2 * width + cols.stop)] = gv.astype(BF16)

    def biases(rows):
        add_small(QB, gmixed_ref[rows, :width].astype(F32))
        add_small(VB, gmixed_ref[rows, 2 * width:].astype(F32))

    done(0, V, PR, K, Q)
    row_steps(256, biases)
    weight(0)
    loaded(X)
    for b in range(0, width, BLOCK):
        gnorm[:, b:b + BLOCK] = dot_cols(gmixed_ref[...], w_qkv[b:b + BLOCK, :])

    def norm1(rows):
        grad = gnorm[rows, :]
        xhat, through = norm_back(x_ref[rows, :].astype(F32), grad, vec(N1G))
        add_small(N1G, grad * xhat)
        add_small(N1S, grad)
        gx_ref[rows, :] = (gmid[rows, :] + through).astype(BF16)

    row_steps(256, norm1)


def backward_kernel(
    layer, scale, given, vec_all,
    x_all, q_all, k_all, v_all, p_all, branch_all, middle_all, dact_all, branch2_all,
    own_qkv, own_proj, own_fc1, own_fc2, oth_qkv, oth_proj, oth_fc1, oth_fc2,
    gx_ref, gmixed_out, gbranch_out, ghidden_out, gb2_out, small_ref, tg_ref, tl_ref,
    g_ref, x_ref, q_ref, k_ref, v_ref, p_ref, branch_ref, middle_ref, dact_ref, branch2_ref,
    w_qkv, w_proj, w_fc1, w_fc2, gmixed_ref, gbranch_ref, ghidden_ref, gb2_ref,
    gmid, gnorm, gmerged, load_sem, weight_sem, store_sem,
):
    own = (own_qkv, own_proj, own_fc1, own_fc2)
    oth = (oth_qkv, oth_proj, oth_fc1, oth_fc2)
    section = lax.axis_index("pipe")
    held = (w_qkv, w_proj, w_fc1, w_fc2)
    kept = (x_ref, q_ref, k_ref, v_ref, p_ref, branch_ref, middle_ref, dact_ref, branch2_ref)
    sources = (x_all, q_all, k_all, v_all, p_all, branch_all, middle_all, dact_all, branch2_all)
    grads = (gmixed_ref, gbranch_ref, ghidden_ref, gb2_ref)
    targets = (gmixed_out, gbranch_out, ghidden_out, gb2_out)

    def load_copy(number):
        source = sources[number].at[0 if number == X else layer]
        return pltpu.make_async_copy(source, kept[number], load_sem.at[number])

    def load_weight(i):
        @pl.when(section == layer)
        def _():
            pltpu.make_async_copy(own[i], held[i], weight_sem.at[i]).start()

        @pl.when(section != layer)
        def _():
            pltpu.make_async_copy(oth[i], held[i], weight_sem.at[i]).start()

    def weight(i):
        pltpu.make_async_copy(own[i], held[i], weight_sem.at[i]).wait()

    def loaded(*numbers):
        for number in numbers:
            if layer == 1 or number != X:
                load_copy(number).wait()

    def store_copy(number):
        return pltpu.make_async_copy(grads[number], targets[number], store_sem.at[number])

    def done(number, *unused):
        store_copy(number).start()

    def vec(row):
        return vec_all[layer * SMALL_ROWS + row:layer * SMALL_ROWS + row + 1, :]

    load_copy(B2).start()
    load_weight(3)
    load_copy(DA).start()
    load_weight(2)
    for number in (MI, BR):
        load_copy(number).start()
    load_weight(1)
    for number in (V, PR, K, Q):
        load_copy(number).start()
    load_weight(0)
    clear(small_ref, tg_ref, tl_ref)
    if layer == 1:
        cg_ref, cl_ref, gcount, lcount = given
        load_copy(X).start()
        live_g = jnp.where(gcount[0] > section, 1.0, 0.0)
        live_l = jnp.where(lcount[0] > section, 1.0, 0.0)
        place_crops(g_ref, cg_ref, cl_ref, section, live_g, live_l)
    else:
        g_ref, xg_ref, xl_ref = given
        place_crops(x_ref, xg_ref, xl_ref, section)
    backward_steps(
        scale, vec, weight, loaded, done, g_ref, gx_ref, kept, held, grads,
        (small_ref, tg_ref, tl_ref), (gmid, gnorm, gmerged),
    )
    for number in range(4):
        store_copy(number).wait()


def shape(*dims, dtype=BF16):
    return jax.ShapeDtypeStruct(dims, dtype)


INSIDE = pl.BlockSpec(memory_space=pltpu.VMEM)
OUTSIDE = pl.BlockSpec(memory_space=pl.ANY)
SCALARS = pl.BlockSpec(memory_space=pltpu.SMEM)
DMA = pltpu.SemaphoreType.DMA


def forward(x_global, x_local, vec, tables, own, keep_both):
    width = x_global.shape[2]
    heads = tables[0].shape[0]
    hidden = own[2].shape[1]
    scale = (width // heads) ** (-0.5)
    kept = (
        ((ROWS, width), BF16), ((ROWS, width), BF16), ((ROWS, width), BF16), ((ROWS, width), BF16),
        ((ROWS, width), BF16), ((heads, ROWS, ROWS), BF16), ((ROWS, width), BF16),
        ((ROWS, width), BF16), ((ROWS, width), F32), ((ROWS, width), BF16),
        ((ROWS, hidden), BF16), ((ROWS, hidden), BF16), ((ROWS, width), BF16),
    )
    scratch = [pltpu.VMEM((2, *w.shape), BF16) for w in own]
    scratch += [pltpu.VMEM((SMALL_ROWS, width), F32)] + [pltpu.VMEM((2 * SMALL_ROWS, width), F32)] * 2
    scratch += [pltpu.VMEM((ROWS, width), BF16)]
    scratch += [pltpu.VMEM((2, *dims), kind) for dims, kind in kept]
    scratch += [
        pltpu.VMEM((2, 16, 16, LANES_G), F32), pltpu.VMEM((2, 16, 8, LANES_L), F32),
        pltpu.VMEM((2, ROWS, ROWS), F32),
        DMA((4,)), DMA((4,)), DMA((4,)), DMA((4,)), DMA((2, 13)), DMA((18,)), DMA((18,)), DMA((2,)),
    ]

    def kernel(xg, xl, *refs):
        count = len(vec)
        forward_kernel(scale, keep_both, xg, xl, refs[:count], *refs[count:])

    return pl.pallas_call(
        kernel,
        out_shape=tuple(shape(*w.shape) for w in own)
        + tuple(shape(3, *dims, dtype=kind) for dims, kind in kept)
        + (shape(2 * SMALL_ROWS, width, dtype=F32),),
        in_specs=[INSIDE] * (6 + len(vec)) + [OUTSIDE] * 4,
        out_specs=(OUTSIDE,) * 17 + (INSIDE,),
        scratch_shapes=scratch,
        compiler_params=pltpu.CompilerParams(
            vmem_limit_bytes=60 * 2**20, collective_id=2, has_side_effects=True
        ),
        name="forward_layers",
    )(x_global, x_local, *vec, *tables, jnp.asarray(INDEX_G), jnp.asarray(INDEX_L), *own)


def backward(layer, given, vec, kept, heads, own, other):
    width = vec.shape[1]
    hidden = own[2].shape[1]
    scale = (width // heads) ** (-0.5)
    first, n1, q, k, v, probs, merged, branch, middle, n2, act, dact, branch2 = kept
    count = len(given)

    def kernel(*refs):
        backward_kernel(layer, scale, refs[:count], *refs[count:])

    return pl.pallas_call(
        kernel,
        out_shape=(
            shape(ROWS, width), shape(ROWS, 3 * width), shape(ROWS, width), shape(ROWS, hidden),
            shape(ROWS, width), shape(16, width, dtype=F32),
            shape(16, 16, LANES_G, dtype=F32), shape(8, 16, LANES_L, dtype=F32),
        ),
        in_specs=[SCALARS if g.ndim == 1 else INSIDE for g in given] + [INSIDE] + [OUTSIDE] * 17,
        out_specs=(INSIDE,) + (OUTSIDE,) * 4 + (INSIDE,) * 3,
        scratch_shapes=[pltpu.VMEM((ROWS, width), BF16)] + kept_scratch(heads, width, hidden)
        + [pltpu.VMEM(w.shape, BF16) for w in own]
        + [pltpu.VMEM((ROWS, c), BF16) for c in (3 * width, width, hidden, width)]
        + work_scratch(width) + [DMA((9,)), DMA((4,)), DMA((4,))],
        compiler_params=pltpu.CompilerParams(vmem_limit_bytes=60 * 2**20),
        name="layer_backward",
    )(*given, vec, first, q, k, v, probs, branch, middle, dact, branch2, *own, *other)


def kept_scratch(heads, width, hidden):
    return [pltpu.VMEM((ROWS, width), BF16) for _ in range(4)] + [
        pltpu.VMEM((heads, ROWS, ROWS), BF16), pltpu.VMEM((ROWS, width), BF16),
        pltpu.VMEM((ROWS, width), F32), pltpu.VMEM((ROWS, hidden), BF16), pltpu.VMEM((ROWS, width), BF16),
    ]


def work_scratch(width):
    return [
        pltpu.VMEM((ROWS, width), F32), pltpu.VMEM((ROWS, width), F32),
        pltpu.VMEM((ROWS, width), BF16),
    ]


def add_rows(total, start, extra, count):
    def one(i, carry):
        rows = pl.ds(pl.multiple_of(start + i * 16, 16), 16)
        here = pl.ds(pl.multiple_of(i * 16, 16), 16)
        total[rows, :] = (total[rows, :].astype(F32) + extra[here, :].astype(F32)).astype(BF16)
        return carry

    lax.fori_loop(0, count // 16, one, 0)


def scatter_kernel(count, scale, *refs):
    lefts, back1, kept_all, own = refs[:4], refs[4:8], refs[8:16], refs[16:20]
    small1, tg1, tl1, index_g, index_l, outs_all, gx1, vec_all, xg_ref, xl_ref, gcount, lcount = refs[20:32]
    refs = refs[32:]
    out_qkv, out_proj, out_fc1, out_fc2, out_g, out_l, gin_g, gin_l = refs[:8]
    out_small, out_tg, out_tl = refs[8:19], *refs[19:21]
    refs = refs[21:]
    held = refs[:8]
    sum_a, sum_b, sum_c = refs[8:11]
    in_a1, in_a2, in_a3, in_b1, in_b2, in_b3, in_c1, in_c2, in_c3 = refs[11:20]
    local_sem, swap_sent, swap_came = refs[20:23]
    sent, came = refs[23:32], refs[32:41]
    small_ref, tg_ref, tl_ref, pair_small, pair_tg, pair_tl, pair_gx, gx0, sums = refs[41:50]
    extra_sent, extra_came, load_sem, weight_sem = refs[50:54]
    kept, scratch = refs[54:63], refs[63:66]
    depth = count // (SIDE * SIDE)
    width = held[0].shape[1]
    section = lax.axis_index("pipe")
    place = lax.axis_index("dp")
    x = place % SIDE
    y = (place // SIDE) % SIDE
    z = place // (SIDE * SIDE)

    def index(zz, yy, xx):
        return (zz * SIDE + yy) * SIDE + xx

    across_x, across_y = index(z, y, 1 - x), index(z, 1 - y, x)

    barrier = pltpu.get_barrier_semaphore()
    pl.semaphore_signal(barrier, inc=1, device_id={"pipe": 1 - section}, device_id_type=MESH)
    for peer in (across_x, across_y):
        pl.semaphore_signal(barrier, inc=1, device_id={"dp": peer}, device_id_type=MESH)
    for step in range(1, depth):
        peer = index((z + step) % depth, y, x)
        pl.semaphore_signal(barrier, inc=1, device_id={"dp": peer}, device_id_type=MESH)
    pl.semaphore_wait(barrier, 3 + depth - 1)

    extras = ((small1, pair_small), (tg1, pair_tg), (tl1, pair_tl), (gx1, pair_gx))
    GX = 3

    def extra_copy(i):
        source, target = extras[i]
        return remote(source, target, extra_sent.at[i], extra_came.at[i], pipe=1 - section)

    order = (2, 1, 0, 3)

    def mine(i, crop=0):
        return held[i].at[pl.ds(crop * ROWS, ROWS), :]

    def swap_copy(i):
        return remote(back1[i], mine(4 + i, 1), swap_sent.at[i], swap_came.at[i], pipe=1 - section)

    def own_copy(i):
        if i < 4:
            return pltpu.make_async_copy(lefts[i].at[1], mine(i), local_sem.at[i])
        return pltpu.make_async_copy(back1[i - 4], mine(i), local_sem.at[i])

    def given_copy(i):
        return pltpu.make_async_copy(lefts[i].at[2], mine(i, 1), local_sem.at[8 + i])

    def left_copy(i, crop):
        return pltpu.make_async_copy(lefts[i].at[2 * crop], mine(i, crop), local_sem.at[4 * crop + i])

    def load_copy(crop, number):
        return pltpu.make_async_copy(
            kept_all[number - Q].at[2 * crop], kept[number], load_sem.at[number]
        )

    def sum_copy(i):
        return pltpu.make_async_copy(extras[i][0], (small_ref, tg_ref, tl_ref)[i], load_sem.at[i])

    hidden = held[3].shape[1]
    weights = (
        sum_c, sum_a.at[:, pl.ds(hidden, width)], sum_a.at[:, pl.ds(0, hidden)], sum_b,
    )

    def weight_copy(i):
        return pltpu.make_async_copy(own[i], weights[i], weight_sem.at[i])

    extra_copy(GX).start()

    @pl.when(section == 0)
    def _():
        for i in order:
            swap_copy(i).start()
        for i in range(GX):
            extra_copy(i).start()
        load_copy(0, B2).start()
        weight_copy(3).start()
        load_copy(0, DA).start()
        weight_copy(2).start()
        for number in (MI, BR):
            load_copy(0, number).start()
        weight_copy(1).start()
        for number in (V, PR, K, Q):
            load_copy(0, number).start()
        weight_copy(0).start()
        for i in range(4):
            left_copy(i, 0).start()
            left_copy(i, 1).start()

    @pl.when(section != 0)
    def _():
        for i in order:
            own_copy(i).start()
            given_copy(i).start()
            own_copy(4 + i).start()
        for i in range(GX):
            sum_copy(i).start()

    def first_layer(crop):
        def vec(row):
            return vec_all[row:row + 1, :]

        def weight(i):
            if crop == 0:
                weight_copy(i).wait()

        def loaded(*numbers):
            for number in numbers:
                if number != X:
                    load_copy(crop, number).wait()

        def done(unused, *numbers):
            if crop == 0:
                for number in numbers:
                    load_copy(1, number).start()

        if crop == 1:
            extra_copy(GX).wait_recv()
        x_ref = kept[0]
        clear(x_ref)
        for ref, start in ((xg_ref, 0), (xl_ref, LOCAL_ROW)):
            x_ref[start:start + ref.shape[0], :] = ref[:, crop, :]
        backward_steps(
            scale, vec, weight, loaded, done, gx1 if crop == 0 else pair_gx, gx0.at[crop], kept, weights,
            tuple(mine(4 + i, crop) for i in range(4)), (small_ref, tg_ref, tl_ref), scratch,
        )

    @pl.when(section == 0)
    def _():
        clear(small_ref, tg_ref, tl_ref)
        first_layer(0)
        first_layer(1)

    def second_sums():
        for i in range(GX):
            extra_copy(i).wait_recv()
            sum_copy(i).wait()
        small_ref[...] += pair_small[...]
        tg_ref[...] += pair_tg[...]
        tl_ref[...] += pair_tl[...]

    def swapped_outputs():
        def live(count_ref, crop):
            return jnp.where(count_ref[0] > crop, 1.0, 0.0)

        def place(crop, values, grads):
            for out, gin, start, count_ref in ((out_g, gin_g, 0, gcount), (out_l, gin_l, LOCAL_ROW, lcount)):
                rows = slice(start, start + out.shape[0])
                out[:, crop, :] = (values[rows].astype(F32) * live(count_ref, crop)).astype(BF16)
                gin[:, crop, :] = grads[rows]

        @pl.when(section == 0)
        def _():
            place(0, outs_all[0], gx0[0])
            place(1, outs_all[2], gx0[1])

        @pl.when(section != 0)
        def _():
            extra_copy(GX).wait_recv()
            place(0, outs_all[2], pair_gx[...])
            place(1, outs_all[1], gx1[...])

    def fold_back(values, index_ref, entries, grid, cls_lane):
        lanes = index_ref.shape[1]
        total = values[0:grid].reshape(grid * 16, lanes)
        high = total.astype(BF16)
        low = (total - high.astype(F32)).astype(BF16)
        found = dot_cols(jnp.concatenate([high, low], 0), hot(index_ref[0:1, :], entries))
        found = found[:grid * 16] + found[grid * 16:]
        result = found[:16]
        for r in range(1, grid):
            result = result + pltpu.roll(found[16 * r:16 * r + 16], r, 1)
        lane = lax.broadcasted_iota(jnp.int32, (1, lanes), 1)
        entry = lax.broadcasted_iota(jnp.int32, (1, entries), 1)
        cls = (2 * grid - 1) ** 2
        to_patch, to_class = values[grid], values[grid + 1]
        for spot, column in (
            (cls, jnp.sum(jnp.where(lane == cls_lane, 0.0, to_patch), axis=1, keepdims=True)),
            (cls + 1, jnp.sum(to_class, axis=1, keepdims=True)),
            (cls + 2, jnp.sum(jnp.where(lane == cls_lane, to_patch, 0.0), axis=1, keepdims=True)),
        ):
            result = result + jnp.where(entry == spot, column, 0.0)
        return result

    levels = (depth - 1).bit_length()
    hops = [across_x, across_y]
    for level in range(levels):
        step = 1 << level
        hops.append(index(z + step * (1 - 2 * ((z // step) % 2)), y, x))
    used = max(ref.shape[1] for ref in out_small) // width + len(out_small) - 1
    per_row = width // 128

    def small_fold():
        sums[0] = jnp.zeros((SUM_ROWS, width), F32)
        sums[0, 0:used, :] = small_ref[0:used, :]
        sums[0, TABLE_ROW:TABLE_ROW + 16, :] = fold_back(tg_ref, index_g, width, GRID_G, 0)
        local = fold_back(tl_ref, index_l, 128, GRID_L, LOCAL_ROW - 128)
        for head in range(out_tl.shape[0]):
            row, column = used + head // per_row, head % per_row * 128
            sums[0, row:row + 1, column:column + 128] = local[head:head + 1]

    def small_hop(stage):
        return remote(
            sums.at[stage], sums.at[len(hops) + 1 + stage],
            extra_sent.at[4 + stage], extra_came.at[4 + stage], dp=hops[stage],
        )

    def small_start():
        small_hop(0).start()

    def small_step(stage):
        small_hop(stage).wait_recv()
        sums[stage + 1] = sums[stage] + sums[len(hops) + 1 + stage]
        if stage + 1 < len(hops):
            small_hop(stage + 1).start()

    def small_end():
        total = sums[len(hops)]
        row = 0
        for ref in out_small:
            for b in range(0, ref.shape[1], width):
                ref[:, b:b + width] = total[row:row + 1]
                row += 1
        out_tg[:, 0, :] = total[TABLE_ROW:TABLE_ROW + out_tg.shape[0], 0:out_tg.shape[2]]
        for head in range(out_tl.shape[0]):
            row, column = used + head // per_row, head % per_row * 128
            out_tl[head] = total[row:row + 1, column:column + out_tl.shape[2]]

    def operands(*numbers):
        @pl.when(section == 0)
        def _():
            for i in numbers:
                if i < 4:
                    left_copy(i, 0).wait()
                    left_copy(i, 1).wait()

        @pl.when(section != 0)
        def _():
            for i in numbers:
                own_copy(i).wait()
                if i < 4:
                    given_copy(i).wait()
                else:
                    swap_copy(i - 4).wait_recv()

    def when_core(number, *steps):
        @pl.when(section == number)
        def _():
            for step in steps:
                step()

    def product(left, right, total, offset):
        def one(i, carry):
            start = pl.multiple_of(i * BLOCK, BLOCK)
            rows = left[:, pl.ds(start, BLOCK)].T
            for b in range(0, right.shape[1], width):
                part = dot(rows, right[:, b:b + width])
                total[pl.ds(start, BLOCK), offset + b:offset + b + width] = part.astype(BF16)
            return carry

        lax.fori_loop(0, left.shape[1] // BLOCK, one, 0)

    def target(k):
        low = jnp.where(k < depth - 1 - z, depth - 1 - k, k - (depth - 1 - z))
        high = jnp.where(k < z, k, depth - 1 - (k - z))
        return jnp.where(z < depth // 2, low, high)

    targets = [target(k) for k in range(depth)]
    ups = [jnp.where(targets[k] > z, 1, 0) for k in range(depth - 1)]
    starts_line = (z == 0) | (z == depth - 1)

    def chunk(total, zz, yy, xx):
        rows = total.shape[0] // count
        return pl.ds(pl.multiple_of(index(zz, yy, xx) * rows, rows), rows)

    def accumulate(total, zz, yy, xx, extra):
        rows = total.shape[0] // count
        add_rows(total, pl.multiple_of(index(zz, yy, xx) * rows, rows), extra, rows)

    def line_copy(total, slots, group, k, c, yy, xx, width_of):
        up = ups[k]
        slot = (targets[k] + up) * width_of + c
        number = k * width_of + c
        source = total.at[chunk(total, targets[k], yy, xx), :]
        peer = index(z + 2 * up - 1, y, x)
        return slot, remote(
            source, slots.at[slot], sent[group].at[number], came[group].at[slot], dp=peer
        )

    def line_receive(total, slots, group, k, slot, yy, xx):
        here = slots.at[slot]
        peer = index(z + 1 - 2 * ups[k], y, x)
        remote(here, here, sent[group].at[0], came[group].at[slot], dp=peer).wait_recv()
        accumulate(total, targets[k], yy, xx, here)

    c_parts = ((1 - y, 1 - x), (y, 1 - x), (1 - y, x), (y, x))
    items_c = 4 * (depth - 1)

    def copy_c(n):
        return line_copy(sum_c, in_c1, 6, n // 4, n % 4, *c_parts[n % 4], 4)

    def line_c(n):
        k, c = n // 4, n % 4
        yy, xx = c_parts[c]

        @pl.when(starts_line)
        def _():
            copy_c(n)[1].wait_send()
            if n + FLIGHT < items_c:
                copy_c(n + FLIGHT)[1].start()

        @pl.when(jnp.logical_not(starts_line))
        def _():
            slot, copy = line_copy(sum_c, in_c1, 6, k, c, yy, xx, 4)
            line_receive(sum_c, in_c1, 6, k, slot, yy, xx)
            copy.start()

    def first_copy(which, i):
        yy_other = i % 2 == 0
        zz = targets[i // 2]
        if which == 0:
            where = (zz, 1 - y if yy_other else y, 1 - x)
            total, slots, peer = sum_a, in_a1, across_x
        else:
            where = (zz, 1 - y, 1 - x if yy_other else x)
            total, slots, peer = sum_b, in_b1, across_y
        source = total.at[chunk(total, *where), :]
        group = 0 if which == 0 else 3
        return remote(source, slots.at[i], sent[group].at[i], came[group].at[i], dp=peer)

    def second_copy(which, i):
        where = (targets[i], 1 - y, x) if which == 0 else (targets[i], y, 1 - x)
        total, slots, peer = (sum_a, in_a2, across_y) if which == 0 else (sum_b, in_b2, across_x)
        group = 1 if which == 0 else 4
        source = total.at[chunk(total, *where), :]
        return remote(source, slots.at[i], sent[group].at[i], came[group].at[i], dp=peer)

    def first_receive(which, i):
        first_copy(which, i).wait_recv()
        if i + FLIGHT < 2 * depth:
            first_copy(which, i + FLIGHT).start()
        zz = targets[i // 2]
        if which == 0:
            where = (zz, 1 - y if i % 2 == 0 else y, x)
            accumulate(sum_a, *where, in_a1.at[i])
        else:
            where = (zz, y, 1 - x if i % 2 == 0 else x)
            accumulate(sum_b, *where, in_b1.at[i])
        if i % 2 == 0:
            second_copy(which, i // 2).start()

    def line_z(which, k):
        total, slots, group = (sum_a, in_a3, 2) if which == 0 else (sum_b, in_b3, 5)
        source = total.at[chunk(total, targets[k], y, x), :]
        peer = index(targets[k], y, x)
        return remote(source, slots.at[z], sent[group].at[k], came[group].at[z], dp=peer)

    def line(which, k):
        total, came_in = (sum_a, in_a2) if which == 0 else (sum_b, in_b2)
        second_copy(which, k).wait_recv()
        accumulate(total, targets[k], y, x, came_in.at[k])
        if k < depth - 1:
            line_z(which, k).start()

    def line_end(total, slots, group, slot_below, slot_above, add):
        @pl.when(z > 0)
        def _():
            here = slots.at[slot_below]
            peer = index(z - 1, y, x)
            remote(here, here, sent[group].at[0], came[group].at[slot_below], dp=peer).wait_recv()
            add(here)

        @pl.when(z < depth - 1)
        def _():
            here = slots.at[slot_above]
            peer = index(z + 1, y, x)
            remote(here, here, sent[group].at[0], came[group].at[slot_above], dp=peer).wait_recv()
            add(here)

    def finish(which):
        total, slots, group = (sum_a, in_a3, 2) if which == 0 else (sum_b, in_b3, 5)
        own = chunk(total, z, y, x)
        if which == 0:
            hidden = out_fc1.shape[1]
            out_fc1[...] = total[own, :hidden].astype(F32)
            out_proj[...] = total[own, hidden:].astype(F32)

            def add(here):
                out_fc1[...] += here[:, :hidden].astype(F32)
                out_proj[...] += here[:, hidden:].astype(F32)
        else:
            out_fc2[...] = total[own, :].astype(F32)

            def add(here):
                out_fc2[...] += here[...].astype(F32)

        for step in range(1, depth):
            source = (z + step) % depth
            here = slots.at[source]
            peer = index(source, y, x)
            remote(here, here, sent[group].at[0], came[group].at[source], dp=peer).wait_recv()
            add(here)

    operands(2, 6, 1, 5)
    product(held[2], held[6], sum_a, 0)
    product(held[1], held[5], sum_a, held[6].shape[1])
    for i in range(FLIGHT):
        first_copy(0, i).start()
    operands(0, 4)
    product(held[0], held[4], sum_c, 0)

    @pl.when(starts_line)
    def _():
        for n in range(min(FLIGHT, items_c)):
            copy_c(n)[1].start()

    operands(3, 7)
    product(held[3], held[7], sum_b, 0)
    for i in range(FLIGHT):
        first_copy(1, i).start()

    when_core(1, second_sums)
    small_fold()
    small_start()
    done_c = 0
    for i in range(2 * depth):
        first_receive(1, i)
        first_receive(0, i)
        while done_c < items_c * (i + 1) // (2 * depth):
            line_c(done_c)
            done_c += 1
        if i >= 2 and i % 2 == 0 and i // 2 - 1 < len(hops) - 1:
            small_step(i // 2 - 1)
        if i % 2 == 1 and i > 1:
            line(1, i // 2 - 1)
            line(0, i // 2 - 1)

    def end_c(c):
        yy, xx = c_parts[c]
        line_end(
            sum_c, in_c1, 6, (z + 1) * 4 + c, z * 4 + c,
            lambda here: accumulate(sum_c, z, yy, xx, here),
        )

    def copy_c2(c):
        yy, xx = c_parts[c]
        source = sum_c.at[chunk(sum_c, z, yy, xx), :]
        return remote(source, in_c2.at[c], sent[7].at[c], came[7].at[c], dp=across_x)

    def copy_c3():
        source = sum_c.at[chunk(sum_c, z, 1 - y, x), :]
        return remote(source, in_c3, sent[8].at[0], came[8].at[0], dp=across_y)

    for c in range(2):
        end_c(c)
        copy_c2(c).start()
    end_c(2)
    end_c(3)
    copy_c2(0).wait_recv()
    accumulate(sum_c, z, 1 - y, x, in_c2.at[0])
    copy_c3().start()
    copy_c2(1).wait_recv()
    accumulate(sum_c, z, y, x, in_c2.at[1])
    swapped_outputs()
    for stage in range(depth - 1, len(hops)):
        small_step(stage)
    line(1, depth - 1)
    line(0, depth - 1)
    copy_c3().wait_recv()
    out_qkv[...] = sum_c[chunk(sum_c, z, y, x), :].astype(F32) + in_c3[...].astype(F32)
    finish(1)
    finish(0)
    small_end()

    extra_copy(GX).wait_send()

    @pl.when(section == 0)
    def _():
        for i in range(GX):
            extra_copy(i).wait_send()
        for i in order:
            swap_copy(i).wait_send()

    for stage in range(len(hops)):
        small_hop(stage).wait_send()
    for which in range(2):
        for i in range(2 * depth):
            first_copy(which, i).wait_send()
        for i in range(depth):
            second_copy(which, i).wait_send()
        for k in range(depth - 1):
            line_z(which, k).wait_send()
    @pl.when(jnp.logical_not(starts_line))
    def _():
        for n in range(items_c):
            copy_c(n)[1].wait_send()

    copy_c2(0).wait_send()
    copy_c2(1).wait_send()
    copy_c3().wait_send()


def scattered(count, kept, back1, crops, vec, own, counts, tokens, entries):
    lefts = [kept[i] for i in (1, 6, 9, 10)]
    widths = [a.shape[2] for a in lefts] + [back1[i].shape[1] for i in (1, 2, 3, 4)]
    n1, merged, n2, act, gmixed, gbranch, ghidden, gb2 = widths
    heads = kept[5].shape[1]
    scale = (n1 // heads) ** (-0.5)
    depth = count // (SIDE * SIDE)
    rows, rows_b = n1 // count, act // count
    cols_a = ghidden + gbranch
    copies = (2 * depth, depth, depth - 1, 2 * depth, depth, depth - 1, 4 * (depth - 1), 2, 1)
    arrivals = (2 * depth, depth, depth, 2 * depth, depth, depth, 4 * (depth + 1), 2, 1)
    tokens_g, tokens_l = tokens
    return pl.pallas_call(
        functools.partial(scatter_kernel, count, scale),
        out_shape=(
            shape(rows, gmixed, dtype=F32), shape(rows, gbranch, dtype=F32),
            shape(rows, ghidden, dtype=F32), shape(rows_b, gb2, dtype=F32),
            shape(tokens_g, 2, n1), shape(tokens_l, 2, n1), shape(tokens_g, 2, n1), shape(tokens_l, 2, n1),
            *(shape(1, n1, dtype=F32) for _ in range(10)), shape(1, act, dtype=F32),
            shape(heads, 1, entries[0], dtype=F32), shape(heads, 1, entries[1], dtype=F32),
        ),
        in_specs=[OUTSIDE] * 23 + [INSIDE] * 7 + [SCALARS] * 2,
        out_specs=(INSIDE,) * 21,
        scratch_shapes=[pltpu.VMEM((2 * ROWS, w), BF16) for w in widths]
        + [pltpu.VMEM((n1, cols_a), BF16), pltpu.VMEM((act, gb2), BF16), pltpu.VMEM((n1, gmixed), BF16)]
        + [pltpu.VMEM((slots, rows, cols_a), BF16) for slots in (2 * depth, depth, depth)]
        + [pltpu.VMEM((slots, rows_b, gb2), BF16) for slots in (2 * depth, depth, depth)]
        + [pltpu.VMEM((4 * (depth + 1), rows, gmixed), BF16), pltpu.VMEM((2, rows, gmixed), BF16),
           pltpu.VMEM((rows, gmixed), BF16)]
        + [DMA((12,)), DMA((4,)), DMA((4,))]
        + [DMA((c,)) for c in copies] + [DMA((a,)) for a in arrivals]
        + 2 * [
            pltpu.VMEM((16, n1), F32), pltpu.VMEM((16, 16, LANES_G), F32),
            pltpu.VMEM((8, 16, LANES_L), F32),
        ]
        + [
            pltpu.VMEM((ROWS, n1), BF16), pltpu.VMEM((2, ROWS, n1), BF16),
            pltpu.VMEM((2 * (2 + (depth - 1).bit_length()) + 1, SUM_ROWS, n1), F32),
            DMA((8 + depth,)), DMA((8 + depth,)), DMA((9,)), DMA((4,)),
        ]
        + kept_scratch(heads, n1, act) + work_scratch(n1),
        compiler_params=pltpu.CompilerParams(
            vmem_limit_bytes=62 * 2**20, collective_id=1, has_side_effects=True
        ),
        name="first_backward_and_scatter",
    )(
        *lefts, *back1[1:5], *(kept[i] for i in (2, 3, 4, 5, 7, 8, 11, 12)), *own, *back1[5:8],
        jnp.asarray(INDEX_G), jnp.asarray(INDEX_L), kept[0], back1[0], vec, *crops, *counts,
    )


def swapped(value):
    return lax.ppermute(value, "pipe", [(0, 1), (1, 0)])


def plain_scattered(kept, back0, back1, counts, tokens, entries):
    section = lax.axis_index("pipe")
    tokens_g, tokens_l = tokens

    def exchange(layer0, layer1):
        keep = jnp.where(section == 0, layer0, layer1)
        send = jnp.where(section == 0, layer1, layer0)
        return keep, swapped(send)

    lefts = [exchange(kept[i][0], kept[i][1]) for i in (1, 6, 9, 10)]
    rights = [exchange(back0[i], back1[i]) for i in (1, 2, 3, 4)]
    shares = [
        lax.psum_scatter(
            dot_rows(jnp.concatenate(a, 0), jnp.concatenate(b, 0)).astype(BF16),
            "dp", scatter_dimension=0, tiled=True,
        ).astype(F32)
        for a, b in zip(lefts, rights)
    ]
    small, tg, tl = (a + b for a, b in (exchange(back0[i], back1[i]) for i in (5, 6, 7)))
    width = small.shape[1]

    def fold(values, index, count):
        flat = jnp.transpose(values, (1, 0, 2)).reshape(values.shape[1], -1)
        high = flat.astype(BF16)
        low = (flat - high.astype(F32)).astype(BF16)
        spot = hot(jnp.asarray(index.reshape(1, -1)), count)
        sums = dot_cols(jnp.concatenate([high, low], 0), spot)
        return sums[: values.shape[1]] + sums[values.shape[1]:]

    small, tg, tl = lax.psum((small, fold(tg, INDEX_G, width), fold(tl, INDEX_L, 128)), "dp")

    def both_crops(keep, came):
        low = jnp.where(section == 0, keep, came)
        high = jnp.where(section == 0, came, keep)
        return (
            jnp.stack([low[:tokens_g], high[:tokens_g]], 1),
            jnp.stack([low[LOCAL_ROW:LOCAL_ROW + tokens_l], high[LOCAL_ROW:LOCAL_ROW + tokens_l]], 1),
        )

    out_g, out_l = both_crops(*exchange(kept[0][0], kept[0][1]))
    crop = jnp.arange(2, dtype=jnp.int32)[None, :, None]
    out_g = jnp.where(crop < counts[0][0], out_g, jnp.zeros_like(out_g))
    out_l = jnp.where(crop < counts[1][0], out_l, jnp.zeros_like(out_l))
    gin_g, gin_l = both_crops(*exchange(back0[0], back1[0]))
    hidden = back0[3].shape[1]
    rows = [small[i:i + 1] for i in range(F1B)]
    rows.append(small[F1B:F1B + hidden // width].reshape(1, hidden))
    heads = kept[5].shape[1]
    tables = (tg[:heads, None, :entries[0]], tl[:heads, None, :entries[1]])
    return (*shares, out_g, out_l, gin_g, gin_l, *rows, *tables)


def finish_kernel(*refs):
    half = len(refs) // 2
    for source, target in zip(refs[:half], refs[half:]):
        target[...] = source[...]


def finished(arrays):
    return pl.pallas_call(
        finish_kernel,
        out_shape=tuple(shape(*a.shape, dtype=a.dtype) for a in arrays),
        in_specs=[INSIDE] * len(arrays),
        out_specs=(INSIDE,) * len(arrays),
        name="results",
    )(*arrays)


def body(
    x_global, x_local, cot_global, cot_local, global_count, local_count,
    w_qkv, w_proj, w_fc1, w_fc2,
    norm1_gain, norm1_shift, q_bias, v_bias, proj_bias, scale_attn,
    norm2_gain, norm2_shift, fc1_bias, fc2_bias, scale_mlp,
    table_global, table_local,
):
    width = x_global.shape[2]
    entries_g, heads = table_global.shape[1:]
    entries_l = table_local.shape[1]
    tokens = (x_global.shape[1], x_local.shape[1])
    own = (w_qkv[0], w_proj[0], w_fc1[0], w_fc2[0])
    vec = (norm1_gain, norm1_shift, q_bias, v_bias, proj_bias, scale_attn, norm2_gain, norm2_shift,
           fc2_bias, scale_mlp, fc1_bias)
    tables = (table_global[0].T, table_local[0].T)
    crops = tuple(jnp.transpose(a, (1, 0, 2)) for a in (x_global, x_local))
    cots = tuple(jnp.transpose(a, (1, 0, 2)) for a in (cot_global, cot_local))
    count = lax.axis_size("dp")
    depth = count // (SIDE * SIDE)
    whole_tiles = depth > 1 and count % depth == 0 and depth & (depth - 1) == 0 and width % (16 * count) == 0
    results = forward(*crops, vec, tables, own, not whole_tiles)
    other, kept, vec = results[:4], results[4:17], results[17]
    counts = (global_count, local_count)
    back1 = backward(1, (*cots, *counts), vec, kept, heads, own, other)
    entries = (entries_g, entries_l)
    if whole_tiles:
        results = finished(scattered(count, kept, back1, crops, vec, own, counts, tokens, entries))
    else:
        back0 = backward(0, (back1[0], *crops), vec, kept, heads, own, other)
        results = plain_scattered(kept, back0, back1, counts, tokens, entries)
    shares, crops, small, tables = results[:4], results[4:8], results[8:19], results[19:]
    vectors = [small[i] for i in (N1G, N1S, QB, VB, PB, SA, N2G, N2S, F1B, F2B, SM)]
    return (
        *(jnp.transpose(c, (1, 0, 2))[None] for c in crops),
        *(s[None] for s in shares),
        *vectors,
        *(jnp.transpose(t, (1, 2, 0)) for t in tables),
    )


def solution(mesh):
    three, two = P("pipe", None, None), P("pipe", None)
    rows = P("dp", None, None)
    in_specs = (rows,) * 4 + (P("dp"),) * 2 + (three,) * 4 + (two,) * 11 + (three,) * 2
    crops = P("pipe", "dp", None, None)
    out_specs = (crops,) * 4 + (P("pipe", "dp", None),) * 4 + (two,) * 11 + (three,) * 2
    return jax.shard_map(body, mesh=mesh, in_specs=in_specs, out_specs=out_specs, check_vma=False)
```
